32 devices in a mesh: seq: 8 (over y, x, core), head: 4 (over z).
Axes of the slice: x: 2, y: 2, z: 4, core: 2. Of those that a mesh axis runs over, the one named last changes fastest.
Arguments:
- inputs: bfloat16 [2, 7168, 512], P(None, 'seq'), may hold values from -8 to 8
- doc_ids: int32 [2, 7168], P(None, 'seq'), may hold values from 0 to 7167, as said below
- pad_mask: int32 [2, 7168], P(None, 'seq'), may hold values 0 or 1
- ln1_gain: float32 [512], replicated, may hold values from 0.25 to 1.75
- ln1_shift: float32 [512], replicated, may hold values from -3 to 3
- w_query: bfloat16 [512, 512], P(None, 'head'), may hold values from -0.25 to 0.25
- w_key: bfloat16 [512, 512], P(None, 'head'), may hold values from -0.25 to 0.25
- w_value: bfloat16 [512, 512], P(None, 'head'), may hold values from -0.25 to 0.25
- w_out: bfloat16 [512, 512], P('head'), may hold values from -0.375 to 0.375
- ln2_gain: float32 [512], replicated, may hold values from 0.25 to 1.75
- ln2_shift: float32 [512], replicated, may hold values from -3 to 3
- w_up: bfloat16 [512, 2048], P(None, 'head'), may hold values from -0.25 to 0.25
- b_up: float32 [2048], P('head'), may hold values from -3 to 3
- w_down: bfloat16 [2048, 512], P('head'), may hold values from -0.125 to 0.125
- b_down: float32 [512], replicated, may hold values from -3 to 3
- out_grad: bfloat16 [2, 7168, 512], P(None, 'seq'), may hold values from -6 to 6
Outputs:
- out: bfloat16 [2, 7168, 512], P(None, 'seq')
- grad_inputs: float32 [2, 7168, 512], P(None, 'seq')
- grad_ln1_gain: float32 [512], replicated
- grad_ln1_shift: float32 [512], replicated
- grad_w_query: float32 [512, 512], P(None, 'head')
- grad_w_key: float32 [512, 512], P(None, 'head')
- grad_w_value: float32 [512, 512], P(None, 'head')
- grad_w_out: float32 [512, 512], P('head')
- grad_ln2_gain: float32 [512], replicated
- grad_ln2_shift: float32 [512], replicated
- grad_w_up: float32 [512, 2048], P(None, 'head')
- grad_b_up: float32 [2048], P('head')
- grad_w_down: float32 [2048, 512], P('head')
- grad_b_down: float32 [512], replicated
The draws below stay inside these ranges and needn't reach their ends.
Inputs may be any that keep to these rules, and one draw needn't show every extreme that they name: `doc_ids`: ids never fall along a row, so that equal ids stand together; each row begins with id 0 and its last document has id 7168 - 1.
All inputs are finite; a program needn't handle non-finite values. No bound on the sum of `pad_mask` on one device may be relied on, other than what follows from the above.
Results may differ from the reference program's by a relative error of at most 0.013.
Values sent between devices are 32-bit elements; how exact they have to be, the bound alone decides.
No kernel may reach another device: no remote copies, remote signals or barrier semaphores. Data moves between devices by JAX's collectives and lax.ppermute only.
A program may use at most 128 MiB of HBM per device.

```python
import math
from functools import partial
import jax
import jax.numpy as jnp
from jax import lax

D = 512
HEADS = 8
HEAD_DIM = 64
FF = 2048
SPAN = 128
ROWS = 2
REGION = 896
SEQLEN = 7168


def draw_inputs(key, part):
    key = jax.random.fold_in(key, 11)
    noise_key, offset_key = jax.random.split(key)
    span_count = SEQLEN // SPAN
    noise = jax.random.normal(noise_key, (ROWS, SEQLEN, D), jnp.float32)
    offset = jax.random.normal(offset_key, (ROWS, span_count, 1, D), jnp.float32)
    values = noise.reshape(ROWS, span_count, SPAN, D) + offset
    return jnp.clip(values.reshape(ROWS, SEQLEN, D), -8.0, 8.0).astype(jnp.bfloat16)


def draw_doc_ids(key, part):
    key = jax.random.fold_in(key, 23)
    row_key, start_key, finish_key, boundary_key = jax.random.split(key, 4)
    place = jnp.arange(SEQLEN, dtype=jnp.int32)[None, :]
    half_region = max(REGION // 2, 2)
    chosen_row = jax.random.randint(row_key, (), 0, ROWS)
    first_place = jax.random.randint(start_key, (ROWS, 1), 1, half_region)
    final_place = SEQLEN - jax.random.randint(finish_key, (ROWS, 1), 1, half_region)
    long_ids = (place >= first_place).astype(jnp.int32) + (place >= final_place).astype(jnp.int32)
    boundary = (jax.random.randint(boundary_key, (ROWS, SEQLEN), 0, REGION) == 0) & (place > 0)
    short_ids = jnp.cumsum(boundary.astype(jnp.int32), axis=1)
    row_index = jnp.arange(ROWS, dtype=jnp.int32)[:, None]
    ids = jnp.where(row_index == chosen_row, long_ids, short_ids).astype(jnp.int32)
    final_ids = ids[:, SEQLEN - 1:SEQLEN]
    return jnp.where(ids == final_ids, SEQLEN - 1, ids).astype(jnp.int32)


def with_ends(entries, stream_key, least, top_value):
    spot = [jax.random.randint(jax.random.fold_in(stream_key, axis), (), 0, length) for axis, length in enumerate(entries.shape)]
    widest = entries.shape.index(max(entries.shape))
    next_to = spot[:widest] + [(spot[widest] + 1) % entries.shape[widest]] + spot[widest + 1:]
    return entries.at[tuple(spot)].set(least).at[tuple(next_to)].set(top_value)


def block_levels(rng, shape, cuts, low, high):
    factor_of = 1.0
    for axis_at, shards_of in cuts:
        heights = jax.random.uniform(jax.random.fold_in(jax.random.fold_in(rng, 6), axis_at), (shards_of,), jnp.float32, low / len(cuts), high / len(cuts))
        factor_of = factor_of * jnp.repeat(jnp.exp(heights), shape[axis_at] // shards_of).reshape((-1,) + (1,) * (len(shape) - 1 - axis_at))
    return factor_of


def normal_values(key, shape, deviation, reach, shards=(), kind=jnp.bfloat16):
    entries = jax.random.normal(key, shape, jnp.float32) * deviation
    if len(shards) > 0:
        entries = block_levels(key, shape, shards, -0.22, 0.18) * entries
    return jnp.clip(entries, min=-reach, max=reach).astype(kind)


def setup_inputs(seed: int = 0) -> dict:
    seeds = jax.random.split(jax.random.key(seed), 17)
    inputs = draw_inputs(jax.random.fold_in(seeds[16], 71), 0)
    doc_ids = draw_doc_ids(jax.random.fold_in(seeds[16], 71), 0)
    pad_mask = with_ends((jax.random.randint(seeds[2], (ROWS, SEQLEN), 0, 8) < 7).astype(jnp.int32), jax.random.fold_in(seeds[2], 1), 0, 1)
    ln1_gain = jnp.clip(1.0 + 0.15 * jax.random.normal(seeds[3], (D,), jnp.float32), 0.25, 1.75)
    ln1_shift = normal_values(seeds[4], (D,), 0.3, 3.0, (), jnp.float32)
    w_query = normal_values(seeds[5], (D, D), D ** -0.5, 0.25, ((1, 4),))
    w_key = normal_values(seeds[6], (D, D), D ** -0.5, 0.25, ((1, 4),))
    w_value = normal_values(seeds[7], (D, D), D ** -0.5, 0.25, ((1, 4),))
    w_out = normal_values(seeds[8], (D, D), (D // 2) ** -0.5, 0.375, ((0, 4),))
    ln2_gain = jnp.clip(1.0 + 0.15 * jax.random.normal(seeds[9], (D,), jnp.float32), 0.25, 1.75)
    ln2_shift = normal_values(seeds[10], (D,), 0.3, 3.0, (), jnp.float32)
    w_up = normal_values(seeds[11], (D, FF), D ** -0.5, 0.25, ((1, 4),))
    b_up = normal_values(seeds[12], (FF,), 0.5, 3.0, ((0, 4),), jnp.float32)
    w_down = normal_values(seeds[13], (FF, D), FF ** -0.5, 0.125, ((0, 4),))
    b_down = normal_values(seeds[14], (D,), 0.5, 3.0, (), jnp.float32)
    out_grad = normal_values(seeds[15], (ROWS, SEQLEN, D), 1.0, 6.0, ((1, 8),))
    return {"inputs": inputs, "doc_ids": doc_ids, "pad_mask": pad_mask, "ln1_gain": ln1_gain, "ln1_shift": ln1_shift, "w_query": w_query, "w_key": w_key, "w_value": w_value, "w_out": w_out, "ln2_gain": ln2_gain, "ln2_shift": ln2_shift, "w_up": w_up, "b_up": b_up, "w_down": w_down, "b_down": b_down, "out_grad": out_grad}


norm_eps = 1e-05
masked_score = -1e+30
highest = lax.Precision.HIGHEST

@jax.custom_vjp
def low(v):
    return lax.optimization_barrier(v.astype(jnp.bfloat16)).astype(jnp.float32)

@jax.custom_vjp
def low_back(v):
    return v

def low_keep(v):
    return (low(v), None)

def low_pass(kept, grad):
    return (grad,)

def back_keep(v):
    return (v, None)

def back_low(kept, grad):
    return (low(grad),)
low.defvjp(low_keep, low_pass)
low_back.defvjp(back_keep, back_low)

def rounded(values):
    return low(low_back(values))

def layer_norm(values, norm_gain, norm_shift):
    average = lax.optimization_barrier(jnp.mean(values, axis=-1, keepdims=True))
    centred = values - average
    spread = lax.optimization_barrier(jnp.mean(centred * centred, axis=-1, keepdims=True))
    return centred * lax.rsqrt(spread + norm_eps) * norm_gain + norm_shift

def gelu_exact(values):
    return jax.nn.gelu(values, approximate=False)

def join_forward(earlier, later_part):
    keys_before, values_before, count_before, tag_before = earlier
    keys_after, values_after, count_after, tag_after = later_part
    same_doc = tag_after == tag_before
    is_empty = tag_after < 0.0
    sum_keys = jnp.where(same_doc[..., None], keys_before + keys_after, keys_after)
    sum_values = jnp.where(same_doc[..., None], values_before + values_after, values_after)
    token_count = jnp.where(same_doc, count_before + count_after, count_after)
    sum_keys = jnp.where(is_empty[..., None], keys_before, sum_keys)
    sum_values = jnp.where(is_empty[..., None], values_before, sum_values)
    token_count = jnp.where(is_empty, count_before, token_count)
    doc_tag = jnp.where(is_empty, tag_before, tag_after)
    return (sum_keys, sum_values, token_count, doc_tag)

def project(left, right):
    return jnp.einsum('rtd,de->rte', left, right, precision=highest)

def row_attention(pieces):
    queries, key_rows, value_rows, row_docs, row_mask = pieces
    span_count = SEQLEN // SPAN
    span_shape = (span_count, SPAN, HEADS, HEAD_DIM)
    query_spans = queries.reshape(span_shape)
    key_spans = key_rows.reshape(span_shape)
    value_spans = value_rows.reshape(span_shape)
    doc_span = row_docs.reshape(span_count, SPAN)
    alive = row_mask.reshape(span_count, SPAN) == 1
    last_doc = doc_span[:, SPAN - 1]
    picked = ((doc_span == last_doc[:, None]) & alive).astype(jnp.float32)
    part_keys = jnp.einsum('st,stc->sc', picked, key_rows.reshape(span_count, SPAN, D), precision=highest)
    part_values = jnp.einsum('st,stc->sc', picked, value_rows.reshape(span_count, SPAN, D), precision=highest)
    part_count = lax.optimization_barrier(jnp.sum(picked, axis=1))
    part_tag = last_doc.astype(jnp.float32)

    def scan_step(state, element):
        return (join_forward(state, element), state)
    initial = (jnp.zeros((D,), jnp.float32), jnp.zeros((D,), jnp.float32), jnp.zeros((), jnp.float32), jnp.full((), -1.0, jnp.float32))
    _, prefix = lax.scan(scan_step, initial, (part_keys, part_values, part_count, part_tag))
    prefix_keys, prefix_values, prefix_count, prefix_tag = prefix
    divisor = jnp.maximum(prefix_count, 1.0)[:, None]
    key_bar = low(prefix_keys / divisor).reshape(span_count, HEADS, HEAD_DIM)
    value_bar = low(prefix_values / divisor).reshape(span_count, HEADS, HEAD_DIM)
    position = jnp.arange(SPAN)
    causal = position[:, None] >= position[None, :]
    diagonal = position[:, None] == position[None, :]
    local_ok = causal[None] & (doc_span[:, :, None] == doc_span[:, None, :]) & (alive[:, None, :] | diagonal[None])
    summary_ok = (doc_span.astype(jnp.float32) == prefix_tag[:, None]) & (prefix_count > 0.0)[:, None]
    local_scores = low_back(jnp.einsum('sthd,suhd->shtu', query_spans, key_spans, precision=highest))
    summary_scores = low_back(jnp.einsum('sthd,shd->sht', query_spans, key_bar, precision=highest)) + math.log(SPAN)
    local_scores = jnp.where(local_ok[:, None], local_scores, masked_score)
    summary_scores = jnp.where(summary_ok[:, None], summary_scores, masked_score)
    top_score = jnp.maximum(lax.optimization_barrier(jnp.max(local_scores, axis=-1)), summary_scores)
    local_exp = jnp.exp(local_scores - top_score[..., None])
    summary_exp = jnp.exp(summary_scores - top_score)
    total_exp = lax.optimization_barrier(jnp.sum(local_exp, axis=-1)) + summary_exp
    local_prob = low(local_exp / total_exp[..., None])
    summary_prob = low(summary_exp / total_exp)
    mixed_heads = jnp.einsum('shtu,suhd->sthd', local_prob, value_spans, precision=highest)
    mixed_heads = mixed_heads + jnp.einsum('sht,shd->sthd', summary_prob, value_bar, precision=highest)
    return mixed_heads.reshape(SEQLEN, D)

def forward(row_docs, row_mask, block_input, ln1_gain, ln1_shift, w_query, w_key, w_value, w_out, ln2_gain, ln2_shift, w_up, b_up, w_down, b_down):
    hidden1 = low(layer_norm(block_input, ln1_gain, ln1_shift))
    queries = rounded(project(hidden1, w_query) * (1.0 / math.sqrt(HEAD_DIM)))
    key_rows = rounded(project(hidden1, w_key))
    value_rows = rounded(project(hidden1, w_value))
    mixed_heads = lax.map(jax.checkpoint(row_attention), (queries, key_rows, value_rows, row_docs, row_mask))
    heads_out = rounded(mixed_heads)
    x_mid = block_input + low_back(project(heads_out, w_out))
    hidden2 = low(layer_norm(x_mid, ln2_gain, ln2_shift))
    up_proj = low_back(project(hidden2, w_up) + b_up)
    activation = low(gelu_exact(up_proj))
    return x_mid + low_back(project(activation, w_down)) + b_down

def reference(inputs, doc_ids, pad_mask, ln1_gain, ln1_shift, w_query, w_key, w_value, w_out, ln2_gain, ln2_shift, w_up, b_up, w_down, b_down, out_grad):
    primals = (inputs.astype(jnp.float32), ln1_gain.astype(jnp.float32), ln1_shift.astype(jnp.float32), w_query.astype(jnp.float32), w_key.astype(jnp.float32), w_value.astype(jnp.float32), w_out.astype(jnp.float32), ln2_gain.astype(jnp.float32), ln2_shift.astype(jnp.float32), w_up.astype(jnp.float32), b_up.astype(jnp.float32), w_down.astype(jnp.float32), b_down.astype(jnp.float32))
    result, pullback = jax.vjp(partial(forward, doc_ids, pad_mask), *primals)
    gradients = pullback(out_grad.astype(jnp.float32))
    return (result.astype(jnp.bfloat16), gradients[0], gradients[1], gradients[2], gradients[3], gradients[4], gradients[5], gradients[6], gradients[7], gradients[8], gradients[9], gradients[10], gradients[11], gradients[12])
```

```python
import math

import jax
import jax.numpy as jnp
from jax import lax
from jax.experimental import pallas as pl
from jax.experimental.pallas import tpu as pltpu
from jax.sharding import PartitionSpec as P

HEAD_DIM = 64
SPAN = 128
LANES = 128
NORM_EPS = 1e-05
MASKED = -1e30
VMEM_BYTES = 56 * 2**20
f32, bf16 = jnp.float32, jnp.bfloat16


def nn(a, b):
    return lax.dot_general(a, b, (((1,), (0,)), ((), ())), preferred_element_type=f32)


def nt(a, b):
    return lax.dot_general(a, b, (((1,), (1,)), ((), ())), preferred_element_type=f32)


def tn(a, b):
    return lax.dot_general(a, b, (((0,), (0,)), ((), ())), preferred_element_type=f32)


def hi_lo(v):
    hi = v.astype(bf16).astype(f32)
    return jnp.concatenate([hi, v - hi], axis=0).astype(bf16)


def twice(v):
    return jnp.concatenate([v, v], axis=0).astype(bf16)


def norm_parts(x):
    mean = jnp.mean(x, axis=-1, keepdims=True)
    centred = x - mean
    rstd = lax.rsqrt(jnp.mean(centred * centred, axis=-1, keepdims=True) + NORM_EPS)
    return centred * rstd, rstd


def norm_back(y, xhat, rstd):
    return rstd * (
        y
        - jnp.mean(y, axis=-1, keepdims=True)
        - xhat * jnp.mean(y * xhat, axis=-1, keepdims=True)
    )


def gelu_parts(u):
    z = jnp.abs(u)
    t = 1.0 / (1.0 + (0.3275911 * math.sqrt(0.5)) * z)
    e = jnp.exp(-0.5 * u * u)
    poly = t * (
        0.5 * 0.254829592
        + t
        * (
            0.5 * -0.284496736
            + t * (0.5 * 1.421413741 + t * (0.5 * -1.453152027 + t * (0.5 * 1.061405429)))
        )
    )
    tail = poly * e
    phi = jnp.where(u >= 0.0, 1.0 - tail, tail)
    return phi, phi + u * e * (1.0 / math.sqrt(2.0 * math.pi))


def call(body, grid, prefetch, in_specs, out_specs, out_shape, scratch=(), flops=0, nbytes=0):
    return pl.pallas_call(
        body,
        grid_spec=pltpu.PrefetchScalarGridSpec(
            num_scalar_prefetch=prefetch,
            grid=grid,
            in_specs=in_specs,
            out_specs=out_specs,
            scratch_shapes=list(scratch),
        ),
        out_shape=out_shape,
        compiler_params=pltpu.CompilerParams(vmem_limit_bytes=VMEM_BYTES),
        cost_estimate=pl.CostEstimate(flops=flops, bytes_accessed=nbytes, transcendentals=0),
    )


def whole(shape):
    return pl.BlockSpec(shape, lambda *_: (0,) * len(shape))


def shape(dims, dtype):
    return jax.ShapeDtypeStruct(dims, dtype)


def project_body(spans, doc_s, doc_ref, pad_ref, x_ref, g_ref, b_ref, w_ref, h_ref, q_ref, k_ref, v_ref, m_ref, p_ref):
    row_at = pl.program_id(0)
    width = x_ref.shape[-1]
    xhat, _ = norm_parts(x_ref[...].astype(f32))
    h = (xhat * g_ref[...] + b_ref[...]).astype(bf16)
    h_ref[...] = h
    q_ref[...] = (nn(h, w_ref[:, :width]) * (1.0 / math.sqrt(HEAD_DIM))).astype(bf16)
    k = nn(h, w_ref[:, width : 2 * width]).astype(bf16)
    v = nn(h, w_ref[:, 2 * width :]).astype(bf16)
    k_ref[...] = k
    v_ref[...] = v
    doc = doc_ref[0]
    alive = pad_ref[0] == 1
    rows, region = m_ref.shape[1:]
    lane = lax.broadcasted_iota(jnp.int32, (rows, region), 1)
    line = lax.broadcasted_iota(jnp.int32, (rows, region), 0)
    tag_line = lax.broadcasted_iota(jnp.int32, (rows, LANES), 0)
    picked = jnp.zeros((rows, region), f32)
    tag = jnp.zeros((rows, LANES), f32)
    for s in range(1, spans + 1):
        last = doc_s[row_at, s * SPAN - 1]
        hit = (line == s) & (lane < s * SPAN) & (doc == last) & alive
        picked = jnp.where(hit, 1.0, picked)
        tag = jnp.where(tag_line == s, last.astype(f32), tag)
    m_ref[0] = picked
    mb = picked.astype(bf16)
    p_ref[0, :, :width] = nn(mb, k)
    p_ref[0, :, width : 2 * width] = nn(mb, v)
    p_ref[0, :, 2 * width : 3 * width] = nn(mb, h)
    count = jnp.sum(picked, axis=1, keepdims=True)
    p_ref[0, :, 3 * width : 3 * width + LANES] = jnp.broadcast_to(count, (rows, LANES))
    p_ref[0, :, 3 * width + LANES :] = tag


def project(docs, pads, x, gain, shift, w, rows, region):
    tokens, width = x.shape
    spans = region // SPAN
    lines = -(-(spans + 1) // 8) * 8
    wide = 3 * width + 2 * LANES
    tok = pl.BlockSpec((region, width), lambda i, *_: (i, 0))
    ids = pl.BlockSpec((1, 1, region), lambda i, *_: (i, 0, 0))

    def body(*refs):
        project_body(spans, *refs)

    return call(
        body,
        (rows,),
        1,
        [ids, ids, tok, whole((1, width)), whole((1, width)), whole(w.shape)],
        [
            tok,
            tok,
            tok,
            tok,
            pl.BlockSpec((1, lines, region), lambda i, *_: (i, 0, 0)),
            pl.BlockSpec((1, lines, wide), lambda i, *_: (i, 0, 0)),
        ],
        [shape((tokens, width), bf16)] * 4
        + [shape((rows, lines, region), f32), shape((rows, lines, wide), f32)],
        flops=2 * tokens * width * 3 * width,
        nbytes=12 * tokens * width,
    )(docs, docs[:, None], pads[:, None], x, gain[None], shift[None], w)


def halves():
    lane = lax.broadcasted_iota(jnp.int32, (1, LANES), 1)
    first = (lane < HEAD_DIM).astype(f32)
    return first.astype(bf16), (1.0 - first).astype(bf16)


def split(v, masks):
    return jnp.concatenate([v * masks[0], v * masks[1]], axis=0)


def local_body(doc_ref, pad_ref, q_ref, k_ref, v_ref, e_ref, o_ref, top_ref, sum_ref):
    doc = doc_ref[0].astype(f32)
    code = jnp.where(pad_ref[0] == 1, doc, -2.0)
    code_u = jnp.broadcast_to(code, (SPAN, SPAN)).T
    u = lax.broadcasted_iota(jnp.int32, (SPAN, SPAN), 0)
    t = lax.broadcasted_iota(jnp.int32, (SPAN, SPAN), 1)
    ok = ((u < t) & (code_u == doc)) | (u == t)
    masks = halves()
    for pair in range(q_ref.shape[-1] // LANES):
        lanes = slice(pair * LANES, (pair + 1) * LANES)
        scores = nt(split(k_ref[:, lanes], masks), q_ref[:, lanes])
        parts = []
        for half in range(2):
            head = 2 * pair + half
            s = jnp.where(ok, scores[half * SPAN : (half + 1) * SPAN], MASKED)
            top = jnp.max(s, axis=0, keepdims=True)
            e = jnp.exp(s - top)
            top_ref[0, head : head + 1, :] = top
            sum_ref[0, head : head + 1, :] = jnp.sum(e, axis=0, keepdims=True)
            parts.append(e.astype(bf16))
        both = jnp.concatenate(parts, axis=0)
        e_ref[0, pair * 2 * SPAN : (pair + 1) * 2 * SPAN, :] = both
        o_ref[:, lanes] = tn(both, split(v_ref[:, lanes], masks))


def local_attention(docs3, pads3, q, k, v):
    tokens, width = q.shape
    count = tokens // SPAN
    heads = width // HEAD_DIM
    ids = pl.BlockSpec((1, 1, SPAN), lambda i: (i, 0, 0))
    tok = pl.BlockSpec((SPAN, width), lambda i: (i, 0))
    per_head = pl.BlockSpec((1, heads, SPAN), lambda i: (i, 0, 0))
    return call(
        local_body,
        (count,),
        0,
        [ids, ids, tok, tok, tok],
        [pl.BlockSpec((1, heads * SPAN, SPAN), lambda i: (i, 0, 0)), tok, per_head, per_head],
        [shape((count, heads * SPAN, SPAN), bf16), shape((tokens, width), f32)]
        + [shape((count, heads, SPAN), f32)] * 2,
        flops=8 * tokens * SPAN * width,
        nbytes=12 * tokens * width,
    )(docs3, pads3, q, k, v)


def head_rows(rows, width):
    line = lax.broadcasted_iota(jnp.int32, (rows, width), 0)
    lane = lax.broadcasted_iota(jnp.int32, (rows, width), 1)
    return lane // HEAD_DIM == line


def merge_body(
    spans, me_s, doc_s, every_ref, p_ref, doc_ref, q_ref, o_ref, top_ref, sum_ref, x_ref, w_ref,
    heads_ref, mid_ref, kb_ref, vb_ref, scale_ref, ps_ref, misc_ref,
):
    row_at = pl.program_id(0)
    me = me_s[0]
    devices = every_ref.shape[0]
    width = q_ref.shape[-1]
    heads = width // HEAD_DIM
    at_count = 3 * width
    at_tag = at_count + LANES

    carry = jnp.zeros((1, at_tag), f32)
    tag_in = jnp.full((1, LANES), -1.0, f32)
    run = carry
    run_tag = tag_in
    for d in range(1, devices):
        before = every_ref[d - 1, row_at]
        tag = before[:, at_tag:]
        same = (tag == run_tag).astype(f32)[:, :1]
        run = before[:, :at_tag] + same * run
        run_tag = tag
        mine = me == d
        carry = jnp.where(mine, run, carry)
        tag_in = jnp.where(mine, tag, tag_in)

    own = head_rows(heads, width)
    spread = twice(own.astype(f32))
    for s in range(spans):
        toks = slice(s * SPAN, (s + 1) * SPAN)
        if s == 0:
            run_doc = tag_in
        else:
            run_doc = jnp.full((1, LANES), doc_s[row_at, s * SPAN - 1].astype(f32))
        flag = (tag_in == run_doc).astype(f32)
        total = p_ref[0, s : s + 1, :at_tag] + flag[:, :1] * carry
        count = total[:, at_count:]
        divisor = jnp.maximum(count, 1.0)
        k_bar = total[:, :width] / divisor[:, :1]
        v_bar = total[:, width : 2 * width] / divisor[:, :1]
        k_bd = jnp.where(own, k_bar, 0.0).astype(bf16)
        v_bd = jnp.where(own, v_bar, 0.0).astype(bf16)
        kb_ref[s] = k_bd
        vb_ref[s] = v_bd
        present = (doc_ref[s].astype(f32) == run_doc) & (count > 0.0)
        scores = nt(k_bd, q_ref[toks]) + math.log(SPAN)
        scores = jnp.where(present, scores, MASKED)
        top_local = top_ref[s]
        top = jnp.maximum(top_local, scores)
        scale = jnp.exp(top_local - top)
        weight = jnp.exp(scores - top)
        inverse = 1.0 / (scale * sum_ref[s] + weight)
        scale = scale * inverse
        weight = weight * inverse
        scale_ref[s] = scale
        ps_ref[s] = weight
        misc_ref[s] = jnp.concatenate([1.0 / divisor, flag], axis=0)
        mixed = o_ref[toks] * tn(hi_lo(scale), spread) + tn(weight.astype(bf16), v_bd)
        heads_ref[toks] = mixed.astype(bf16)
    mid_ref[...] = x_ref[...].astype(f32) + nn(heads_ref[...], w_ref[...])


def merge(me, docs, docs3, every, prefix, q, o_local, top, total, x, w_out, rows, region):
    tokens, width = q.shape
    spans = region // SPAN
    heads = width // HEAD_DIM
    count = tokens // SPAN
    tok = pl.BlockSpec((region, width), lambda i, *_: (i, 0))
    ids = pl.BlockSpec((spans, 1, SPAN), lambda i, *_: (i, 0, 0))
    per_head = pl.BlockSpec((spans, heads, SPAN), lambda i, *_: (i, 0, 0))
    bars = pl.BlockSpec((spans, heads, width), lambda i, *_: (i, 0, 0))

    def body(*refs):
        merge_body(spans, *refs)

    return call(
        body,
        (rows,),
        2,
        [
            whole(every.shape),
            pl.BlockSpec((1,) + prefix.shape[1:], lambda i, *_: (i, 0, 0)),
            ids, tok, tok, per_head, per_head, tok, whole(w_out.shape),
        ],
        [tok, tok, bars, bars, per_head, per_head, pl.BlockSpec((spans, 2, SPAN), lambda i, *_: (i, 0, 0))],
        [
            shape((tokens, width), bf16),
            shape((tokens, width), f32),
            shape((count, heads, width), bf16),
            shape((count, heads, width), bf16),
            shape((count, heads, SPAN), f32),
            shape((count, heads, SPAN), f32),
            shape((count, 2, SPAN), f32),
        ],
        flops=2 * tokens * width * width,
        nbytes=14 * tokens * width,
    )(me, docs, every, prefix, docs3, q, o_local, top, total, x, w_out)


def ffn_body(
    at_s, mid_ref, g_ref, heads_ref, gain_ref, shift_ref, wu_ref, bu_ref, wd_ref, bd_ref, wo_ref,
    out_ref, dmid_ref, do_ref, gwu_ref, gwd_ref, gwo_ref, gbu_ref, small_ref, y_acc, dn_acc,
):
    groups = wu_ref.shape[0]

    @pl.when(pl.program_id(0) == 0)
    def _():
        gwu_ref[...] = jnp.zeros_like(gwu_ref)
        gwd_ref[...] = jnp.zeros_like(gwd_ref)
        gwo_ref[...] = jnp.zeros_like(gwo_ref)
        gbu_ref[...] = jnp.zeros_like(gbu_ref)
        small_ref[...] = jnp.zeros_like(small_ref)

    xhat, _ = norm_parts(mid_ref[...])
    h = (xhat * gain_ref[...] + shift_ref[...]).astype(bf16)
    y_acc[...] = jnp.zeros_like(y_acc)
    dn_acc[...] = jnp.zeros_like(dn_acc)

    def hidden(j, _):
        gm = g_ref[...]
        up = nn(h, wu_ref[j]) + bu_ref[j]
        phi, slope = gelu_parts(up)
        a = (up * phi).astype(bf16)
        y_acc[...] += nn(a, wd_ref[j])
        du = (nt(gm, wd_ref[j]) * slope).astype(bf16)
        dn_acc[...] += nt(du, wu_ref[j])

        @pl.when(j == at_s[0])
        def _():
            gwd_ref[...] += tn(a, gm)
            gwu_ref[...] += tn(h, du)
            gbu_ref[...] += jnp.sum(du.astype(f32), axis=0, keepdims=True)

        return 0

    lax.fori_loop(0, groups, hidden, 0)
    mid = mid_ref[...]
    out_ref[...] = (mid + y_acc[...] + bd_ref[...]).astype(bf16)
    xhat, rstd = norm_parts(mid)
    g = g_ref[...].astype(f32)
    dn = dn_acc[...]
    small_ref[0:1] += jnp.sum(dn * xhat, axis=0, keepdims=True)
    small_ref[1:2] += jnp.sum(dn, axis=0, keepdims=True)
    small_ref[2:3] += jnp.sum(g, axis=0, keepdims=True)
    dmid = g + norm_back(dn * gain_ref[...], xhat, rstd)
    dmid_ref[...] = dmid
    gx = dmid.astype(bf16)
    do_ref[...] = nt(gx, wo_ref[...]).astype(bf16)
    gwo_ref[...] += tn(heads_ref[...], gx)


def feed_forward(at, mid, g, heads_out, gain, shift, wu, bu, wd, bd, wo, block):
    tokens, width = mid.shape
    groups, _, hidden = wu.shape
    chunk = tokens // 4
    tok = pl.BlockSpec((chunk, width), lambda i, *_: (i, 0))
    fixed = whole
    return call(
        ffn_body,
        (4,),
        1,
        [
            tok, tok,
            pl.BlockSpec((chunk, block), lambda i, s: (i, s[1])),
            fixed((1, width)), fixed((1, width)), fixed(wu.shape), fixed((groups, 1, hidden)), fixed(wd.shape),
            fixed((1, width)), fixed(wo.shape),
        ],
        [tok, tok, tok, fixed((width, hidden)), fixed((hidden, width)), fixed((block, width)),
         fixed((1, hidden)), fixed((8, width))],
        [
            shape((tokens, width), bf16),
            shape((tokens, width), f32),
            shape((tokens, width), bf16),
            shape((width, hidden), f32),
            shape((hidden, width), f32),
            shape((block, width), f32),
            shape((1, hidden), f32),
            shape((8, width), f32),
        ],
        scratch=[pltpu.VMEM((chunk, width), f32)] * 2,
        flops=8 * tokens * width * hidden * groups,
        nbytes=16 * tokens * width,
    )(at, mid, g, heads_out, gain[None], shift[None], wu, bu.reshape(groups, 1, hidden), wd, bd[None], wo)


def back_body(
    spans, q_ref, k_ref, v_ref, do_ref, e_ref, scale_ref, ps_ref, kb_ref, vb_ref, m_ref, misc_ref,
    dq_ref, dk_ref, dv_ref, g_ref, shares,
):
    s = spans - 1 - pl.program_id(1)
    width = q_ref.shape[-1]

    @pl.when(pl.program_id(1) == 0)
    def _():
        shares[...] = jnp.zeros_like(shares)
        g_ref[...] = jnp.zeros_like(g_ref)

    masks = halves()
    own = head_rows(width // HEAD_DIM, width)
    later = hi_lo(shares[...])
    reach = twice(m_ref[0])
    do_all = do_ref[...]
    weight = ps_ref[0]
    dp_sum = nt(vb_ref[0], do_all)
    r_rows = []
    for pair in range(width // LANES):
        lanes = slice(pair * LANES, (pair + 1) * LANES)
        q, k, v, do = q_ref[:, lanes], k_ref[:, lanes], v_ref[:, lanes], do_ref[:, lanes]
        dp = nt(split(v, masks), do)
        probs, grads = [], []
        for half in range(2):
            head = 2 * pair + half
            p = e_ref[0, head * SPAN : (head + 1) * SPAN, :].astype(f32) * scale_ref[0, head : head + 1, :]
            dp_head = dp[half * SPAN : (half + 1) * SPAN]
            r = jnp.sum(p * dp_head, axis=0, keepdims=True)
            r = r + weight[head : head + 1] * dp_sum[head : head + 1]
            r_rows.append(r)
            probs.append(p.astype(bf16))
            grads.append((p * (dp_head - r)).astype(bf16))
        dv = nn(jnp.concatenate(probs, axis=1), split(do, masks))
        dk = nn(jnp.concatenate(grads, axis=1), split(q, masks))
        dq_ref[:, lanes] = tn(jnp.concatenate(grads, axis=0), split(k, masks)).astype(bf16)
        wide = slice(width + pair * LANES, width + (pair + 1) * LANES)
        dk_ref[:, lanes] = (dk + tn(reach, later[:, lanes])).astype(bf16)
        dv_ref[:, lanes] = (dv + tn(reach, later[:, wide])).astype(bf16)
    ds_sum = (weight * (dp_sum - jnp.concatenate(r_rows, axis=0))).astype(bf16)
    dq = dq_ref[...].astype(f32) + tn(ds_sum, kb_ref[0])
    dq_ref[...] = (dq.astype(bf16).astype(f32) * (1.0 / math.sqrt(HEAD_DIM))).astype(bf16)
    inverse = misc_ref[0, 0:1, :1]
    flag = misc_ref[0, 1:2, :1]
    gk = jnp.sum(jnp.where(own, nn(ds_sum, q_ref[...]), 0.0), axis=0, keepdims=True) * inverse
    gv = jnp.sum(jnp.where(own, nn(weight.astype(bf16), do_all), 0.0), axis=0, keepdims=True) * inverse
    shares[pl.ds(s, 1), :width] = gk
    shares[pl.ds(s, 1), width:] = gv
    g_ref[0, :, :width] += flag * gk
    g_ref[0, :, width:] += flag * gv


def attention_back(q, k, v, do, e, scale, ps, kb, vb, m, misc, rows, region):
    tokens, width = q.shape
    spans = region // SPAN
    heads = width // HEAD_DIM
    lines = m.shape[1]

    def at(r, i):
        return r * spans + spans - 1 - i

    tok = pl.BlockSpec((SPAN, width), lambda r, i: (at(r, i), 0))
    per_head = pl.BlockSpec((1, heads, SPAN), lambda r, i: (at(r, i), 0, 0))
    bars = pl.BlockSpec((1, heads, width), lambda r, i: (at(r, i), 0, 0))

    def body(*refs):
        back_body(spans, *refs)

    return call(
        body,
        (rows, spans),
        0,
        [
            tok, tok, tok, tok,
            pl.BlockSpec((1, heads * SPAN, SPAN), lambda r, i: (at(r, i), 0, 0)),
            per_head, per_head, bars, bars,
            pl.BlockSpec((1, lines, SPAN), lambda r, i: (r, 0, spans - 1 - i)),
            pl.BlockSpec((1, 2, SPAN), lambda r, i: (at(r, i), 0, 0)),
        ],
        [tok, tok, tok, pl.BlockSpec((1, 1, 2 * width), lambda r, i: (r, 0, 0))],
        [shape((tokens, width), bf16)] * 3 + [shape((rows, 1, 2 * width), f32)],
        scratch=[pltpu.VMEM((lines, 2 * width), f32)],
        flops=16 * tokens * SPAN * width,
        nbytes=20 * tokens * width,
    )(q, k, v, do, e, scale, ps, kb, vb, m, misc)


def weights_body(h_ref, dq_ref, dk_ref, dv_ref, o_ref):
    @pl.when(pl.program_id(0) == 0)
    def _():
        o_ref[...] = jnp.zeros_like(o_ref)

    h = h_ref[...]
    for i, ref in enumerate((dq_ref, dk_ref, dv_ref)):
        o_ref[i] += tn(h, ref[...])


def weight_grads(at, h, dq, dk, dv, block):
    tokens, width = h.shape
    chunk = tokens // 2
    mine = pl.BlockSpec((chunk, block), lambda i, s: (i, s[1]))

    def body(at_s, *refs):
        weights_body(*refs)

    return call(
        body,
        (2,),
        1,
        [pl.BlockSpec((chunk, width), lambda i, *_: (i, 0)), mine, mine, mine],
        whole((3, width, block)),
        shape((3, width, block), f32),
        flops=6 * tokens * width * block,
        nbytes=2 * tokens * (width + 3 * block),
    )(at, h, dq, dk, dv)


def input_body(
    spans, me_s, every_ref, back_ref, m_ref, x_ref, gain_ref, dmid_ref, dq_ref, dk_ref, dv_ref, w_ref,
    gi_ref, small_ref, in_ref,
):
    row_at = pl.program_id(0)
    me = me_s[0]
    devices = every_ref.shape[0]
    width = x_ref.shape[-1]
    at_tag = 3 * width + LANES

    @pl.when(row_at == 0)
    def _():
        small_ref[...] = jnp.zeros_like(small_ref)

    run = jnp.zeros((1, 2 * width), f32)
    mine = run
    in_ref[0, devices - 1 : devices, :] = run
    tag = every_ref[devices - 1, row_at][:, at_tag:]
    for d in reversed(range(devices - 1)):
        tag_here = every_ref[d, row_at][:, at_tag:]
        same = (tag == tag_here).astype(f32)[:, :1]
        run = back_ref[d + 1, row_at] + same * run
        tag = tag_here
        in_ref[0, d : d + 1, :] = run
        mine = jnp.where(me == d, run, mine)

    lines = m_ref.shape[1]
    arrived = jnp.broadcast_to(mine, (8, 2 * width))
    through = nt(hi_lo(arrived), w_ref[:, width:])
    through = through[0:8] + through[8:16]
    line = lax.broadcasted_iota(jnp.int32, (lines, width), 0)
    through = jnp.where(line == spans, jnp.broadcast_to(through[:1], (lines, width)), 0.0)
    dn = (
        nt(dq_ref[...], w_ref[:, :width])
        + nt(dk_ref[...], w_ref[:, width : 2 * width])
        + nt(dv_ref[...], w_ref[:, 2 * width :])
        + tn(twice(m_ref[0]), hi_lo(through))
    )
    xhat, rstd = norm_parts(x_ref[...].astype(f32))
    small_ref[0:1] += jnp.sum(dn * xhat, axis=0, keepdims=True)
    small_ref[1:2] += jnp.sum(dn, axis=0, keepdims=True)
    gi_ref[...] = dmid_ref[...] + norm_back(dn * gain_ref[...], xhat, rstd)


def input_grads(me, every, back, m, x, gain, dmid, dq, dk, dv, w, rows, region):
    tokens, width = x.shape
    devices = every.shape[0]
    tok = pl.BlockSpec((region, width), lambda i, *_: (i, 0))

    def body(*refs):
        input_body(region // SPAN, *refs)

    return call(
        body,
        (rows,),
        1,
        [
            whole(every.shape), whole(back.shape),
            pl.BlockSpec((1,) + m.shape[1:], lambda i, *_: (i, 0, 0)),
            tok, whole((1, width)), tok, tok, tok, tok, whole(w.shape),
        ],
        [tok, whole((8, width)), pl.BlockSpec((1, devices, 2 * width), lambda i, *_: (i, 0, 0))],
        [shape((tokens, width), f32), shape((8, width), f32), shape((rows, devices, 2 * width), f32)],
        flops=6 * tokens * width * width,
        nbytes=16 * tokens * width,
    )(me, every, back, m, x, gain[None], dmid, dq, dk, dv, w)


def narrow_body(w_ref, o_ref):
    o_ref[...] = w_ref[...].astype(bf16)


def narrow(w):
    lines, width = w.shape
    chunk = lines // 4
    block = pl.BlockSpec((chunk, width), lambda i: (i, 0))
    return call(narrow_body, (4,), 0, [block], block, shape(w.shape, bf16), nbytes=6 * w.size)(w)


def side_by_side(every, parts):
    groups, width, wide = every.shape
    share = wide // parts
    if share % LANES:
        flat = narrow(every.reshape(groups * width, wide)).reshape(groups, width, parts, share)
        return flat.transpose(1, 2, 0, 3).reshape(width, parts * groups * share)

    def body(w_ref, o_ref):
        o_ref[...] = w_ref[0].astype(bf16)

    return call(
        body,
        (parts, groups),
        0,
        [pl.BlockSpec((1, width, share), lambda p, g: (g, 0, p))],
        pl.BlockSpec((width, share), lambda p, g: (0, p * groups + g)),
        shape((width, parts * groups * share), bf16),
        nbytes=6 * every.size,
    )(every)


def spread_weights(part, devices, here):
    rows = part.shape[0] // devices
    mine = lax.dynamic_slice_in_dim(part, here * rows, rows, 0).astype(f32)
    return lax.all_gather(mine, ("head", "seq"), tiled=True)


def on_device(
    inputs, doc_ids, pad_mask, ln1_gain, ln1_shift, w_query, w_key, w_value, w_out,
    ln2_gain, ln2_shift, w_up, b_up, w_down, b_down, out_grad,
):
    rows, region, width = inputs.shape
    tokens = rows * region
    devices = lax.axis_size("seq")
    groups = lax.axis_size("head")
    here = lax.axis_index("seq")
    group = lax.axis_index("head")
    share = width // groups
    block = max(share, LANES)
    me = here.astype(jnp.int32)[None]
    at = jnp.stack([group, group * share // block]).astype(jnp.int32)

    w_in = spread_weights(jnp.concatenate([w_query, w_key, w_value], axis=1), devices, here)
    w_in = side_by_side(w_in.reshape(groups, width, 3 * share), 3)
    wo = narrow(spread_weights(w_out, devices, here))
    wu = narrow(spread_weights(w_up, devices, here)).reshape((groups,) + w_up.shape)
    wd = narrow(spread_weights(w_down, devices, here)).reshape((groups,) + w_down.shape)
    bu = lax.all_gather(b_up, "head")

    x = inputs.reshape(tokens, width)
    g = out_grad.reshape(tokens, width)
    docs3 = doc_ids.reshape(tokens // SPAN, 1, SPAN)
    pads3 = pad_mask.reshape(tokens // SPAN, 1, SPAN)

    h1, q, k, v, m, prefix = project(doc_ids, pad_mask, x, ln1_gain, ln1_shift, w_in, rows, region)
    spans = region // SPAN
    every = lax.all_gather(prefix[:, spans : spans + 1], "seq")
    e, o_local, top, total = local_attention(docs3, pads3, q, k, v)
    heads_out, mid, kb, vb, scale, ps, misc = merge(
        me, doc_ids, docs3, every, prefix, q, o_local, top, total, x, wo, rows, region
    )
    out, dmid, do, gwu, gwd, gwo, gbu, small2 = feed_forward(
        at, mid, g, heads_out, ln2_gain, ln2_shift, wu, bu, wd, b_down, wo, block
    )
    dq, dk, dv, g_back = attention_back(q, k, v, do, e, scale, ps, kb, vb, m, misc, rows, region)
    back = lax.all_gather(g_back, "seq")
    gw = weight_grads(at, h1, dq, dk, dv, block)
    grad_inputs, small1, arrived = input_grads(
        me, every, back, m, x, ln1_gain, dmid, dq, dk, dv, w_in, rows, region
    )

    gwu, gwd, gwo, gbu, small2 = lax.psum((gwu, gwd, gwo, gbu, small2), "seq")
    gw = lax.psum(gw, "seq")
    small1 = lax.psum(small1, "seq")
    picked = every[:, :, 0, 2 * width : 3 * width].transpose(1, 0, 2).reshape(rows * devices, width)
    arrived = arrived.reshape(rows * devices, 2, width)
    arrived = lax.dynamic_slice_in_dim(arrived, at[1] * block, block, 2)
    late = jnp.einsum("nc,nie->ice", picked, arrived, precision=lax.Precision.HIGHEST)
    gw = gw + jnp.concatenate([jnp.zeros_like(late[:1]), late], axis=0)
    if block != share:
        inner = group * share - at[1] * block
        gw = lax.dynamic_slice_in_dim(gw, inner, share, 2)
        gwo = lax.dynamic_slice_in_dim(gwo, inner, share, 0)
    return (
        out.reshape(rows, region, width),
        grad_inputs.reshape(rows, region, width),
        small1[0],
        small1[1],
        gw[0],
        gw[1],
        gw[2],
        gwo,
        small2[0],
        small2[1],
        gwu,
        gbu[0],
        gwd,
        small2[2],
    )


def solution(mesh):
    tok = P(None, "seq", None)
    ids = P(None, "seq")
    cols, lines = P(None, "head"), P("head", None)
    in_specs = (
        tok, ids, ids, P(), P(), cols, cols, cols, lines, P(), P(), cols, P("head"), lines, P(), tok,
    )
    out_specs = (
        tok, tok, P(), P(), cols, cols, cols, lines, P(), P(), cols, P("head"), lines, P(),
    )
    return jax.shard_map(on_device, mesh=mesh, in_specs=in_specs, out_specs=out_specs, check_vma=False)
```

```python
import math

import jax
import jax.numpy as jnp
from jax import lax
from jax.experimental import pallas as pl
from jax.experimental.pallas import tpu as pltpu
from jax.sharding import PartitionSpec as P

HEAD_DIM = 64
SPAN = 128
LANES = 128
NORM_EPS = 1e-05
MASKED = -1e30
f32, bf16 = jnp.float32, jnp.bfloat16


def nn(a, b):
    return lax.dot_general(a, b, (((1,), (0,)), ((), ())), preferred_element_type=f32)


def nt(a, b):
    return lax.dot_general(a, b, (((1,), (1,)), ((), ())), preferred_element_type=f32)


def tn(a, b):
    return lax.dot_general(a, b, (((0,), (0,)), ((), ())), preferred_element_type=f32)


def hi_lo(v):
    hi = v.astype(bf16).astype(f32)
    return jnp.concatenate([hi, v - hi], axis=0).astype(bf16)


def twice(v):
    return jnp.concatenate([v, v], axis=0).astype(bf16)


def norm_parts(x):
    mean = jnp.mean(x, axis=-1, keepdims=True)
    centred = x - mean
    rstd = lax.rsqrt(jnp.mean(centred * centred, axis=-1, keepdims=True) + NORM_EPS)
    return centred * rstd, rstd


def norm_back(y, xhat, rstd):
    return rstd * (
        y
        - jnp.mean(y, axis=-1, keepdims=True)
        - xhat * jnp.mean(y * xhat, axis=-1, keepdims=True)
    )


def gelu_parts(u):
    z = jnp.abs(u)
    t = 1.0 / (1.0 + (0.3275911 * math.sqrt(0.5)) * z)
    e = jnp.exp(-0.5 * u * u)
    poly = t * (
        0.5 * 0.254829592
        + t
        * (
            0.5 * -0.284496736
            + t * (0.5 * 1.421413741 + t * (0.5 * -1.453152027 + t * (0.5 * 1.061405429)))
        )
    )
    tail = poly * e
    phi = jnp.where(u >= 0.0, 1.0 - tail, tail)
    return phi, phi + u * e * (1.0 / math.sqrt(2.0 * math.pi))


def call(body, grid, prefetch, in_specs, out_specs, out_shape, scratch=(), us=2, mib=56, aliases=None, after=()):
    first, last = prefetch + len(in_specs), prefetch + len(in_specs) + len(after)

    def only(*refs):
        body(*refs[:first], *refs[last:])

    kernel = pl.pallas_call(
        only,
        input_output_aliases=aliases or {},
        grid_spec=pltpu.PrefetchScalarGridSpec(
            num_scalar_prefetch=prefetch,
            grid=grid,
            in_specs=list(in_specs) + [pl.BlockSpec(memory_space=pl.ANY)] * len(after),
            out_specs=out_specs,
            scratch_shapes=list(scratch),
        ),
        out_shape=out_shape,
        compiler_params=pltpu.CompilerParams(vmem_limit_bytes=mib * 2**20),
        cost_estimate=pl.CostEstimate(flops=int(us * 1.1e9), bytes_accessed=int(us * 3.5e6), transcendentals=0),
    )
    return lambda *operands: kernel(*operands, *after)


def whole(shape):
    return pl.BlockSpec(shape, lambda *_: (0,) * len(shape))


def shape(dims, dtype):
    return jax.ShapeDtypeStruct(dims, dtype)


def halves():
    lane = lax.broadcasted_iota(jnp.int32, (1, LANES), 1)
    first = (lane < HEAD_DIM).astype(f32)
    return first.astype(bf16), (1.0 - first).astype(bf16)


def split(v, masks):
    return jnp.concatenate([v * masks[0], v * masks[1]], axis=0)


def head_lines(bars):
    line = lax.broadcasted_iota(jnp.int32, (8, LANES), 0)
    lane = lax.broadcasted_iota(jnp.int32, (8, LANES), 1)
    own = lane // HEAD_DIM == line
    lines = [jnp.where(own, bars[s : s + 1], 0.0) for s in range(bars.shape[0])]
    return jnp.concatenate(lines, axis=0).astype(bf16)


def eight(rows):
    return jnp.concatenate(rows + [jnp.zeros((8 - len(rows), rows[0].shape[1]), f32)], axis=0)


def diagonal(blocks, lines):
    zero = jnp.zeros_like(blocks[0])
    rows = [jnp.concatenate([b if i == j else zero for j in range(len(blocks))], axis=1) for i, b in enumerate(blocks)]
    rows += [jnp.zeros_like(rows[0])] * (lines - len(blocks))
    return jnp.concatenate(rows, axis=0).astype(bf16)


def shares_body(at_s, q_ref, k_ref, v_ref, a_ref):
    rows = q_ref.shape[0]
    for i, ref in enumerate((q_ref, k_ref, v_ref)):
        a_ref[i * rows : (i + 1) * rows] = ref[...].astype(f32)


def attention_share(at, wq, wk, wv, devices):
    width, share = wq.shape
    rows = width // devices
    spec = pl.BlockSpec((rows, share), lambda i, s: (s[0], 0))
    return call(
        shares_body, (1,), 1, [spec] * 3, whole((3 * rows, share)), shape((3 * rows, share), f32)
    )(at, wq, wk, wv)


def down_rows(device):
    return device % 4, device // 4 * 2 + device % 2


def hidden_body(at_s, u_ref, o_ref, b_ref, upper_ref, lower_ref, up_ref, down_ref):
    at = 0
    for ref in (u_ref, o_ref):
        up_ref[at : at + ref.shape[0]] = ref[...].astype(f32)
        at += ref.shape[0]
    up_ref[at:] = jnp.broadcast_to(b_ref[...], (8, b_ref.shape[1]))
    rows = upper_ref.shape[0]
    down_ref[:rows] = upper_ref[...].astype(f32)
    down_ref[rows:] = lower_ref[...].astype(f32)


def hidden_share(at, wu, wo, bu, wd, devices, after):
    width, hidden = wu.shape
    rows, lines, deep = width // devices, wo.shape[0] // devices, hidden // devices
    mine = lambda i, s: (s[0], 0)
    outs = [shape((rows + lines + 8, width), f32), shape((2 * deep, width), f32)]
    return call(
        hidden_body,
        (1,),
        1,
        [
            pl.BlockSpec((rows, hidden), mine),
            pl.BlockSpec((lines, width), mine),
            whole((1, hidden)),
            pl.BlockSpec((deep, width), lambda i, s: (down_rows(s[0])[0], 0)),
            pl.BlockSpec((deep, width), lambda i, s: (4 + down_rows(s[0])[1], 0)),
        ],
        [whole(v.shape) for v in outs],
        outs,
        after=after,
    )(at, wu, wo, bu[None], wd, wd)


def cat(groups, after=()):
    arrays, outs = [], []
    for group in groups:
        arrays += [v for v, _, _ in group]
        outs.append(shape((sum(n for _, _, n in group),) + group[0][0].shape[1:], f32))

    def body(*refs):
        ins, got = refs[: len(arrays)], 0
        for group, out in zip(groups, refs[len(arrays) :]):
            at = 0
            for _, first, n in group:
                out[at : at + n] = ins[got][first : first + n]
                at += n
                got += 1

    return call(body, (1,), 0, [whole(v.shape) for v in arrays], [whole(v.shape) for v in outs], outs, after=after)(*arrays)


def pile(parts, lines=None, after=()):
    lines = lines or parts[0].shape[0]
    rest = parts[0].shape[1:]
    zeros = (0,) * len(rest)

    def body(*refs):
        for i in range(len(parts)):
            refs[-1][i] = refs[i][...]

    return call(
        body,
        (1,),
        0,
        [pl.BlockSpec((lines,) + rest, lambda i: (0,) + zeros)] * len(parts),
        whole((len(parts), lines) + rest),
        shape((len(parts), lines) + rest, f32),
        after=after,
    )(*parts)


def norm_body(spans, doc_s, doc_ref, pad_ref, x_ref, g_ref, b_ref, h_ref, m_ref, p_ref, t_ref):
    row_at = pl.program_id(0)
    width = x_ref.shape[-1]
    xhat, _ = norm_parts(x_ref[...].astype(f32))
    h = (xhat * g_ref[...] + b_ref[...]).astype(bf16)
    h_ref[...] = h
    doc = doc_ref[pl.ds(row_at, 1)]
    alive = pad_ref[pl.ds(row_at, 1)] == 1
    rows, region = m_ref.shape[1:]
    lane = lax.broadcasted_iota(jnp.int32, (rows, region), 1)
    line = lax.broadcasted_iota(jnp.int32, (rows, region), 0)
    tag_line = lax.broadcasted_iota(jnp.int32, (rows, LANES), 0)
    picked = jnp.zeros((rows, region), f32)
    tag = jnp.zeros((rows, LANES), f32)
    for s in range(1, spans + 1):
        last = doc_s[row_at, s * SPAN - 1]
        hit = (line == s) & (lane < s * SPAN) & (doc == last) & alive
        picked = jnp.where(hit, 1.0, picked)
        tag = jnp.where(tag_line == s, last.astype(f32), tag)
    m_ref[0] = picked
    sums = nn(picked.astype(bf16), h)
    count = jnp.broadcast_to(jnp.sum(picked, axis=1, keepdims=True), (rows, LANES))
    p_ref[0, :, :width] = sums
    p_ref[0, :, width : width + LANES] = count
    p_ref[0, :, width + LANES :] = tag
    tiles = width // LANES
    for c in range(tiles):
        t_ref[0, c : c + 1] = sums[spans : spans + 1, c * LANES : (c + 1) * LANES]
    t_ref[0, tiles : tiles + 1] = count[spans : spans + 1]
    t_ref[0, tiles + 1 : tiles + 2] = tag[spans : spans + 1]
    t_ref[0, tiles + 2 :] = jnp.zeros((8 - tiles - 2, LANES), f32)


def first_norm(docs, pads, x, gain, shift, rows, region, after):
    tokens, width = x.shape
    spans = region // SPAN
    lines = -(-(spans + 1) // 8) * 8
    wide = width + 2 * LANES
    tok = pl.BlockSpec((region, width), lambda i, *_: (i, 0))

    def row(n, w):
        return pl.BlockSpec((1, n, w), lambda i, *_: (i, 0, 0))

    def body(*refs):
        norm_body(spans, *refs)

    return call(
        body,
        (rows,),
        1,
        [whole(docs.shape), whole(docs.shape), tok, whole((1, width)), whole((1, width))],
        [tok, row(lines, region), row(lines, wide), row(8, LANES)],
        [
            shape((tokens, width), bf16),
            shape((rows, lines, region), f32),
            shape((rows, lines, wide), f32),
            shape((rows, 8, LANES), f32),
        ],
        after=after,
        us=4,
    )(docs, docs, pads, x, gain[None], shift[None])


def state_of(every_ref, d, row_at, tiles):
    lines = every_ref[d, row_at * 8 : row_at * 8 + 8]
    sums = jnp.concatenate([lines[c : c + 1] for c in range(tiles)], axis=1)
    return sums, lines[tiles : tiles + 1], lines[tiles + 1 : tiles + 2]


def means_body(rows, spans, take, me_s, doc_s, doc_ref, pad_ref, p_ref, mean_ref, misc_ref, every_ref):
    me = me_s[0]
    take(me)
    devices = every_ref.shape[0]
    width = mean_ref.shape[-1]
    tiles = width // LANES
    mean_ref[...] = jnp.zeros_like(mean_ref)
    misc_ref[...] = jnp.zeros_like(misc_ref)
    for row_at in range(rows):
        sums = carry = jnp.zeros((1, width), f32)
        count = carry_count = jnp.zeros((1, LANES), f32)
        tag = tag_in = jnp.full((1, LANES), -1.0, f32)
        for d in range(1, devices):
            new_sums, new_count, new_tag = state_of(every_ref, d - 1, row_at, tiles)
            same = (new_tag == tag).astype(f32)
            sums = new_sums + same[:, :1] * sums
            count = new_count + same * count
            tag = new_tag
            mine = me == d
            carry = jnp.where(mine, sums, carry)
            carry_count = jnp.where(mine, count, carry_count)
            tag_in = jnp.where(mine, tag, tag_in)
        for s in range(spans):
            if s == 0:
                run_doc = tag_in
            else:
                run_doc = jnp.full((1, LANES), doc_s[row_at, s * SPAN - 1].astype(f32))
            flag = (tag_in == run_doc).astype(f32)
            total = p_ref[row_at, s : s + 1, :width] + flag[:, :1] * carry
            count_here = p_ref[row_at, s : s + 1, width : width + LANES] + flag * carry_count
            divisor = jnp.maximum(count_here, 1.0)
            mean_ref[row_at, s : s + 1] = total / divisor[:, :1]
            at = row_at * spans + s
            toks = slice(s * SPAN, (s + 1) * SPAN)
            doc = doc_ref[row_at : row_at + 1, toks].astype(f32)
            misc_ref[at, 0:1] = 1.0 / divisor
            misc_ref[at, 1:2] = flag
            misc_ref[at, 2:3] = run_doc
            misc_ref[at, 3:4] = count_here
            misc_ref[at, 4:5] = doc
            misc_ref[at, 5:6] = jnp.where(pad_ref[row_at : row_at + 1, toks] == 1, doc, -2.0)


def document_means(me, docs, pads, prefix, sent, devices, rows, region):
    spans = region // SPAN
    lines = prefix.shape[1]
    width = prefix.shape[2] - 2 * LANES
    in_order = len(sent) == 1
    tall = rows * 8
    outs = [
        shape((rows, lines, width), f32),
        shape((rows * spans, 8, LANES), f32),
        shape((devices, tall, LANES), f32),
    ]

    def body(me_s, doc_s, doc_ref, pad_ref, p_ref, *refs):
        got, outs = refs[: len(sent)], refs[len(sent) :]

        def take(me):
            if in_order:
                outs[2][...] = got[0][...]
                return
            for core, ref in enumerate(got):
                for j in range(ref.shape[0]):
                    outs[2][me ^ (2 * j + core)] = ref[j]

        means_body(rows, spans, take, me_s, doc_s, doc_ref, pad_ref, p_ref, *outs)

    def tail(v):
        last = v.shape[1] // tall - 1
        return pl.BlockSpec((v.shape[0], tall, LANES), lambda *_: (0, last, 0))

    return call(
        body,
        (1,),
        2,
        [whole(docs.shape), whole(docs.shape), whole(prefix.shape)] + [tail(v) for v in sent],
        [whole(v.shape) for v in outs],
        outs,
    )(me, docs, docs, pads, prefix, *sent)


def take_pieces(at_s, came, w_ref):
    here = at_s[0]
    for core, ref in enumerate(came):
        pieces = ref.shape[0]
        rows = w_ref.shape[0] // (2 * pieces)
        for j in range(pieces):
            at = pl.multiple_of((here ^ (2 * j + core)) * rows, rows)
            for i in range(3):
                w_ref[pl.ds(at, rows), i * LANES : (i + 1) * LANES] = ref[j, i * rows : (i + 1) * rows].astype(bf16)


def pair_body(spans, load, mean_ref, misc_ref, h_ref, w_ref, qkv_ref, p_ref, ps_ref, o_ref, bar_ref, mix_s):
    row_at = pl.program_id(1)

    @pl.when(row_at == 0)
    def _():
        load()
        both = nn(hi_lo(mean_ref[...].reshape(-1, mean_ref.shape[-1])), w_ref[:, LANES:])
        half = both.shape[0] // 2
        bar_ref[0] = (both[:half] + both[half:]).reshape(bar_ref.shape[1:])

    qkv = nn(h_ref[...], w_ref[...])
    qkv_ref[:, :LANES] = (qkv[:, :LANES] * (1.0 / math.sqrt(HEAD_DIM))).astype(bf16)
    qkv_ref[:, LANES:] = qkv[:, LANES:].astype(bf16)
    bars = bar_ref[0, row_at]
    k_lines, v_lines = head_lines(bars[:, :LANES]), head_lines(bars[:, LANES:])
    summaries = nt(k_lines, qkv_ref[:, :LANES]) + math.log(SPAN)
    masks = halves()
    u = lax.broadcasted_iota(jnp.int32, (SPAN, SPAN), 0)
    t = lax.broadcasted_iota(jnp.int32, (SPAN, SPAN), 1)
    all_weights = []
    for s in range(spans):
        toks = slice(s * SPAN, (s + 1) * SPAN)
        q, k, v = (qkv_ref[toks, i * LANES : (i + 1) * LANES] for i in range(3))
        doc, code = misc_ref[s, 4:5], misc_ref[s, 5:6]
        ok = ((u < t) & (jnp.broadcast_to(code, (SPAN, SPAN)).T == doc)) | (u == t)
        present = (doc == misc_ref[s, 2:3]) & (misc_ref[s, 3:4] > 0.0)
        scores = nt(split(k, masks), q)
        probs, weights = [], []
        for half in range(2):
            score = jnp.where(ok, scores[half * SPAN : (half + 1) * SPAN], MASKED)
            far = jnp.where(present, summaries[8 * s + half : 8 * s + half + 1, toks], MASKED)
            top = jnp.maximum(jnp.max(score, axis=0, keepdims=True), far)
            e = jnp.exp(score - top)
            w = jnp.exp(far - top)
            inverse = 1.0 / (jnp.sum(e, axis=0, keepdims=True) + w)
            probs.append((e * inverse).astype(bf16))
            weights.append(w * inverse)
        probs = jnp.concatenate(probs, axis=0)
        weights = eight(weights)
        p_ref[0, s] = probs
        ps_ref[0, s] = weights
        all_weights.append(weights)
        mix_s[toks] = tn(probs, split(v, masks))
    o_ref[...] = (mix_s[...] + tn(diagonal(all_weights, bars.shape[0]), v_lines)).astype(bf16)


def pair_forward(at, means, misc, h, source, first, parts, region, kept):
    tokens, width = h.shape
    rows = tokens // region
    spans = region // SPAN
    pairs = width // LANES
    lines = means.shape[1]
    kind, *weights = source

    def row(n, *rest):
        return pl.BlockSpec((n,) + rest, lambda i, r, s: (r,) + (0,) * len(rest))

    def pair(i, s):
        return i if kind == "all" else s[1] ^ (first + i)

    in_specs = [whole(means.shape), row(spans, 8, LANES), row(region, width)]
    w_spec = pl.BlockSpec((width, 3 * LANES), lambda i, r, s: (0, pair(i, s)))
    if kind == "all":
        in_specs.append(w_spec)
    else:
        pieces = 2 * weights[3].shape[0]
        in_specs += [whole(w.shape) for w in weights[:3]]
        in_specs += [
            pl.BlockSpec(
                (w.shape[0], 3 * width // pieces, LANES), lambda i, r, s: (0, jnp.maximum(first + i - 1, 0), 0)
            )
            for w in weights[3:]
        ]
    out_specs = [
        pl.BlockSpec((region, 3 * LANES), lambda i, r, s: (r, pair(i, s))),
        pl.BlockSpec((1, spans, 2 * SPAN, SPAN), lambda i, r, s: (pair(i, s), r, 0, 0)),
        pl.BlockSpec((1, spans, 8, SPAN), lambda i, r, s: (pair(i, s), r, 0, 0)),
        pl.BlockSpec((region, LANES), lambda i, r, s: (r, pair(i, s))),
        pl.BlockSpec((1, rows, lines, 2 * LANES), lambda i, r, s: (pair(i, s), 0, 0, 0)),
    ]
    out_shape = [
        shape((tokens, 3 * width), bf16),
        shape((pairs, tokens // SPAN, 2 * SPAN, SPAN), bf16),
        shape((pairs, tokens // SPAN, 8, SPAN), f32),
        shape((tokens, width), bf16),
        shape((pairs, rows, lines, 2 * LANES), f32),
    ]
    if kind != "all":
        out_specs.append(w_spec)
        out_shape.append(shape((width, 3 * width), bf16))
    n_in = 3 + len(weights)
    kept = list(kept or ())

    def body(at_s, *refs):
        ins, got, outs, mix_s = refs[:3], refs[3:n_in], refs[n_in + len(kept) : -1], refs[-1]
        if kind == "all":
            w_ref = got[0]
            load = lambda: None
        else:
            w_ref = outs[5]

            def load():
                if first == 0:

                    @pl.when(pl.program_id(0) == 0)
                    def _():
                        for i in range(3):
                            w_ref[:, i * LANES : (i + 1) * LANES] = got[i][...]

                @pl.when(first + pl.program_id(0) > 0)
                def _():
                    take_pieces(at_s, got[3:], w_ref)

        pair_body(spans, load, *ins, w_ref, *outs[:5], mix_s)

    return call(
        body,
        (parts, rows),
        1,
        in_specs + [pl.BlockSpec(memory_space=pl.ANY)] * len(kept),
        out_specs,
        out_shape,
        us=5 * parts,
        aliases={1 + n_in + i: i for i in range(len(kept))},
        scratch=[pltpu.VMEM((region, LANES), f32)],
    )(at, means, misc, h, *weights, *kept)


def take_hidden(at_s, own, came, wu_s, wo_s, wd_s, bu_s):
    here, group = at_s[0], at_s[2]
    others = wu_s.shape[0] - 1
    lines = own[1].shape[0]
    wu_s[group] = own[0][...]
    wo_s[pl.ds(pl.multiple_of(group * lines, lines), lines)] = own[1][...]
    bu_s[group] = jnp.broadcast_to(own[2][...], bu_s.shape[1:])
    wd_s[group] = own[3][...]
    for core, (up, down) in enumerate(came):
        pieces = up.shape[0]
        rows, thin = wu_s.shape[1] // (2 * pieces), lines // (2 * pieces)
        deep = down.shape[1] // others
        for k in range(others):
            to = group ^ (k + 1)
            for j in range(pieces):
                owner = here ^ (2 * j + core)
                first = k * (rows + thin)
                wu_s[to, pl.ds(pl.multiple_of(owner * rows, rows), rows)] = up[j, first : first + rows].astype(bf16)
                at = pl.multiple_of(to * lines + owner * thin, thin)
                wo_s[pl.ds(at, thin)] = up[j, first + rows : first + rows + thin].astype(bf16)
            for j in range(down.shape[0]):
                owner = here ^ core ^ (0, 2, 0, 4)[j]
                place = 4 * (j // 2) + down_rows(owner)[j // 2]
                at = pl.ds(pl.multiple_of(place * deep, deep), deep)
                wd_s[to, at] = down[j, k * deep : (k + 1) * deep].astype(bf16)


def ffn_body(
    at_s, x_ref, g_ref, o_ref, mine_ref, gain_ref, shift_ref, bd_ref, load, wo_ref,
    out_ref, dmid_ref, do_ref, gwu_ref, gwd_ref, gwo_ref, gbu_ref, small_ref, wu_ref, wd_ref, bu_ref, a_s, du_s,
):
    @pl.when(pl.program_id(0) == 0)
    def _():
        load()
        gwu_ref[...] = jnp.zeros_like(gwu_ref)
        gwd_ref[...] = jnp.zeros_like(gwd_ref)
        gwo_ref[...] = jnp.zeros_like(gwo_ref)
        gbu_ref[...] = jnp.zeros_like(gbu_ref)
        small_ref[...] = jnp.zeros_like(small_ref)

    mid = x_ref[...].astype(f32) + nn(o_ref[...], wo_ref[...])
    xhat, rstd = norm_parts(mid)
    h = (xhat * gain_ref[...] + shift_ref[...]).astype(bf16)
    gm = g_ref[...]
    y = dn = None
    for j in range(wu_ref.shape[0]):
        up = nn(h, wu_ref[j]) + bu_ref[j, :1]
        phi, slope = gelu_parts(up)
        a = (up * phi).astype(bf16)
        du = (nt(gm, wd_ref[j]) * slope).astype(bf16)
        a_s[j] = a
        du_s[j] = du
        y_part = nn(a, wd_ref[j])
        dn_part = nt(du, wu_ref[j])
        y = y_part if y is None else y + y_part
        dn = dn_part if dn is None else dn + dn_part
    out_ref[...] = (mid + y + bd_ref[...]).astype(bf16)
    g = gm.astype(f32)
    small_ref[2:3] += jnp.sum(dn * xhat, axis=0, keepdims=True)
    small_ref[3:4] += jnp.sum(dn, axis=0, keepdims=True)
    small_ref[4:5] += jnp.sum(g, axis=0, keepdims=True)
    dmid = g + norm_back(dn * gain_ref[...], xhat, rstd)
    dmid_ref[...] = dmid
    gx = dmid.astype(bf16)
    do_ref[...] = nt(gx, wo_ref[...]).astype(bf16)
    gwo_ref[...] += tn(mine_ref[...], gx)
    group = at_s[2]
    du = du_s[group]
    gwd_ref[...] += tn(a_s[group], gm)
    gwu_ref[...] += tn(h, du)
    gbu = jnp.sum(du.astype(f32), axis=0, keepdims=True)
    gbu_ref[...] += gbu
    if gbu.shape[1] == small_ref.shape[1]:
        small_ref[5:6] += gbu


def feed_forward(at, x, g, o, gain, shift, bd, source):
    tokens, width = x.shape
    kind, *weights = source
    came = kind == "came"
    if came:
        wu, wo, bu, wd, mine, theirs, biases = weights
        hidden, groups = wu.shape[1], 1 + len(biases)
        args = [wu, wo, bu, wd, *mine, *theirs, *biases]
        last = biases[0].shape[0] // 8 - 1
        specs = [whole(w.shape) for w in args[:8]]
        specs += [pl.BlockSpec((8, width), lambda i, *_: (last, 0))] * len(biases)
    else:
        args = weights
        groups, _, hidden = args[0].shape
        specs = [whole(w.shape) for w in args]
    steps = 4
    chunk = tokens // steps
    tok = pl.BlockSpec((chunk, width), lambda i, *_: (i, 0))
    n_w = len(args)
    scratch = [pltpu.VMEM((groups, chunk, hidden), bf16)] * 2
    if came:
        scratch += [
            pltpu.VMEM((groups, width, hidden), bf16),
            pltpu.VMEM((width, width), bf16),
            pltpu.VMEM((groups, 8, hidden), f32),
            pltpu.VMEM((groups, hidden, width), bf16),
        ]

    def body(at_s, *refs):
        ins, got = refs[:7], refs[7 : 7 + n_w]
        outs, acts, held = refs[7 + n_w : 15 + n_w], refs[15 + n_w : 17 + n_w], refs[17 + n_w :]

        def load():
            if came:
                wu_s, wo_s, bu_s, wd_s = held
                take_hidden(at_s, got[:4], (got[4:6], got[6:8]), wu_s, wo_s, wd_s, bu_s)
                for k, ref in enumerate(got[8:]):
                    bu_s[at_s[2] ^ (k + 1)] = ref[...]

        wu_r, wo_r, bu_r, wd_r = held if came else got
        ffn_body(at_s, *ins, load, wo_r, *outs, wu_r, wd_r, bu_r, *acts)

    return call(
        body,
        (steps,),
        1,
        [tok, tok, tok, pl.BlockSpec((chunk, LANES), lambda i, s: (i, s[1])),
         whole((1, width)), whole((1, width)), whole((1, width))] + specs,
        [tok, tok, tok, whole((width, hidden)), whole((hidden, width)), whole((LANES, width)),
         whole((1, hidden)), whole((8, width))],
        [
            shape((tokens, width), bf16),
            shape((tokens, width), f32),
            shape((tokens, width), bf16),
            shape((width, hidden), f32),
            shape((hidden, width), f32),
            shape((LANES, width), f32),
            shape((1, hidden), f32),
            shape((8, width), f32),
        ],
        scratch=scratch,
        us=38,
    )(at, x, g, o, o, gain[None], shift[None], bd[None], *args)


def pair_back_body(spans, qkv_ref, do_ref, p_ref, ps_ref, bar_ref, misc_ref, d_ref, g_ref, d_s):
    row_at = pl.program_id(1)
    masks = halves()
    wide = 2 * LANES
    bars = bar_ref[0, row_at]
    lines = bars.shape[0]
    k_lines, v_lines = head_lines(bars[:, :LANES]), head_lines(bars[:, LANES:])
    dp_far = nt(v_lines, do_ref[...])
    all_far, all_weights = [], []
    for s in range(spans):
        toks = slice(s * SPAN, (s + 1) * SPAN)
        q, k, v = (qkv_ref[toks, i * LANES : (i + 1) * LANES] for i in range(3))
        do = do_ref[toks]
        weight = ps_ref[0, s]
        dp = nt(split(v, masks), do)
        probs, grads, far = [], [], []
        for half in range(2):
            p_half = p_ref[0, s, half * SPAN : (half + 1) * SPAN, :]
            p = p_half.astype(f32)
            dp_half = dp[half * SPAN : (half + 1) * SPAN]
            w, dw = weight[half : half + 1], dp_far[8 * s + half : 8 * s + half + 1, toks]
            r = jnp.sum(p * dp_half, axis=0, keepdims=True) + w * dw
            probs.append(p_half)
            grads.append((p * (dp_half - r)).astype(bf16))
            far.append(w * (dw - r))
        all_far.append(eight(far))
        all_weights.append(weight)
        d_s[toks, :LANES] = tn(jnp.concatenate(grads, axis=0), split(k, masks))
        d_s[toks, LANES:wide] = nn(jnp.concatenate(grads, axis=1), split(q, masks))
        d_s[toks, wide:] = nn(jnp.concatenate(probs, axis=1), split(do, masks))
    far = diagonal(all_far, lines)
    dq = d_s[:, :LANES] + tn(far, k_lines)
    d_ref[:, :LANES] = (dq.astype(bf16).astype(f32) * (1.0 / math.sqrt(HEAD_DIM))).astype(bf16)
    line = lax.broadcasted_iota(jnp.int32, (8 * lines, LANES), 0)
    lane = lax.broadcasted_iota(jnp.int32, (8 * lines, LANES), 1)
    own = lane // HEAD_DIM == line % 8
    gk = jnp.where(own, nn(far, qkv_ref[:, :LANES]), 0.0)
    gv = jnp.where(own, nn(diagonal(all_weights, lines), do_ref[...]), 0.0)
    out = jnp.zeros((1, wide), f32)
    after = None
    for s in reversed(range(spans)):
        toks = slice(s * SPAN, (s + 1) * SPAN)
        dkv = d_s[toks, LANES:]
        gkv = [jnp.sum(v[8 * s : 8 * s + 8], axis=0, keepdims=True) for v in (gk, gv)]
        inverse, flag = misc_ref[s, 0:1, :], misc_ref[s, 1:2, :]
        gkv = jnp.concatenate(gkv, axis=1) * jnp.concatenate([inverse, inverse], axis=1)
        out = out + jnp.concatenate([flag, flag], axis=1) * gkv
        if after is None:
            after = gkv
        else:
            reached = jnp.broadcast_to(misc_ref[s, 5:6], (SPAN, SPAN)).T == misc_ref[s + 1, 2:3]
            dkv = dkv + jnp.where(jnp.concatenate([reached, reached], axis=1), after, 0.0)
            same = (misc_ref[s, 2:3] == misc_ref[s + 1, 2:3]).astype(f32)
            after = gkv + jnp.concatenate([same, same], axis=1) * after
        d_ref[toks, LANES:] = dkv.astype(bf16)
    g_ref[0, :, :LANES] = jnp.zeros((1, LANES), f32)
    g_ref[0, :, LANES:] = out


def pair_backward(at, qkv, do, p, ps, bars, misc, h, region, first, parts, kept):
    tokens, width = do.shape
    rows = tokens // region
    spans = region // SPAN
    lines = bars.shape[2]
    own = h is not None

    def pair(i, s):
        return s[1] ^ (first + i)

    def row(n, *rest):
        return pl.BlockSpec((n,) + rest, lambda i, r, s: (r,) + (0,) * len(rest))

    tok3 = pl.BlockSpec((region, 3 * LANES), lambda i, r, s: (r, pair(i, s)))
    back = pl.BlockSpec((1, 1, 3 * LANES), lambda i, r, s: (r, 0, pair(i, s)))
    in_specs = [
        tok3,
        pl.BlockSpec((region, LANES), lambda i, r, s: (r, pair(i, s))),
        pl.BlockSpec((1, spans, 2 * SPAN, SPAN), lambda i, r, s: (pair(i, s), r, 0, 0)),
        pl.BlockSpec((1, spans, 8, SPAN), lambda i, r, s: (pair(i, s), r, 0, 0)),
        pl.BlockSpec((1, rows, lines, 2 * LANES), lambda i, r, s: (pair(i, s), 0, 0, 0)),
        row(spans, 8, LANES),
    ]
    args = [qkv, do, p, ps, bars, misc]
    out_specs = [tok3, back]
    out_shape = [shape((tokens, 3 * width), bf16), shape((rows, 1, 3 * width), f32)]
    if own:
        in_specs.append(row(region, width))
        args.append(h)
        out_specs.append(whole((width, 3 * LANES)))
        out_shape.append(shape((width, 3 * LANES), f32))
    n_in = len(args)
    kept = list(kept or ())

    def body(at_s, *refs):
        outs = refs[n_in + len(kept) : -1]
        pair_back_body(spans, *refs[:6], outs[0], outs[1], refs[-1])
        if own:
            grads = tn(refs[6][...], outs[0][...])

            @pl.when(pl.program_id(1) == 0)
            def _():
                outs[2][...] = grads

            @pl.when(pl.program_id(1) > 0)
            def _():
                outs[2][...] += grads

    return call(
        body,
        (parts, rows),
        1,
        in_specs + [pl.BlockSpec(memory_space=pl.ANY)] * len(kept),
        out_specs,
        out_shape,
        us=6 * parts,
        aliases={1 + n_in + i: i for i in range(len(kept))},
        scratch=[pltpu.VMEM((region, 3 * LANES), f32)],
    )(at, *args, *kept)


def input_body(
    spans, at_s, every_ref, back_ref, mine_ref, m_ref, x_ref, gain_ref, dmid_ref, d_ref, w_ref, so_far_ref,
    gi_ref, small_ref, late_ref,
):
    row_at = pl.program_id(0)
    me = at_s[0]
    devices = every_ref.shape[0]
    rows = back_ref.shape[1]
    width = x_ref.shape[-1]
    tiles = width // LANES
    wide = w_ref.shape[1]
    lines = m_ref.shape[1]

    @pl.when(row_at == 0)
    def _():
        small_ref[...] = so_far_ref[...]
        heads, tails = [], []
        for r in range(rows):
            run = jnp.zeros((1, mine_ref.shape[-1]), f32)
            tag = None
            for d in reversed(range(devices)):
                sums, _, tag_here = state_of(every_ref, d, r, tiles)
                if tag is not None:
                    run = mine_ref[d + 1, r] + (tag == tag_here).astype(f32)[:, :1] * run
                tag = tag_here
                heads.append(sums)
                tails.append(run)
        late_ref[...] = lax.dot_general(
            jnp.concatenate(heads, axis=0), jnp.concatenate(tails, axis=0), (((0,), (0,)), ((), ())),
            preferred_element_type=f32, precision=lax.Precision.HIGHEST,
        )

    run = jnp.zeros((1, wide), f32)
    mine = run
    tag = None
    for d in reversed(range(devices)):
        tag_here = every_ref[d, pl.ds(row_at * 8, 8)][tiles + 1 : tiles + 2]
        if tag is not None:
            run = back_ref[d + 1, row_at] + (tag == tag_here).astype(f32)[:, :1] * run
            mine = jnp.where(me == d, run, mine)
        tag = tag_here

    through = nt(hi_lo(jnp.broadcast_to(mine, (8, wide))), w_ref[...])
    through = through[0:1] + through[8:9]
    line = lax.broadcasted_iota(jnp.int32, (lines, width), 0)
    through = jnp.where(line == spans, jnp.broadcast_to(through, (lines, width)), 0.0)
    dn = nt(d_ref[...], w_ref[...]) + tn(twice(m_ref[0]), hi_lo(through))
    xhat, rstd = norm_parts(x_ref[...].astype(f32))
    small_ref[0:1] += jnp.sum(dn * xhat, axis=0, keepdims=True)
    small_ref[1:2] += jnp.sum(dn, axis=0, keepdims=True)
    gi_ref[...] = dmid_ref[...] + norm_back(dn * gain_ref[...], xhat, rstd)


def input_grads(at, every, back, m, x, gain, dmid, d, w, small, region):
    tokens, width = x.shape
    rows = tokens // region
    devices = every.shape[0]
    tok = pl.BlockSpec((region, width), lambda i, *_: (i, 0))

    def body(*refs):
        input_body(region // SPAN, *refs)

    return call(
        body,
        (rows,),
        1,
        [
            whole(every.shape), whole(back.shape),
            pl.BlockSpec((devices, rows, 1, 3 * LANES), lambda i, s: (0, 0, 0, s[1])),
            pl.BlockSpec((1,) + m.shape[1:], lambda i, *_: (i, 0, 0)),
            tok, whole((1, width)), tok,
            pl.BlockSpec((region, 3 * width), lambda i, *_: (i, 0)),
            whole(w.shape),
            whole(small.shape),
        ],
        [tok, whole((8, width)), whole((width, 3 * LANES))],
        [shape((tokens, width), f32), shape((8, width), f32), shape((width, 3 * LANES), f32)],
        us=12,
    )(at, every, back, back, m, x, gain[None], dmid, d, w, small)


def pack_body(at_s, gu_ref, gd_ref, go_ref, gw_ref, keep_ref, give_ref):
    core = at_s[0] % 2
    chips = keep_ref.shape[0]
    rows = gu_ref.shape[0] // (2 * chips)
    lines = go_ref.shape[0] // (2 * chips)
    for out, c in ((keep_ref, core), (give_ref, 1 - core)):
        for j in range(chips):
            at = pl.multiple_of((2 * j + c) * rows, rows)
            out[j, :rows] = gu_ref[pl.ds(at, rows)]
            out[j, rows : 2 * rows] = gd_ref[pl.ds(at, rows)]
            out[j, 2 * rows :, : 3 * LANES] = gw_ref[pl.ds(at, rows)]
            at = pl.multiple_of((2 * j + c) * lines, lines)
            go = go_ref[pl.ds(at, lines)]
            for i in range(go.shape[1] // LANES):
                out[j, 2 * rows + i * lines : 2 * rows + (i + 1) * lines, 3 * LANES :] = go[:, i * LANES : (i + 1) * LANES]


def pack(at, gu, gd, go, gw, devices):
    width = gu.shape[1]
    rows = gu.shape[0] // devices
    out = (devices // 2, 3 * rows, width)
    return call(
        pack_body, (1,), 1, [whole(v.shape) for v in (gu, gd, go, gw)], [whole(out), whole(out)], [shape(out, f32)] * 2
    )(at, gu, gd, go, gw)


def fold_body(at_s, keep_ref, got_ref, *outs):
    chip = at_s[0] // 2
    for j, out in enumerate(outs):
        out[...] = keep_ref[chip ^ j] + got_ref[chip ^ j]


def fold(at, keep, got, after):
    chips = keep.shape[0]
    return call(
        fold_body, (1,), 1, [whole(keep.shape)] * 2, [whole(keep.shape[1:])] * chips,
        [shape(keep.shape[1:], f32)] * chips,
        after=after,
    )(at, keep, got)


def add_body(*refs):
    total = refs[0][...]
    for ref in refs[1:-1]:
        total = total + ref[...]
    refs[-1][...] = total


def add_up(parts, after):
    spec = whole(parts[0].shape)
    return call(add_body, (1,), 0, [spec] * len(parts), spec, shape(parts[0].shape, f32), after=after)(*parts)


def unpack_body(at_s, mine_ref, theirs_ref, late_ref, small_ref, gq_ref, gk_ref, gv_ref, go_ref, gu_ref, gd_ref, *tiny):
    here = at_s[0]
    rows = gu_ref.shape[0] // (2 * mine_ref.shape[0])
    lines = go_ref.shape[0] // (2 * mine_ref.shape[0])
    for core, ref in enumerate((mine_ref, theirs_ref)):
        for j in range(ref.shape[0]):
            owner = here ^ (2 * j + core)
            at = pl.ds(pl.multiple_of(owner * rows, rows), rows)
            gu_ref[at] = ref[j, :rows]
            gd_ref[at] = ref[j, rows : 2 * rows]
            for i, out in enumerate((gq_ref, gk_ref, gv_ref)):
                lanes = slice(i * LANES, (i + 1) * LANES)
                out[at] = ref[j, 2 * rows :, lanes] + late_ref[at, lanes]
            at = pl.ds(pl.multiple_of(owner * lines, lines), lines)
            for i in range(go_ref.shape[1] // LANES):
                first = 2 * rows + i * lines
                go_ref[at, i * LANES : (i + 1) * LANES] = ref[j, first : first + lines, 3 * LANES :]
    total = small_ref[0]
    for d in range(1, small_ref.shape[0]):
        total = total + small_ref[d]
    for i, out in enumerate(tiny):
        out[...] = total[i : i + 1]


def unpack(at, mine, theirs, late, small):
    width = mine.shape[2]
    thin = shape((width, LANES), f32)
    outs = [thin, thin, thin, shape((LANES, width), f32), shape((width, width), f32), shape((width, width), f32)]
    outs += [shape((1, width), f32)] * 6
    return call(
        unpack_body, (1,), 1, [whole(v.shape) for v in (mine, theirs, late, small)], [whole(v.shape) for v in outs], outs
    )(at, mine, theirs, late, small)


def narrow_body(w_ref, o_ref):
    o_ref[...] = w_ref[...].astype(bf16)


def gathered(part):
    every = lax.all_gather(part.astype(f32), "head")
    flat = every.reshape(-1, part.shape[1])
    chunk = flat.shape[0] // 8
    block = pl.BlockSpec((chunk, part.shape[1]), lambda i: (i, 0))
    return call(narrow_body, (8,), 0, [block], block, shape(flat.shape, bf16))(flat).reshape(every.shape)


def swap(v, axis, mask):
    return lax.ppermute(v, axis, [(i, i ^ mask) for i in range(lax.axis_size(axis))])


def on_device(
    inputs, doc_ids, pad_mask, ln1_gain, ln1_shift, w_query, w_key, w_value, w_out,
    ln2_gain, ln2_shift, w_up, b_up, w_down, b_down, out_grad,
):
    rows, region, width = inputs.shape
    tokens = rows * region
    devices = lax.axis_size("seq")
    groups = lax.axis_size("head")
    here = lax.axis_index("seq")
    group = lax.axis_index("head")
    share = width // groups
    pairs = width // LANES
    spans = region // SPAN
    own_pair = group * share // LANES
    at = jnp.stack([here, own_pair, group]).astype(jnp.int32)
    x = inputs.reshape(tokens, width)
    g = out_grad.reshape(tokens, width)
    by_share = share == LANES and devices == 8 and groups & (groups - 1) == 0

    if by_share:
        others = range(2, devices, 2)
        ks = range(1, groups)
        a_mine = attention_share(at, w_query, w_key, w_value, devices)
        a_came = [swap(a_mine, "head", k) for k in ks]
        up_mine, down_mine = hidden_share(at, w_up, w_out, b_up, w_down, devices, a_came[:1])
        up_came = [swap(up_mine, "head", k) for k in ks]
        down_came = [swap(down_mine, "head", k) for k in ks]
    h1, m, prefix, tiny = first_norm(
        doc_ids, pad_mask, x, ln1_gain, ln1_shift, rows, region, [up_mine] if by_share else []
    )
    tiny = tiny.reshape(rows * 8, LANES)
    if by_share:
        (a_sent,) = cat([[(v, 0, v.shape[0]) for v in a_came + [tiny]]])
        a_moved = [swap(a_sent, "seq", j) for j in others]
        thick = up_mine.shape[0] - 8
        (up_sent,) = cat([[(v, 0, thick) for v in up_came]])
        up_moved = [swap(up_sent, "seq", j) for j in others]
        mine = pile([a_sent] + a_moved, after=[up_sent])
        a_block = (mine, swap(mine, "seq", 1))
        means, misc, every = document_means(at, doc_ids, pad_mask, prefix, a_block, devices, rows, region)
        source = ("came", w_query, w_key, w_value) + a_block
        kept = pair_forward(at, means, misc, h1, source, 0, pairs // 2, region, None)
        deep = down_mine.shape[0] // 2
        upper, lower = cat([[(v, first, deep) for v in down_came] for first in (0, deep)], after=[kept[3]])
        down_moved = [upper, swap(upper, "seq", 2), lower, swap(lower, "seq", 4)]
        kept = pair_forward(at, means, misc, h1, source, pairs // 2, pairs - pairs // 2, region, kept)
        qkv, p, ps, o, bars, w_in = kept
        up_block = pile([up_sent] + up_moved, after=[upper])
        down_block = pile(down_moved, after=[o])
        ffn_source = (
            "came", w_up, w_out, b_up[None], w_down, (up_block, down_block),
            (swap(up_block, "seq", 1), swap(down_block, "seq", 1)), up_came,
        )
    else:
        every = lax.all_gather(tiny, "seq")
        means, misc, every = document_means(at, doc_ids, pad_mask, prefix, [every], devices, rows, region)
        w_in = gathered(jnp.concatenate([w_query, w_key, w_value], axis=1))
        w_in = w_in.reshape(groups, width, 3, share).transpose(1, 2, 0, 3).reshape(width, 3, pairs, LANES)
        w_in = w_in.transpose(0, 2, 1, 3).reshape(width, 3 * width)
        qkv, p, ps, o, bars = pair_forward(at, means, misc, h1, ("all", w_in), 0, pairs, region, None)
        bu = lax.all_gather(b_up, "head")
        bu = jnp.broadcast_to(bu[:, None], (groups, 8, bu.shape[1]))
        ffn_source = ("all", gathered(w_up), gathered(w_out).reshape(width, width), bu, gathered(w_down))

    out, dmid, do, gwu, gwd, gwo, gbu, small = feed_forward(
        at, x, g, o, ln2_gain, ln2_shift, b_down, ffn_source
    )
    back_args = (at, qkv, do, p, ps, bars, misc)
    d, g_back, gw = pair_backward(*back_args, h1, region, 0, 1, None)
    if by_share:
        keep, give = pack(at, gwu, gwd, gwo, gw, devices)
        got = swap(give, "seq", 1)
        d, g_back = pair_backward(*back_args, None, region, 1, 1, (d, g_back))
        folded = fold(at, keep, got, [g_back])
        arrived = [swap(v, "seq", j) for v, j in zip(folded[1:], others)]
        d, g_back = pair_backward(*back_args, None, region, 2, pairs - 2, (d, g_back))
        total = add_up([folded[0]] + arrived, [g_back])
        spread = [swap(total, "seq", j) for j in others]
    else:
        d, g_back = pair_backward(*back_args, None, region, 1, pairs - 1, (d, g_back))
    back = lax.all_gather(g_back, "seq")
    grad_inputs, small, late = input_grads(at, every, back, m, x, ln1_gain, dmid, d, w_in, small, region)
    out = out.reshape(rows, region, width)
    grad_inputs = grad_inputs.reshape(rows, region, width)
    if by_share:
        mine = pile([total] + spread, after=[small])
        gq, gk, gv, gwo, gwu, gwd, *tiny = unpack(
            at, mine, swap(mine, "seq", 1), late, lax.all_gather(small, "seq")
        )
        g1, s1, g2, s2, gbd, gbu = (v[0] for v in tiny)
        return out, grad_inputs, g1, s1, gq, gk, gv, gwo, g2, s2, gwu, gbu, gwd, gbd

    gwu, gwd, gwo, gbu, small, gw = lax.psum((gwu, gwd, gwo, gbu, small, gw), "seq")
    gw = gw + late
    gq, gk, gv = (gw[:, i * LANES : (i + 1) * LANES] for i in range(3))
    if share != LANES:
        inner = group * share - own_pair * LANES
        gq, gk, gv = (lax.dynamic_slice_in_dim(v, inner, share, 1) for v in (gq, gk, gv))
        gwo = lax.dynamic_slice_in_dim(gwo, inner, share, 0)
    return (
        out, grad_inputs, small[0], small[1], gq, gk, gv, gwo, small[2], small[3], gwu, gbu[0], gwd, small[4]
    )


def solution(mesh):
    tok = P(None, "seq", None)
    ids = P(None, "seq")
    cols, lines = P(None, "head"), P("head", None)
    in_specs = (
        tok, ids, ids, P(), P(), cols, cols, cols, lines, P(), P(), cols, P("head"), lines, P(), tok,
    )
    out_specs = (
        tok, tok, P(), P(), cols, cols, cols, lines, P(), P(), cols, P("head"), lines, P(),
    )
    return jax.shard_map(on_device, mesh=mesh, in_specs=in_specs, out_specs=out_specs, check_vma=False)
```

```python
import math

import jax
import jax.numpy as jnp
from jax import lax
from jax.experimental import pallas as pl
from jax.experimental.pallas import tpu as pltpu
from jax.sharding import PartitionSpec as P

HEAD_DIM = 64
SPAN = 128
LANES = 128
NORM_EPS = 1e-05
MASKED = -1e30
f32, bf16 = jnp.float32, jnp.bfloat16


def nn(a, b):
    return lax.dot_general(a, b, (((1,), (0,)), ((), ())), preferred_element_type=f32)


def nt(a, b):
    return lax.dot_general(a, b, (((1,), (1,)), ((), ())), preferred_element_type=f32)


def tn(a, b):
    return lax.dot_general(a, b, (((0,), (0,)), ((), ())), preferred_element_type=f32)


def hi_lo(v):
    hi = v.astype(bf16).astype(f32)
    return jnp.concatenate([hi, v - hi], axis=0).astype(bf16)


def twice(v):
    return jnp.concatenate([v, v], axis=0).astype(bf16)


def norm_parts(x):
    mean = jnp.mean(x, axis=-1, keepdims=True)
    centred = x - mean
    rstd = lax.rsqrt(jnp.mean(centred * centred, axis=-1, keepdims=True) + NORM_EPS)
    return centred * rstd, rstd


def norm_back(y, xhat, rstd):
    return rstd * (
        y
        - jnp.mean(y, axis=-1, keepdims=True)
        - xhat * jnp.mean(y * xhat, axis=-1, keepdims=True)
    )


def gelu_parts(u):
    z = jnp.abs(u)
    t = 1.0 / (1.0 + (0.3275911 * math.sqrt(0.5)) * z)
    e = jnp.exp(-0.5 * u * u)
    poly = t * (
        0.5 * 0.254829592
        + t
        * (
            0.5 * -0.284496736
            + t * (0.5 * 1.421413741 + t * (0.5 * -1.453152027 + t * (0.5 * 1.061405429)))
        )
    )
    tail = poly * e
    phi = jnp.where(u >= 0.0, 1.0 - tail, tail)
    return phi, phi + u * e * (1.0 / math.sqrt(2.0 * math.pi))


def call(body, grid, prefetch, in_specs, out_specs, out_shape, scratch=(), us=2, mib=6, aliases=None, after=()):
    first, last = prefetch + len(in_specs), prefetch + len(in_specs) + len(after)

    def only(*refs):
        body(*refs[:first], *refs[last:])

    kernel = pl.pallas_call(
        only,
        input_output_aliases=aliases or {},
        grid_spec=pltpu.PrefetchScalarGridSpec(
            num_scalar_prefetch=prefetch,
            grid=grid,
            in_specs=list(in_specs) + [pl.BlockSpec(memory_space=pl.ANY)] * len(after),
            out_specs=out_specs,
            scratch_shapes=list(scratch),
        ),
        out_shape=out_shape,
        compiler_params=pltpu.CompilerParams(vmem_limit_bytes=mib * 2**20),
        cost_estimate=pl.CostEstimate(flops=int(us * 1.1e9), bytes_accessed=int(us * 3.5e6), transcendentals=0),
    )
    return lambda *operands: kernel(*operands, *after)


def whole(shape):
    return pl.BlockSpec(shape, lambda *_: (0,) * len(shape))


def shape(dims, dtype):
    return jax.ShapeDtypeStruct(dims, dtype)


def halves():
    lane = lax.broadcasted_iota(jnp.int32, (1, LANES), 1)
    first = (lane < HEAD_DIM).astype(f32)
    return first.astype(bf16), (1.0 - first).astype(bf16)


def split(v, masks):
    return jnp.concatenate([v * masks[0], v * masks[1]], axis=0)


def head_lines(bars):
    line = lax.broadcasted_iota(jnp.int32, (8, LANES), 0)
    lane = lax.broadcasted_iota(jnp.int32, (8, LANES), 1)
    own = lane // HEAD_DIM == line
    lines = [jnp.where(own, bars[s : s + 1], 0.0) for s in range(bars.shape[0])]
    return jnp.concatenate(lines, axis=0).astype(bf16)


def eight(rows):
    return jnp.concatenate(rows + [jnp.zeros((8 - len(rows), rows[0].shape[1]), f32)], axis=0)


def diagonal(blocks, lines):
    zero = jnp.zeros_like(blocks[0])
    rows = [jnp.concatenate([b if i == j else zero for j in range(len(blocks))], axis=1) for i, b in enumerate(blocks)]
    rows += [jnp.zeros_like(rows[0])] * (lines - len(blocks))
    return jnp.concatenate(rows, axis=0).astype(bf16)


def from_hbm(*arrays):
    return [pltpu.with_memory_space_constraint(v, pltpu.HBM) for v in arrays]


def put_shares(at_s, ins, both_ref, one_ref):
    at = 0
    for ref in ins:
        rows = ref.shape[0] // 2
        both_ref[2 * at : 2 * (at + rows)] = ref[...].astype(f32)
        mine = pl.ds(pl.multiple_of(at_s[0] % 2 * rows, rows), rows)
        one_ref[at : at + rows] = ref[mine].astype(f32)
        at += rows


def shares_body(at_s, *refs):
    put_shares(at_s, refs[:3], *refs[3:])


def attention_share(at, wq, wk, wv, devices):
    width, share = wq.shape
    rows = width // devices
    spec = pl.BlockSpec((2 * rows, share), lambda i, s: (s[0] // 2, 0))
    outs = [shape((6 * rows, share), f32), shape((3 * rows, share), f32)]
    return call(
        shares_body, (1,), 1, [spec] * 3, [whole(v.shape) for v in outs], outs
    )(at, *from_hbm(wq, wk, wv))


def hidden_body(at_s, u_ref, o_ref, b_ref, upper_ref, lower_ref, up_both, up_one, down_both, down_one):
    put_shares(at_s, (u_ref, o_ref), up_both, up_one)
    for ref in (up_both, up_one):
        ref[ref.shape[0] - 8 :] = jnp.broadcast_to(b_ref[...], (8, b_ref.shape[1]))
    put_shares(at_s, (upper_ref, lower_ref), down_both, down_one)


def hidden_share(at, wu, wo, bu, wd, devices, after):
    width, hidden = wu.shape
    rows, lines, deep = width // devices, wo.shape[0] // devices, 2 * hidden // devices
    chip = lambda i, s: (s[0] // 2, 0)
    heights = [2 * (rows + lines) + 8, rows + lines + 8, 2 * deep, deep]
    outs = [shape((n, width), f32) for n in heights]
    return call(
        hidden_body,
        (1,),
        1,
        [
            pl.BlockSpec((2 * rows, hidden), chip),
            pl.BlockSpec((2 * lines, width), chip),
            whole((1, hidden)),
            pl.BlockSpec((deep, width), lambda i, s: (s[0] // 2 % 2, 0)),
            pl.BlockSpec((deep, width), lambda i, s: (2 + s[0] // 4, 0)),
        ],
        [whole(v.shape) for v in outs],
        outs,
        after=after,
    )(at, *from_hbm(wu, wo, bu[None], wd, wd))


def cat(groups, after=()):
    arrays, outs = [], []
    for group in groups:
        arrays += [v for v, _, _ in group]
        outs.append(shape((sum(n for _, _, n in group),) + group[0][0].shape[1:], f32))

    def body(*refs):
        ins, got = refs[: len(arrays)], 0
        for group, out in zip(groups, refs[len(arrays) :]):
            at = 0
            for _, first, n in group:
                out[at : at + n] = ins[got][first : first + n]
                at += n
                got += 1

    return call(body, (1,), 0, [whole(v.shape) for v in arrays], [whole(v.shape) for v in outs], outs, after=after)(*arrays)


def norm_body(spans, doc_s, doc_ref, pad_ref, x_ref, g_ref, b_ref, h_ref, m_ref, p_ref, t_ref):
    row_at = pl.program_id(0)
    width = x_ref.shape[-1]
    xhat, _ = norm_parts(x_ref[...].astype(f32))
    h = (xhat * g_ref[...] + b_ref[...]).astype(bf16)
    h_ref[...] = h
    doc = doc_ref[pl.ds(row_at, 1)]
    alive = pad_ref[pl.ds(row_at, 1)] == 1
    rows, region = m_ref.shape[1:]
    lane = lax.broadcasted_iota(jnp.int32, (rows, region), 1)
    line = lax.broadcasted_iota(jnp.int32, (rows, region), 0)
    tag_line = lax.broadcasted_iota(jnp.int32, (rows, LANES), 0)
    picked = jnp.zeros((rows, region), f32)
    tag = jnp.zeros((rows, LANES), f32)
    for s in range(1, spans + 1):
        last = doc_s[row_at, s * SPAN - 1]
        hit = (line == s) & (lane < s * SPAN) & (doc == last) & alive
        picked = jnp.where(hit, 1.0, picked)
        tag = jnp.where(tag_line == s, last.astype(f32), tag)
    m_ref[0] = picked
    sums = nn(picked.astype(bf16), h)
    count = jnp.broadcast_to(jnp.sum(picked, axis=1, keepdims=True), (rows, LANES))
    p_ref[0, :, :width] = sums
    p_ref[0, :, width : width + LANES] = count
    p_ref[0, :, width + LANES :] = tag
    tiles = width // LANES
    for c in range(tiles):
        t_ref[0, c : c + 1] = sums[spans : spans + 1, c * LANES : (c + 1) * LANES]
    t_ref[0, tiles : tiles + 1] = count[spans : spans + 1]
    t_ref[0, tiles + 1 : tiles + 2] = tag[spans : spans + 1]
    t_ref[0, tiles + 2 :] = jnp.zeros((8 - tiles - 2, LANES), f32)


def first_norm(docs, pads, x, gain, shift, rows, region, after):
    tokens, width = x.shape
    spans = region // SPAN
    lines = -(-(spans + 1) // 8) * 8
    wide = width + 2 * LANES
    tok = pl.BlockSpec((region, width), lambda i, *_: (i, 0))

    def row(n, w):
        return pl.BlockSpec((1, n, w), lambda i, *_: (i, 0, 0))

    def body(*refs):
        norm_body(spans, *refs)

    return call(
        body,
        (rows,),
        1,
        [whole(docs.shape), whole(docs.shape), tok, whole((1, width)), whole((1, width))],
        [tok, row(lines, region), row(lines, wide), row(8, LANES)],
        [
            shape((tokens, width), bf16),
            shape((rows, lines, region), f32),
            shape((rows, lines, wide), f32),
            shape((rows, 8, LANES), f32),
        ],
        after=after,
        us=4,
    )(docs, docs, pads, x, gain[None], shift[None])


def state_of(every_ref, d, row_at, tiles):
    lines = every_ref[d, row_at * 8 : row_at * 8 + 8]
    sums = jnp.concatenate([lines[c : c + 1] for c in range(tiles)], axis=1)
    return sums, lines[tiles : tiles + 1], lines[tiles + 1 : tiles + 2]


def owners(me, refs):
    half = len(refs) // 2
    return [(me ^ (2 * (i % half) + i // half), ref) for i, ref in enumerate(refs)]


def means_body(rows, spans, take, me_s, doc_s, doc_ref, pad_ref, p_ref, mean_ref, misc_ref, every_ref):
    me = me_s[0]
    take(me)
    devices = every_ref.shape[0]
    width = mean_ref.shape[-1]
    tiles = width // LANES
    mean_ref[...] = jnp.zeros_like(mean_ref)
    misc_ref[...] = jnp.zeros_like(misc_ref)
    for row_at in range(rows):
        sums = carry = jnp.zeros((1, width), f32)
        count = carry_count = jnp.zeros((1, LANES), f32)
        tag = tag_in = jnp.full((1, LANES), -1.0, f32)
        for d in range(1, devices):
            new_sums, new_count, new_tag = state_of(every_ref, d - 1, row_at, tiles)
            same = (new_tag == tag).astype(f32)
            sums = new_sums + same[:, :1] * sums
            count = new_count + same * count
            tag = new_tag
            mine = me == d
            carry = jnp.where(mine, sums, carry)
            carry_count = jnp.where(mine, count, carry_count)
            tag_in = jnp.where(mine, tag, tag_in)
        for s in range(spans):
            if s == 0:
                run_doc = tag_in
            else:
                run_doc = jnp.full((1, LANES), doc_s[row_at, s * SPAN - 1].astype(f32))
            flag = (tag_in == run_doc).astype(f32)
            total = p_ref[row_at, s : s + 1, :width] + flag[:, :1] * carry
            count_here = p_ref[row_at, s : s + 1, width : width + LANES] + flag * carry_count
            divisor = jnp.maximum(count_here, 1.0)
            mean_ref[row_at, s : s + 1] = total / divisor[:, :1]
            at = row_at * spans + s
            toks = slice(s * SPAN, (s + 1) * SPAN)
            doc = doc_ref[row_at : row_at + 1, toks].astype(f32)
            misc_ref[at, 0:1] = 1.0 / divisor
            misc_ref[at, 1:2] = flag
            misc_ref[at, 2:3] = run_doc
            misc_ref[at, 3:4] = count_here
            misc_ref[at, 4:5] = doc
            misc_ref[at, 5:6] = jnp.where(pad_ref[row_at : row_at + 1, toks] == 1, doc, -2.0)


def document_means(me, docs, pads, prefix, sent, devices, rows, region):
    spans = region // SPAN
    lines = prefix.shape[1]
    width = prefix.shape[2] - 2 * LANES
    in_order = len(sent) == 1
    tall = rows * 8
    outs = [
        shape((rows, lines, width), f32),
        shape((rows * spans, 8, LANES), f32),
        shape((devices, tall, LANES), f32),
    ]

    def body(me_s, doc_s, doc_ref, pad_ref, p_ref, *refs):
        got, outs = refs[: len(sent)], refs[len(sent) :]

        def take(me):
            if in_order:
                outs[2][...] = got[0][...]
                return
            for owner, ref in owners(me, got):
                outs[2][owner] = ref[...]

        means_body(rows, spans, take, me_s, doc_s, doc_ref, pad_ref, p_ref, *outs)

    def tail(v):
        if in_order:
            return whole(v.shape)
        last = v.shape[0] // tall - 1
        return pl.BlockSpec((tall, LANES), lambda *_: (last, 0))

    return call(
        body,
        (1,),
        2,
        [whole(docs.shape), whole(docs.shape), whole(prefix.shape)] + [tail(v) for v in sent],
        [whole(v.shape) for v in outs],
        outs,
    )(me, docs, docs, pads, prefix, *sent)


def take_pieces(at_s, k, came, w_ref):
    here = at_s[0]
    rows = w_ref.shape[0] // len(came)

    def take(ref, first, owner, n):
        at = pl.ds(pl.multiple_of(owner * n, n), n)
        for i in range(3):
            w_ref[at, i * LANES : (i + 1) * LANES] = ref[first + i * n : first + (i + 1) * n].astype(bf16)

    if k == 3:
        for owner, ref in owners(here, came):
            take(ref, 6 * rows, owner, rows)
        return
    half = len(came) // 2
    for core in range(2):

        @pl.when((here + core) % 2 == k - 1)
        def _():
            for j in range(half):
                take(came[core * half + j], 0, here // 2 ^ j, 2 * rows)


def pair_body(load, mean_ref, misc_ref, h_ref, w_ref, qkv_ref, p_ref, ps_ref, o_ref, bar_ref, mix_s):
    load()
    rows = mean_ref.shape[0]
    region = h_ref.shape[0] // rows
    both = nn(hi_lo(mean_ref[...].reshape(-1, mean_ref.shape[-1])), w_ref[:, LANES:])
    half = both.shape[0] // 2
    bars = both[:half] + both[half:]
    bar_ref[0] = bars.reshape(bar_ref.shape[1:])
    masks = halves()
    u = lax.broadcasted_iota(jnp.int32, (SPAN, SPAN), 0)
    t = lax.broadcasted_iota(jnp.int32, (SPAN, SPAN), 1)
    lines = half // rows
    for row_at in range(rows):
        here = slice(row_at * region, (row_at + 1) * region)
        qkv = nn(h_ref[here], w_ref[...])
        qkv_ref[here, :LANES] = (qkv[:, :LANES] * (1.0 / math.sqrt(HEAD_DIM))).astype(bf16)
        qkv_ref[here, LANES:] = qkv[:, LANES:].astype(bf16)
        bars_here = bars[row_at * lines : (row_at + 1) * lines]
        k_lines, v_lines = head_lines(bars_here[:, :LANES]), head_lines(bars_here[:, LANES:])
        summaries = nt(k_lines, qkv_ref[here, :LANES]) + math.log(SPAN)
        all_weights = []
        for s in range(region // SPAN):
            at = row_at * (region // SPAN) + s
            inside = slice(s * SPAN, (s + 1) * SPAN)
            toks = slice(at * SPAN, (at + 1) * SPAN)
            q, k, v = (qkv_ref[toks, i * LANES : (i + 1) * LANES] for i in range(3))
            doc, code = misc_ref[at, 4:5], misc_ref[at, 5:6]
            ok = ((u < t) & (jnp.broadcast_to(code, (SPAN, SPAN)).T == doc)) | (u == t)
            present = (doc == misc_ref[at, 2:3]) & (misc_ref[at, 3:4] > 0.0)
            scores = nt(split(k, masks), q)
            probs, weights = [], []
            for half_at in range(2):
                score = jnp.where(ok, scores[half_at * SPAN : (half_at + 1) * SPAN], MASKED)
                far = jnp.where(present, summaries[8 * s + half_at : 8 * s + half_at + 1, inside], MASKED)
                top = jnp.maximum(jnp.max(score, axis=0, keepdims=True), far)
                e = jnp.exp(score - top)
                w = jnp.exp(far - top)
                inverse = 1.0 / (jnp.sum(e, axis=0, keepdims=True) + w)
                probs.append((e * inverse).astype(bf16))
                weights.append(w * inverse)
            probs = jnp.concatenate(probs, axis=0)
            weights = eight(weights)
            p_ref[0, at] = probs
            ps_ref[0, at] = weights
            all_weights.append(weights)
            mix_s[toks] = tn(probs, split(v, masks))
        o_ref[here] = (mix_s[here] + tn(diagonal(all_weights, lines), v_lines)).astype(bf16)


def pair_forward(at, means, misc, h, source, first, parts, region, kept):
    tokens, width = h.shape
    rows = tokens // region
    spans = region // SPAN
    pairs = width // LANES
    lines = means.shape[1]
    kind, *weights = source

    def pair(i, s):
        return i if kind == "all" else s[1] ^ (first + i)

    in_specs = [whole(means.shape), whole(misc.shape), whole(h.shape)]
    w_spec = pl.BlockSpec((width, 3 * LANES), lambda i, s: (0, pair(i, s)))
    if kind == "all":
        in_specs.append(w_spec)
    else:
        in_specs += [whole(w.shape) for w in weights]
    out_specs = [
        pl.BlockSpec((tokens, 3 * LANES), lambda i, s: (0, pair(i, s))),
        pl.BlockSpec((1, rows * spans, 2 * SPAN, SPAN), lambda i, s: (pair(i, s), 0, 0, 0)),
        pl.BlockSpec((1, rows * spans, 8, SPAN), lambda i, s: (pair(i, s), 0, 0, 0)),
        pl.BlockSpec((tokens, LANES), lambda i, s: (0, pair(i, s))),
        pl.BlockSpec((1, rows, lines, 2 * LANES), lambda i, s: (pair(i, s), 0, 0, 0)),
    ]
    out_shape = [
        shape((tokens, 3 * width), bf16),
        shape((pairs, tokens // SPAN, 2 * SPAN, SPAN), bf16),
        shape((pairs, tokens // SPAN, 8, SPAN), f32),
        shape((tokens, width), bf16),
        shape((pairs, rows, lines, 2 * LANES), f32),
    ]
    if kind != "all":
        out_specs.append(w_spec)
        out_shape.append(shape((width, 3 * width), bf16))
    n_in = 3 + len(weights)
    kept = list(kept or ())

    def body(at_s, *refs):
        ins, got, outs, mix_s = refs[:3], refs[3:n_in], refs[n_in + len(kept) : -1], refs[-1]
        if kind == "all":
            w_ref = got[0]
            load = lambda: None
        else:
            w_ref = outs[5]

            def load():
                for i in range(parts):

                    @pl.when(pl.program_id(0) == i)
                    def _(i=i):
                        if first + i == 0:
                            for m in range(3):
                                w_ref[:, m * LANES : (m + 1) * LANES] = got[m][...]
                        else:
                            take_pieces(at_s, first + i, got[3:], w_ref)

        pair_body(load, *ins, w_ref, *outs[:5], mix_s)

    return call(
        body,
        (parts,),
        1,
        in_specs + [pl.BlockSpec(memory_space=pl.ANY)] * len(kept),
        out_specs,
        out_shape,
        us=5 * parts,
        mib=12,
        aliases={1 + n_in + i: i for i in range(len(kept))},
        scratch=[pltpu.VMEM((tokens, LANES), f32)],
    )(at, means, misc, h, *weights, *kept)


def take_hidden(at_s, own, ups, downs, wu_s, wo_s, wd_s, bu_s):
    here, group = at_s[0], at_s[2]
    lines = own[1].shape[0]
    wu_s[group] = own[0][...]
    wo_s[pl.ds(pl.multiple_of(group * lines, lines), lines)] = own[1][...]
    bu_s[group] = jnp.broadcast_to(own[2][...], bu_s.shape[1:])
    wd_s[group] = own[3][...]
    rows, thin = wu_s.shape[1] // 8, lines // 8
    thick = 3 * (rows + thin)
    deep = downs[0].shape[0] // 12
    for core in range(2):
        up, down = ups[core], downs[core]
        sender = (here ^ core) % 2
        near = group ^ (1 + sender)
        bu_s[near] = up[4 * thick :]
        for j in range(4):
            owner = here ^ (2 * j + core)
            first = j * thick
            for to, who, n in ((near, owner // 2, 2), (group ^ 3, owner, 1)):
                at = pl.multiple_of(who * n * rows, n * rows)
                wu_s[to, pl.ds(at, n * rows)] = up[first : first + n * rows].astype(bf16)
                first += n * rows
                at = pl.multiple_of(to * lines + who * n * thin, n * thin)
                wo_s[pl.ds(at, n * thin)] = up[first : first + n * thin].astype(bf16)
                first += n * thin
            chip = here ^ (0, 0, 2, 4)[j]
            place = 4 + chip // 4 * 2 if j % 2 else chip // 2 % 2 * 2
            at = pl.multiple_of(place * deep, 2 * deep)
            wd_s[near, pl.ds(at, 2 * deep)] = down[3 * j * deep : (3 * j + 2) * deep].astype(bf16)
            at = pl.multiple_of((place + sender) * deep, deep)
            wd_s[group ^ 3, pl.ds(at, deep)] = down[(3 * j + 2) * deep : (3 * j + 3) * deep].astype(bf16)


def ffn_body(
    at_s, x_ref, g_ref, o_ref, mine_ref, gain_ref, shift_ref, bd_ref, load, wo_ref,
    out_ref, dmid_ref, do_ref, gwo_ref, gbu_ref, small_ref, gwu_ref, gwd_ref, wu_ref, wd_ref, bu_ref, a_s, du_s,
):
    @pl.when(pl.program_id(0) == 0)
    def _():
        load()
        gwu_ref[...] = jnp.zeros_like(gwu_ref)
        gwd_ref[...] = jnp.zeros_like(gwd_ref)
        gwo_ref[...] = jnp.zeros_like(gwo_ref)
        gbu_ref[...] = jnp.zeros_like(gbu_ref)
        small_ref[...] = jnp.zeros_like(small_ref)

    mid = x_ref[...].astype(f32) + nn(o_ref[...], wo_ref[...])
    xhat, rstd = norm_parts(mid)
    h = (xhat * gain_ref[...] + shift_ref[...]).astype(bf16)
    gm = g_ref[...]
    y = dn = None
    n = wu_ref.shape[0]
    for j in range(n):
        up = nn(h, wu_ref[j]) + bu_ref[j, :1]
        da = nt(gm, wd_ref[j])
        if j > 0:
            y_part = nn(a, wd_ref[j - 1])
            dn_part = nt(du, wu_ref[j - 1])
            y = y_part if y is None else y + y_part
            dn = dn_part if dn is None else dn + dn_part
        phi, slope = gelu_parts(up)
        a = (up * phi).astype(bf16)
        du = (da * slope).astype(bf16)
        a_s[j] = a
        du_s[j] = du
    y = y + nn(a, wd_ref[n - 1])
    dn = dn + nt(du, wu_ref[n - 1])
    out_ref[...] = (mid + y + bd_ref[...]).astype(bf16)
    g = gm.astype(f32)
    small_ref[2:3] += jnp.sum(dn * xhat, axis=0, keepdims=True)
    small_ref[3:4] += jnp.sum(dn, axis=0, keepdims=True)
    small_ref[4:5] += jnp.sum(g, axis=0, keepdims=True)
    dmid = g + norm_back(dn * gain_ref[...], xhat, rstd)
    dmid_ref[...] = dmid
    gx = dmid.astype(bf16)
    do_ref[...] = nt(gx, wo_ref[...]).astype(bf16)
    gwo_ref[...] += tn(mine_ref[...], gx)
    group = at_s[2]
    du = du_s[group]
    gwd_ref[...] += tn(a_s[group], gm)
    gwu_ref[...] += tn(h, du)
    gbu = jnp.sum(du.astype(f32), axis=0, keepdims=True)
    gbu_ref[...] += gbu
    if gbu.shape[1] == small_ref.shape[1]:
        small_ref[5:6] += gbu


def by_core(core, keep_ref, give_ref):
    return (keep_ref, core), (give_ref, 1 - core)


def feed_forward(at, x, g, o, gain, shift, bd, source, devices):
    tokens, width = x.shape
    kind, *weights = source
    came = kind == "came"
    if came:
        *own, ups, downs, bias = weights
        hidden, groups = own[0].shape[1], 4
        args = [*own, *ups, *downs, bias]
        n_up, n_down = 4 + len(ups), 4 + len(ups) + len(downs)
        last = bias.shape[0] // 8 - 1
        specs = [whole(w.shape) for w in args[:n_down]] + [pl.BlockSpec((8, width), lambda i, *_: (last, 0))]
    else:
        args = weights
        groups, _, hidden = args[0].shape
        specs = [whole(w.shape) for w in args]
    steps = 4
    chunk = tokens // steps
    tok = pl.BlockSpec((chunk, width), lambda i, *_: (i, 0))
    n_w = len(args)
    scratch = [pltpu.VMEM((groups, chunk, hidden), bf16)] * 2
    grads = [shape((width, hidden), f32), shape((hidden, width), f32)]
    if came:
        scratch += [pltpu.VMEM(v.shape, f32) for v in grads]
        scratch += [
            pltpu.VMEM((groups, width, hidden), bf16),
            pltpu.VMEM((width, width), bf16),
            pltpu.VMEM((groups, 8, hidden), f32),
            pltpu.VMEM((groups, hidden, width), bf16),
        ]
        grads = [shape((devices // 2, (width + hidden) // devices, width), f32)] * 2

    def body(at_s, *refs):
        ins, got = refs[:7], refs[7 : 7 + n_w]
        outs, acts, held = refs[7 + n_w : 15 + n_w], refs[15 + n_w : 17 + n_w], refs[17 + n_w :]
        if not came:
            wu_r, wo_r, bu_r, wd_r = got
            ffn_body(at_s, *ins, lambda: None, wo_r, *outs, wu_r, wd_r, bu_r, *acts)
            return
        gwu_s, gwd_s, wu_s, wo_s, bu_s, wd_s = held

        def load():
            take_hidden(at_s, got[:4], got[4:n_up], got[n_up:n_down], wu_s, wo_s, wd_s, bu_s)
            bu_s[at_s[2] ^ 3] = got[n_down][...]

        ffn_body(at_s, *ins, load, wo_s, *outs[:6], gwu_s, gwd_s, wu_s, wd_s, bu_s, *acts)

        @pl.when(pl.program_id(0) == steps - 1)
        def _():
            rows = width // devices
            for out, c in by_core(at_s[0] % 2, *outs[6:]):
                for j in range(devices // 2):
                    lines = pl.ds(pl.multiple_of((2 * j + c) * rows, rows), rows)
                    out[j, :rows] = gwu_s[lines]
                    out[j, rows:] = gwd_s[lines]

    return call(
        body,
        (steps,),
        1,
        [tok, tok, tok, pl.BlockSpec((chunk, LANES), lambda i, s: (i, s[1])),
         whole((1, width)), whole((1, width)), whole((1, width))] + specs,
        [tok, tok, tok, whole((LANES, width)), whole((1, hidden)), whole((8, width))] + [whole(v.shape) for v in grads],
        [
            shape((tokens, width), bf16),
            shape((tokens, width), f32),
            shape((tokens, width), bf16),
            shape((LANES, width), f32),
            shape((1, hidden), f32),
            shape((8, width), f32),
        ] + grads,
        scratch=scratch,
        us=38,
        mib=26,
    )(at, x, g, o, o, gain[None], shift[None], bd[None], *args)


def pair_back_body(rows, qkv_ref, do_ref, p_ref, ps_ref, bar_ref, misc_ref, d_ref, g_ref, d_s):
    masks = halves()
    wide = 2 * LANES
    region = do_ref.shape[0] // rows
    spans = region // SPAN
    for row_at in range(rows):
        here = slice(row_at * region, (row_at + 1) * region)
        bars = bar_ref[0, row_at]
        lines = bars.shape[0]
        k_lines, v_lines = head_lines(bars[:, :LANES]), head_lines(bars[:, LANES:])
        dp_far = nt(v_lines, do_ref[here])
        all_far, all_weights = [], []
        for s in range(spans):
            at = row_at * spans + s
            inside = slice(s * SPAN, (s + 1) * SPAN)
            toks = slice(at * SPAN, (at + 1) * SPAN)
            q, k, v = (qkv_ref[toks, i * LANES : (i + 1) * LANES] for i in range(3))
            do = do_ref[toks]
            weight = ps_ref[0, at]
            dp = nt(split(v, masks), do)
            probs, grads, far = [], [], []
            for half in range(2):
                p_half = p_ref[0, at, half * SPAN : (half + 1) * SPAN, :]
                p = p_half.astype(f32)
                dp_half = dp[half * SPAN : (half + 1) * SPAN]
                w, dw = weight[half : half + 1], dp_far[8 * s + half : 8 * s + half + 1, inside]
                r = jnp.sum(p * dp_half, axis=0, keepdims=True) + w * dw
                probs.append(p_half)
                grads.append((p * (dp_half - r)).astype(bf16))
                far.append(w * (dw - r))
            all_far.append(eight(far))
            all_weights.append(weight)
            d_s[toks, :LANES] = tn(jnp.concatenate(grads, axis=0), split(k, masks))
            d_s[toks, LANES:wide] = nn(jnp.concatenate(grads, axis=1), split(q, masks))
            d_s[toks, wide:] = nn(jnp.concatenate(probs, axis=1), split(do, masks))
        far = diagonal(all_far, lines)
        dq = d_s[here, :LANES] + tn(far, k_lines)
        d_ref[here, :LANES] = (dq.astype(bf16).astype(f32) * (1.0 / math.sqrt(HEAD_DIM))).astype(bf16)
        line = lax.broadcasted_iota(jnp.int32, (8 * lines, LANES), 0)
        lane = lax.broadcasted_iota(jnp.int32, (8 * lines, LANES), 1)
        own = lane // HEAD_DIM == line % 8
        gk = jnp.where(own, nn(far, qkv_ref[here, :LANES]), 0.0)
        gv = jnp.where(own, nn(diagonal(all_weights, lines), do_ref[here]), 0.0)
        out = jnp.zeros((1, wide), f32)
        after = None
        for s in reversed(range(spans)):
            at = row_at * spans + s
            toks = slice(at * SPAN, (at + 1) * SPAN)
            dkv = d_s[toks, LANES:]
            gkv = [jnp.sum(v[8 * s : 8 * s + 8], axis=0, keepdims=True) for v in (gk, gv)]
            inverse, flag = misc_ref[at, 0:1, :], misc_ref[at, 1:2, :]
            gkv = jnp.concatenate(gkv, axis=1) * jnp.concatenate([inverse, inverse], axis=1)
            out = out + jnp.concatenate([flag, flag], axis=1) * gkv
            if after is None:
                after = gkv
            else:
                reached = jnp.broadcast_to(misc_ref[at, 5:6], (SPAN, SPAN)).T == misc_ref[at + 1, 2:3]
                dkv = dkv + jnp.where(jnp.concatenate([reached, reached], axis=1), after, 0.0)
                same = (misc_ref[at, 2:3] == misc_ref[at + 1, 2:3]).astype(f32)
                after = gkv + jnp.concatenate([same, same], axis=1) * after
            d_ref[toks, LANES:] = dkv.astype(bf16)
        g_ref[row_at, :, :LANES] = jnp.zeros((1, LANES), f32)
        g_ref[row_at, :, LANES:] = out


def pair_backward(at, qkv, do, p, ps, bars, misc, h, gwo, devices, region, first, parts, kept):
    tokens, width = do.shape
    rows = tokens // region
    spans = region // SPAN
    lines = bars.shape[2]
    own = h is not None

    def pair(i, s):
        return s[1] ^ (first + i)

    tok3 = pl.BlockSpec((tokens, 3 * LANES), lambda i, s: (0, pair(i, s)))
    back = pl.BlockSpec((rows, 1, 3 * LANES), lambda i, s: (0, 0, pair(i, s)))
    in_specs = [
        tok3,
        pl.BlockSpec((tokens, LANES), lambda i, s: (0, pair(i, s))),
        pl.BlockSpec((1, rows * spans, 2 * SPAN, SPAN), lambda i, s: (pair(i, s), 0, 0, 0)),
        pl.BlockSpec((1, rows * spans, 8, SPAN), lambda i, s: (pair(i, s), 0, 0, 0)),
        pl.BlockSpec((1, rows, lines, 2 * LANES), lambda i, s: (pair(i, s), 0, 0, 0)),
        whole(misc.shape),
    ]
    args = [qkv, do, p, ps, bars, misc]
    out_specs = [tok3, back]
    out_shape = [shape((tokens, 3 * width), bf16), shape((rows, 1, 3 * width), f32)]
    if own:
        in_specs.append(whole(h.shape))
        args.append(h)
        grads = [shape((width, 3 * LANES), f32)]
        if gwo is not None:
            in_specs.append(whole(gwo.shape))
            args.append(gwo)
            grads = [shape((devices // 2, width // devices, width), f32)] * 2
        out_specs += [whole(v.shape) for v in grads]
        out_shape += grads
    n_in = len(args)
    kept = list(kept or ())

    def body(at_s, *refs):
        outs = refs[n_in + len(kept) : n_in + len(kept) + len(out_shape)]
        held = refs[n_in + len(kept) + len(out_shape) :]
        pair_back_body(rows, *refs[:6], outs[0], outs[1], held[0])
        if own:
            grads = tn(refs[6][...], outs[0][...])
            if gwo is None:
                outs[2][...] = grads
            else:
                held[1][...] = grads
                lines_q, lines_o = width // devices, LANES // devices
                for out, c in by_core(at_s[0] % 2, *outs[2:]):
                    for j in range(devices // 2):
                        owner = 2 * j + c
                        out[j, :, : 3 * LANES] = held[1][pl.ds(pl.multiple_of(owner * lines_q, lines_q), lines_q)]
                        go = refs[7][pl.ds(pl.multiple_of(owner * lines_o, lines_o), lines_o)]
                        for i in range(width // LANES):
                            out[j, i * lines_o : (i + 1) * lines_o, 3 * LANES :] = go[:, i * LANES : (i + 1) * LANES]

    return call(
        body,
        (parts,),
        1,
        in_specs + [pl.BlockSpec(memory_space=pl.ANY)] * len(kept),
        out_specs,
        out_shape,
        us=6 * parts,
        mib=12,
        aliases={1 + n_in + i: i for i in range(len(kept))},
        scratch=[pltpu.VMEM((tokens, 3 * LANES), f32), pltpu.VMEM((width, 3 * LANES), f32)],
    )(at, *args, *kept)


def input_body(
    rows, at_s, every_ref, backs, misc_ref, x_ref, gain_ref, dmid_ref, d_ref, w_ref, so_far_ref,
    gi_ref, small_ref, late_ref, through_s, tag_s, back_s,
):
    me = at_s[0]
    devices = every_ref.shape[0]
    width = x_ref.shape[-1]
    tiles = width // LANES
    wide = w_ref.shape[1]

    @pl.when(pl.program_id(0) == 0)
    def _():
        small_ref[...] = so_far_ref[...]
        if len(backs) == 1:
            for d in range(devices):
                back_s[d] = backs[0][d * rows : (d + 1) * rows]
        else:
            for core, ref in enumerate(backs):
                for j in range(devices // 2):
                    back_s[me ^ (2 * j + core)] = ref[j * rows : (j + 1) * rows]
        mine_lanes = pl.ds(pl.multiple_of(at_s[1] * 3 * LANES, LANES), 3 * LANES)
        heads, tails = [], []
        for r in range(rows):
            run = mine = jnp.zeros((1, wide), f32)
            own_run = jnp.zeros((1, 3 * LANES), f32)
            tag = None
            for d in reversed(range(devices)):
                sums, _, tag_here = state_of(every_ref, d, r, tiles)
                if tag is not None:
                    same = (tag == tag_here).astype(f32)[:, :1]
                    run = back_s[d + 1, r : r + 1] + same * run
                    own_run = back_s[d + 1, r : r + 1, mine_lanes] + same * own_run
                    mine = jnp.where(me == d, run, mine)
                tag = tag_here
                tag_s[r : r + 1] = jnp.where(me == d, tag, tag_s[r : r + 1])
                heads.append(sums)
                tails.append(own_run)
            through = nt(hi_lo(jnp.broadcast_to(mine, (8, wide))), w_ref[...])
            through_s[r : r + 1] = through[0:1] + through[8:9]
        late_ref[...] = lax.dot_general(
            jnp.concatenate(heads, axis=0), jnp.concatenate(tails, axis=0), (((0,), (0,)), ((), ())),
            preferred_element_type=f32, precision=lax.Precision.HIGHEST,
        )

    dn = nt(d_ref[...], w_ref[...])
    spans = misc_ref.shape[0]
    added = []
    for i in range(spans):
        at = pl.program_id(0) * spans + i
        row_at = at // (pl.num_programs(0) * spans // rows)
        reached = jnp.broadcast_to(misc_ref[i, 5:6], (SPAN, SPAN)).T == tag_s[pl.ds(row_at, 1)]
        added.append(jnp.where(jnp.concatenate([reached] * tiles, axis=1), through_s[pl.ds(row_at, 1)], 0.0))
    dn = dn + jnp.concatenate(added, axis=0)
    xhat, rstd = norm_parts(x_ref[...].astype(f32))
    small_ref[0:1] += jnp.sum(dn * xhat, axis=0, keepdims=True)
    small_ref[1:2] += jnp.sum(dn, axis=0, keepdims=True)
    gi_ref[...] = dmid_ref[...] + norm_back(dn * gain_ref[...], xhat, rstd)


def input_grads(at, every, back, misc, x, gain, dmid, d, w, small, rows):
    tokens, width = x.shape
    devices = every.shape[0]
    steps = 7 if tokens // SPAN % 7 == 0 else tokens // SPAN
    chunk = tokens // steps
    tok = pl.BlockSpec((chunk, width), lambda i, *_: (i, 0))

    def body(at_s, every_ref, *refs):
        input_body(rows, at_s, every_ref, refs[: len(back)], *refs[len(back) :])

    return call(
        body,
        (steps,),
        1,
        [
            whole(every.shape),
            *[whole(v.shape) for v in back],
            pl.BlockSpec((chunk // SPAN,) + misc.shape[1:], lambda i, *_: (i, 0, 0)),
            tok, whole((1, width)), tok,
            pl.BlockSpec((chunk, 3 * width), lambda i, *_: (i, 0)),
            whole(w.shape),
            whole(small.shape),
        ],
        [tok, whole((8, width)), whole((width, 3 * LANES))],
        [shape((tokens, width), f32), shape((8, width), f32), shape((width, 3 * LANES), f32)],
        scratch=[
            pltpu.VMEM((rows, width), f32), pltpu.VMEM((rows, LANES), f32), pltpu.VMEM((devices, rows, 3 * width), f32)
        ],
        us=10,
        mib=10,
    )(at, every, *back, misc, x, gain[None], dmid, d, w, small)


def fold_body(count, at_s, *refs):
    chip = at_s[0] // 2
    outs = refs[2 * count :]
    at = 0
    for keep, got in zip(refs[:count], refs[count : 2 * count]):
        rows = keep.shape[1]
        for j, out in enumerate(outs):
            out[at : at + rows] = keep[chip ^ j] + got[chip ^ j]
        at += rows


def fold(at, keeps, gots):
    chips, _, width = keeps[0].shape
    outs = [shape((sum(v.shape[1] for v in keeps), width), f32)] * chips

    def body(*refs):
        fold_body(len(keeps), *refs)

    args = [*keeps, *gots]
    return call(body, (1,), 1, [whole(v.shape) for v in args], [whole(v.shape) for v in outs], outs)(at, *args)


def add_body(*refs):
    total = refs[0][...]
    for ref in refs[1:-1]:
        total = total + ref[...]
    refs[-1][...] = total


def add_up(parts, after):
    spec = whole(parts[0].shape)
    return call(add_body, (1,), 0, [spec] * len(parts), spec, shape(parts[0].shape, f32), after=after)(*parts)


def unpack_body(at_s, *refs):
    *pieces, late_ref, gq_ref, gk_ref, gv_ref, go_ref, gu_ref, gd_ref = refs
    rows = gu_ref.shape[0] // len(pieces)
    lines = go_ref.shape[0] // len(pieces)
    for owner, ref in owners(at_s[0], pieces):
        at = pl.ds(pl.multiple_of(owner * rows, rows), rows)
        gu_ref[at] = ref[:rows]
        gd_ref[at] = ref[rows : 2 * rows]
        for i, out in enumerate((gq_ref, gk_ref, gv_ref)):
            lanes = slice(i * LANES, (i + 1) * LANES)
            out[at] = ref[2 * rows :, lanes] + late_ref[at, lanes]
        at = pl.ds(pl.multiple_of(owner * lines, lines), lines)
        for i in range(go_ref.shape[1] // LANES):
            first = 2 * rows + i * lines
            go_ref[at, i * LANES : (i + 1) * LANES] = ref[first : first + lines, 3 * LANES :]


def unpack(at, pieces, late):
    width = pieces[0].shape[1]
    thin = shape((width, LANES), f32)
    outs = [thin, thin, thin, shape((LANES, width), f32), shape((width, width), f32), shape((width, width), f32)]
    args = [*pieces, late]
    return call(
        unpack_body, (1,), 1, [whole(v.shape) for v in args], [whole(v.shape) for v in outs], outs
    )(at, *args)


def totals_body(small_ref, *outs):
    total = small_ref[0]
    for d in range(1, small_ref.shape[0]):
        total = total + small_ref[d]
    for i, out in enumerate(outs):
        out[...] = total[i : i + 1]


def totals(small):
    outs = [shape((1, small.shape[2]), f32)] * 6
    return call(totals_body, (1,), 0, [whole(small.shape)], [whole(v.shape) for v in outs], outs)(small)


def narrow_body(w_ref, o_ref):
    o_ref[...] = w_ref[...].astype(bf16)


def gathered(part):
    every = lax.all_gather(part.astype(f32), "head")
    flat = every.reshape(-1, part.shape[1])
    chunk = flat.shape[0] // 8
    block = pl.BlockSpec((chunk, part.shape[1]), lambda i: (i, 0))
    return call(narrow_body, (8,), 0, [block], block, shape(flat.shape, bf16))(flat).reshape(every.shape)


def swap(v, axis, mask):
    return lax.ppermute(v, axis, [(i, i ^ mask) for i in range(lax.axis_size(axis))])


def along_z(both, one):
    groups, devices = lax.axis_size("head"), lax.axis_size("seq")
    by_core = [(d * groups + h, d * groups + (h ^ (1 + d % 2))) for d in range(devices) for h in range(groups)]
    return lax.ppermute(both, ("seq", "head"), by_core), swap(one, "head", 3)


def both_cores(pieces, after):
    first, *rest = pieces
    theirs = [swap(first, "seq", 1)]
    held = lax.optimization_barrier((after, *rest))
    return pieces + theirs + [swap(v, "seq", 1) for v in held[1:]]


def on_device(
    inputs, doc_ids, pad_mask, ln1_gain, ln1_shift, w_query, w_key, w_value, w_out,
    ln2_gain, ln2_shift, w_up, b_up, w_down, b_down, out_grad,
):
    rows, region, width = inputs.shape
    tokens = rows * region
    devices = lax.axis_size("seq")
    groups = lax.axis_size("head")
    here = lax.axis_index("seq")
    group = lax.axis_index("head")
    share = width // groups
    pairs = width // LANES
    spans = region // SPAN
    own_pair = group * share // LANES
    at = jnp.stack([here, own_pair, group]).astype(jnp.int32)
    x = inputs.reshape(tokens, width)
    g = out_grad.reshape(tokens, width)
    by_share = share == LANES and devices == 8 and groups == 4

    if by_share:
        others = range(2, devices, 2)
        a_both, a_one = along_z(*attention_share(at, w_query, w_key, w_value, devices))
    h1, m, prefix, tiny = first_norm(
        doc_ids, pad_mask, x, ln1_gain, ln1_shift, rows, region, []
    )
    tiny = tiny.reshape(rows * 8, LANES)
    if by_share:
        (a_sent,) = cat([[(v, 0, v.shape[0]) for v in (a_both, a_one, tiny)]])
        a_moved = [swap(a_sent, "seq", j) for j in others]
        up_both, up_one, down_both, down_one = hidden_share(at, w_up, w_out, b_up, w_down, devices, [h1])
        up_both, up_one = along_z(up_both, up_one)
        down_both, down_one = along_z(down_both, down_one)
        (up_sent,) = cat([[(v, 0, v.shape[0] - 8) for v in (up_both, up_one)]])
        a_pieces = both_cores([a_sent] + a_moved, up_sent)
        up_moved = [swap(up_sent, "seq", j) for j in others]
        means, misc, every = document_means(at, doc_ids, pad_mask, prefix, a_pieces, devices, rows, region)
        source = ("came", w_query, w_key, w_value, *a_pieces)
        qkv, p, ps, o, bars, w_in = pair_forward(at, means, misc, h1, source, 0, pairs, region, None)
        deep = down_one.shape[0] // 2
        upper, lower = cat([[(down_both, 2 * i * deep, 2 * deep), (down_one, i * deep, deep)] for i in range(2)], after=[o])
        down_moved = [upper, lower, swap(upper, "seq", 2), swap(lower, "seq", 4)]
        (up_half,) = cat(
            [[(v, 0, v.shape[0]) for v in [up_sent] + up_moved] + [(up_both, up_both.shape[0] - 8, 8)]], after=[upper]
        )
        (down_half,) = cat([[(v, 0, v.shape[0]) for v in down_moved]], after=[up_half])
        up_pieces = [up_half, swap(up_half, "seq", 1)]
        down_pieces = [down_half, swap(down_half, "seq", 1)]
        ffn_source = ("came", w_up, w_out, b_up[None], w_down, up_pieces, down_pieces, up_one)
    else:
        every = lax.all_gather(tiny, "seq")
        means, misc, every = document_means(at, doc_ids, pad_mask, prefix, [every], devices, rows, region)
        w_in = gathered(jnp.concatenate([w_query, w_key, w_value], axis=1))
        w_in = w_in.reshape(groups, width, 3, share).transpose(1, 2, 0, 3).reshape(width, 3, pairs, LANES)
        w_in = w_in.transpose(0, 2, 1, 3).reshape(width, 3 * width)
        qkv, p, ps, o, bars = pair_forward(at, means, misc, h1, ("all", w_in), 0, pairs, region, None)
        bu = lax.all_gather(b_up, "head")
        bu = jnp.broadcast_to(bu[:, None], (groups, 8, bu.shape[1]))
        ffn_source = ("all", gathered(w_up), gathered(w_out).reshape(width, width), bu, gathered(w_down))

    out, dmid, do, gwo, gbu, small, *hidden_grads = feed_forward(
        at, x, g, o, ln2_gain, ln2_shift, b_down, ffn_source, devices
    )
    back_args = (at, qkv, do, p, ps, bars, misc)
    d, g_back, *pair_grads = pair_backward(
        *back_args, h1, gwo if by_share else None, devices, region, 0, 1, None
    )
    if by_share:
        keeps, gives = zip(hidden_grads, pair_grads)
        folded = fold(at, keeps, [swap(v, "seq", 1) for v in gives])
        arrived = [swap(v, "seq", j) for v, j in zip(folded[1:], others)]
    d, g_back = pair_backward(*back_args, None, None, devices, region, 1, pairs - 1, (d, g_back))
    if by_share:
        g_back = g_back.reshape(rows, 3 * width)
        (back,) = cat([[(v, 0, rows) for v in [g_back] + [swap(g_back, "seq", j) for j in others]]])
        total = add_up([folded[0]] + arrived, [back])
        spread = [swap(total, "seq", j) for j in others]
        back = [back, swap(back, "seq", 1)]
    else:
        back = [lax.all_gather(g_back, "seq").reshape(devices * rows, 3 * width)]
    grad_inputs, small, late = input_grads(at, every, back, misc, x, ln1_gain, dmid, d, w_in, small, rows)
    out = out.reshape(rows, region, width)
    grad_inputs = grad_inputs.reshape(rows, region, width)
    if by_share:
        pieces = both_cores([total] + spread, small)
        gq, gk, gv, gwo, gwu, gwd = unpack(at, pieces, late)
        g1, s1, g2, s2, gbd, gbu = (v[0] for v in totals(lax.all_gather(small, "seq")))
        return out, grad_inputs, g1, s1, gq, gk, gv, gwo, g2, s2, gwu, gbu, gwd, gbd

    gwu, gwd = hidden_grads
    (gw,) = pair_grads
    gwu, gwd, gwo, gbu, small, gw = lax.psum((gwu, gwd, gwo, gbu, small, gw), "seq")
    gw = gw + late
    gq, gk, gv = (gw[:, i * LANES : (i + 1) * LANES] for i in range(3))
    if share != LANES:
        inner = group * share - own_pair * LANES
        gq, gk, gv = (lax.dynamic_slice_in_dim(v, inner, share, 1) for v in (gq, gk, gv))
        gwo = lax.dynamic_slice_in_dim(gwo, inner, share, 0)
    return (
        out, grad_inputs, small[0], small[1], gq, gk, gv, gwo, small[2], small[3], gwu, gbu[0], gwd, small[4]
    )


def solution(mesh):
    tok = P(None, "seq", None)
    ids = P(None, "seq")
    cols, lines = P(None, "head"), P("head", None)
    in_specs = (
        tok, ids, ids, P(), P(), cols, cols, cols, lines, P(), P(), cols, P("head"), lines, P(), tok,
    )
    out_specs = (
        tok, tok, P(), P(), cols, cols, cols, lines, P(), P(), cols, P("head"), lines, P(),
    )
    return jax.shard_map(on_device, mesh=mesh, in_specs=in_specs, out_specs=out_specs, check_vma=False)
```

```python
import math

import jax
import jax.numpy as jnp
from jax import lax
from jax.experimental import pallas as pl
from jax.experimental.pallas import tpu as pltpu
from jax.sharding import PartitionSpec as P

HEAD_DIM = 64
SPAN = 128
LANES = 128
NORM_EPS = 1e-05
MASKED = -1e30
f32, bf16 = jnp.float32, jnp.bfloat16


def nn(a, b):
    return lax.dot_general(a, b, (((1,), (0,)), ((), ())), preferred_element_type=f32)


def nt(a, b):
    return lax.dot_general(a, b, (((1,), (1,)), ((), ())), preferred_element_type=f32)


def tn(a, b):
    return lax.dot_general(a, b, (((0,), (0,)), ((), ())), preferred_element_type=f32)


def hi_lo(v):
    hi = v.astype(bf16).astype(f32)
    return jnp.concatenate([hi, v - hi], axis=0).astype(bf16)


def twice(v):
    return jnp.concatenate([v, v], axis=0).astype(bf16)


def norm_parts(x):
    mean = jnp.mean(x, axis=-1, keepdims=True)
    centred = x - mean
    rstd = lax.rsqrt(jnp.mean(centred * centred, axis=-1, keepdims=True) + NORM_EPS)
    return centred * rstd, rstd


def norm_back(y, xhat, rstd):
    return rstd * (
        y
        - jnp.mean(y, axis=-1, keepdims=True)
        - xhat * jnp.mean(y * xhat, axis=-1, keepdims=True)
    )


def gelu_parts(u):
    z = jnp.abs(u)
    t = 1.0 / (1.0 + (0.3275911 * math.sqrt(0.5)) * z)
    e = jnp.exp(-0.5 * u * u)
    poly = t * (
        0.5 * 0.254829592
        + t
        * (
            0.5 * -0.284496736
            + t * (0.5 * 1.421413741 + t * (0.5 * -1.453152027 + t * (0.5 * 1.061405429)))
        )
    )
    tail = poly * e
    phi = jnp.where(u >= 0.0, 1.0 - tail, tail)
    return phi, phi + u * e * (1.0 / math.sqrt(2.0 * math.pi))


def call(body, grid, prefetch, in_specs, out_specs, out_shape, scratch=(), us=2, mib=6, aliases=None, after=()):
    first, last = prefetch + len(in_specs), prefetch + len(in_specs) + len(after)

    def only(*refs):
        body(*refs[:first], *refs[last:])

    kernel = pl.pallas_call(
        only,
        input_output_aliases=aliases or {},
        grid_spec=pltpu.PrefetchScalarGridSpec(
            num_scalar_prefetch=prefetch,
            grid=grid,
            in_specs=list(in_specs) + [pl.BlockSpec(memory_space=pl.ANY)] * len(after),
            out_specs=out_specs,
            scratch_shapes=list(scratch),
        ),
        out_shape=out_shape,
        compiler_params=pltpu.CompilerParams(vmem_limit_bytes=mib * 2**20),
        cost_estimate=pl.CostEstimate(flops=int(us * 1.1e9), bytes_accessed=int(us * 3.5e6), transcendentals=0),
    )
    return lambda *operands: kernel(*operands, *after)


def whole(shape):
    return pl.BlockSpec(shape, lambda *_: (0,) * len(shape))


def shape(dims, dtype):
    return jax.ShapeDtypeStruct(dims, dtype)


def halves():
    lane = lax.broadcasted_iota(jnp.int32, (1, LANES), 1)
    first = (lane < HEAD_DIM).astype(f32)
    return first.astype(bf16), (1.0 - first).astype(bf16)


def split(v, masks):
    return jnp.concatenate([v * masks[0], v * masks[1]], axis=0)


def head_lines(bars):
    line = lax.broadcasted_iota(jnp.int32, (8, LANES), 0)
    lane = lax.broadcasted_iota(jnp.int32, (8, LANES), 1)
    own = lane // HEAD_DIM == line
    lines = [jnp.where(own, bars[s : s + 1], 0.0) for s in range(bars.shape[0])]
    return jnp.concatenate(lines, axis=0).astype(bf16)


def eight(rows):
    return jnp.concatenate(rows + [jnp.zeros((8 - len(rows), rows[0].shape[1]), f32)], axis=0)


def diagonal(blocks, lines):
    zero = jnp.zeros_like(blocks[0])
    rows = [jnp.concatenate([b if i == j else zero for j in range(len(blocks))], axis=1) for i, b in enumerate(blocks)]
    rows += [jnp.zeros_like(rows[0])] * (lines - len(blocks))
    return jnp.concatenate(rows, axis=0).astype(bf16)


def from_hbm(*arrays):
    return [pltpu.with_memory_space_constraint(v, pltpu.HBM) for v in arrays]


def put_shares(at_s, ins, both_ref, one_ref):
    at = 0
    for ref in ins:
        rows = ref.shape[0] // 2
        both_ref[2 * at : 2 * (at + rows)] = ref[...].astype(f32)
        mine = pl.ds(pl.multiple_of(at_s[0] % 2 * rows, rows), rows)
        one_ref[at : at + rows] = ref[mine].astype(f32)
        at += rows


def shares_body(at_s, *refs):
    put_shares(at_s, refs[:3], *refs[3:])


def attention_share(at, wq, wk, wv, devices):
    width, share = wq.shape
    rows = width // devices
    spec = pl.BlockSpec((2 * rows, share), lambda i, s: (s[0] // 2, 0))
    outs = [shape((6 * rows, share), f32), shape((3 * rows, share), f32)]
    return call(
        shares_body, (1,), 1, [spec] * 3, [whole(v.shape) for v in outs], outs
    )(at, *from_hbm(wq, wk, wv))


def hidden_body(at_s, u_ref, o_ref, b_ref, upper_ref, lower_ref, up_both, up_one, down_both, down_one):
    put_shares(at_s, (u_ref, o_ref), up_both, up_one)
    for ref in (up_both, up_one):
        ref[ref.shape[0] - 8 :] = jnp.broadcast_to(b_ref[...], (8, b_ref.shape[1]))
    put_shares(at_s, (upper_ref, lower_ref), down_both, down_one)


def hidden_share(at, wu, wo, bu, wd, devices, after):
    width, hidden = wu.shape
    rows, lines, deep = width // devices, wo.shape[0] // devices, 2 * hidden // devices
    chip = lambda i, s: (s[0] // 2, 0)
    heights = [2 * (rows + lines) + 8, rows + lines + 8, 2 * deep, deep]
    outs = [shape((n, width), f32) for n in heights]
    return call(
        hidden_body,
        (1,),
        1,
        [
            pl.BlockSpec((2 * rows, hidden), chip),
            pl.BlockSpec((2 * lines, width), chip),
            whole((1, hidden)),
            pl.BlockSpec((deep, width), lambda i, s: (s[0] // 2 % 2, 0)),
            pl.BlockSpec((deep, width), lambda i, s: (2 + s[0] // 4, 0)),
        ],
        [whole(v.shape) for v in outs],
        outs,
        after=after,
    )(at, *from_hbm(wu, wo, bu[None], wd, wd))


def cat(groups, after=()):
    arrays, outs = [], []
    for group in groups:
        arrays += [v for v, _, _ in group]
        outs.append(shape((sum(n for _, _, n in group),) + group[0][0].shape[1:], f32))

    def body(*refs):
        ins, got = refs[: len(arrays)], 0
        for group, out in zip(groups, refs[len(arrays) :]):
            at = 0
            for _, first, n in group:
                out[at : at + n] = ins[got][first : first + n]
                at += n
                got += 1

    return call(body, (1,), 0, [whole(v.shape) for v in arrays], [whole(v.shape) for v in outs], outs, after=after)(*arrays)


def norm_body(spans, doc_s, doc_ref, pad_ref, x_ref, g_ref, b_ref, h_ref, m_ref, p_ref, t_ref):
    row_at = pl.program_id(0)
    width = x_ref.shape[-1]
    xhat, _ = norm_parts(x_ref[...].astype(f32))
    h = (xhat * g_ref[...] + b_ref[...]).astype(bf16)
    h_ref[...] = h
    doc = doc_ref[pl.ds(row_at, 1)]
    alive = pad_ref[pl.ds(row_at, 1)] == 1
    rows, region = m_ref.shape[1:]
    lane = lax.broadcasted_iota(jnp.int32, (rows, region), 1)
    line = lax.broadcasted_iota(jnp.int32, (rows, region), 0)
    tag_line = lax.broadcasted_iota(jnp.int32, (rows, LANES), 0)
    picked = jnp.zeros((rows, region), f32)
    tag = jnp.zeros((rows, LANES), f32)
    for s in range(1, spans + 1):
        last = doc_s[row_at, s * SPAN - 1]
        hit = (line == s) & (lane < s * SPAN) & (doc == last) & alive
        picked = jnp.where(hit, 1.0, picked)
        tag = jnp.where(tag_line == s, last.astype(f32), tag)
    m_ref[0] = picked
    sums = nn(picked.astype(bf16), h)
    count = jnp.broadcast_to(jnp.sum(picked, axis=1, keepdims=True), (rows, LANES))
    p_ref[0, :, :width] = sums
    p_ref[0, :, width : width + LANES] = count
    p_ref[0, :, width + LANES :] = tag
    tiles = width // LANES
    for c in range(tiles):
        t_ref[0, c : c + 1] = sums[spans : spans + 1, c * LANES : (c + 1) * LANES]
    t_ref[0, tiles : tiles + 1] = count[spans : spans + 1]
    t_ref[0, tiles + 1 : tiles + 2] = tag[spans : spans + 1]
    t_ref[0, tiles + 2 :] = jnp.zeros((8 - tiles - 2, LANES), f32)


def first_norm(docs, pads, x, gain, shift, rows, region, after):
    tokens, width = x.shape
    spans = region // SPAN
    lines = -(-(spans + 1) // 8) * 8
    wide = width + 2 * LANES
    tok = pl.BlockSpec((region, width), lambda i, *_: (i, 0))

    def row(n, w):
        return pl.BlockSpec((1, n, w), lambda i, *_: (i, 0, 0))

    def body(*refs):
        norm_body(spans, *refs)

    return call(
        body,
        (rows,),
        1,
        [whole(docs.shape), whole(docs.shape), tok, whole((1, width)), whole((1, width))],
        [tok, row(lines, region), row(lines, wide), row(8, LANES)],
        [
            shape((tokens, width), bf16),
            shape((rows, lines, region), f32),
            shape((rows, lines, wide), f32),
            shape((rows, 8, LANES), f32),
        ],
        after=after,
        us=4,
    )(docs, docs, pads, x, gain[None], shift[None])


def state_of(every_ref, d, row_at, tiles):
    lines = every_ref[d, row_at * 8 : row_at * 8 + 8]
    sums = jnp.concatenate([lines[c : c + 1] for c in range(tiles)], axis=1)
    return sums, lines[tiles : tiles + 1], lines[tiles + 1 : tiles + 2]


def owners(me, refs):
    half = len(refs) // 2
    return [(me ^ (2 * (i % half) + i // half), ref) for i, ref in enumerate(refs)]


def means_body(rows, spans, take, me_s, doc_s, doc_ref, pad_ref, p_ref, mean_ref, misc_ref, every_ref):
    me = me_s[0]
    take(me)
    devices = every_ref.shape[0]
    width = mean_ref.shape[-1]
    tiles = width // LANES
    mean_ref[...] = jnp.zeros_like(mean_ref)
    misc_ref[...] = jnp.zeros_like(misc_ref)
    for row_at in range(rows):
        sums = carry = jnp.zeros((1, width), f32)
        count = carry_count = jnp.zeros((1, LANES), f32)
        tag = tag_in = jnp.full((1, LANES), -1.0, f32)
        for d in range(1, devices):
            new_sums, new_count, new_tag = state_of(every_ref, d - 1, row_at, tiles)
            same = (new_tag == tag).astype(f32)
            sums = new_sums + same[:, :1] * sums
            count = new_count + same * count
            tag = new_tag
            mine = me == d
            carry = jnp.where(mine, sums, carry)
            carry_count = jnp.where(mine, count, carry_count)
            tag_in = jnp.where(mine, tag, tag_in)
        for s in range(spans):
            if s == 0:
                run_doc = tag_in
            else:
                run_doc = jnp.full((1, LANES), doc_s[row_at, s * SPAN - 1].astype(f32))
            flag = (tag_in == run_doc).astype(f32)
            total = p_ref[row_at, s : s + 1, :width] + flag[:, :1] * carry
            count_here = p_ref[row_at, s : s + 1, width : width + LANES] + flag * carry_count
            divisor = jnp.maximum(count_here, 1.0)
            mean_ref[row_at, s : s + 1] = total / divisor[:, :1]
            at = row_at * spans + s
            toks = slice(s * SPAN, (s + 1) * SPAN)
            doc = doc_ref[row_at : row_at + 1, toks].astype(f32)
            misc_ref[at, 0:1] = 1.0 / divisor
            misc_ref[at, 1:2] = flag
            misc_ref[at, 2:3] = run_doc
            misc_ref[at, 3:4] = count_here
            misc_ref[at, 4:5] = doc
            misc_ref[at, 5:6] = jnp.where(pad_ref[row_at : row_at + 1, toks] == 1, doc, -2.0)


def document_means(me, docs, pads, prefix, sent, devices, rows, region):
    spans = region // SPAN
    lines = prefix.shape[1]
    width = prefix.shape[2] - 2 * LANES
    in_order = len(sent) == 1
    tall = rows * 8
    outs = [
        shape((rows, lines, width), f32),
        shape((rows * spans, 8, LANES), f32),
        shape((devices, tall, LANES), f32),
    ]

    def body(me_s, doc_s, doc_ref, pad_ref, p_ref, *refs):
        got, outs = refs[: len(sent)], refs[len(sent) :]

        def take(me):
            if in_order:
                outs[2][...] = got[0][...]
                return
            for owner, ref in owners(me, got):
                outs[2][owner] = ref[...]

        means_body(rows, spans, take, me_s, doc_s, doc_ref, pad_ref, p_ref, *outs)

    def tail(v):
        if in_order:
            return whole(v.shape)
        last = v.shape[0] // tall - 1
        return pl.BlockSpec((tall, LANES), lambda *_: (last, 0))

    return call(
        body,
        (1,),
        2,
        [whole(docs.shape), whole(docs.shape), whole(prefix.shape)] + [tail(v) for v in sent],
        [whole(v.shape) for v in outs],
        outs,
    )(me, docs, docs, pads, prefix, *sent)


def take_pieces(at_s, k, came, w_ref):
    here = at_s[0]
    rows = w_ref.shape[0] // len(came)

    def take(ref, first, owner, n):
        at = pl.ds(pl.multiple_of(owner * n, n), n)
        for i in range(3):
            w_ref[at, i * LANES : (i + 1) * LANES] = ref[first + i * n : first + (i + 1) * n].astype(bf16)

    if k == 3:
        for owner, ref in owners(here, came):
            take(ref, 6 * rows, owner, rows)
        return
    half = len(came) // 2
    for core in range(2):

        @pl.when((here + core) % 2 == k - 1)
        def _():
            for j in range(half):
                take(came[core * half + j], 0, here // 2 ^ j, 2 * rows)


def pair_body(load, mean_ref, misc_ref, h_ref, w_ref, qkv_ref, p_ref, ps_ref, o_ref, bar_ref, mix_s):
    load()
    rows = mean_ref.shape[0]
    region = h_ref.shape[0] // rows
    both = nn(hi_lo(mean_ref[...].reshape(-1, mean_ref.shape[-1])), w_ref[:, LANES:])
    half = both.shape[0] // 2
    bars = both[:half] + both[half:]
    bar_ref[0] = bars.reshape(bar_ref.shape[1:])
    masks = halves()
    u = lax.broadcasted_iota(jnp.int32, (SPAN, SPAN), 0)
    t = lax.broadcasted_iota(jnp.int32, (SPAN, SPAN), 1)
    lines = half // rows
    for row_at in range(rows):
        here = slice(row_at * region, (row_at + 1) * region)
        qkv = nn(h_ref[here], w_ref[...])
        qkv_ref[here, :LANES] = (qkv[:, :LANES] * (1.0 / math.sqrt(HEAD_DIM))).astype(bf16)
        qkv_ref[here, LANES:] = qkv[:, LANES:].astype(bf16)
        bars_here = bars[row_at * lines : (row_at + 1) * lines]
        k_lines, v_lines = head_lines(bars_here[:, :LANES]), head_lines(bars_here[:, LANES:])
        summaries = nt(k_lines, qkv_ref[here, :LANES]) + math.log(SPAN)
        all_weights = []
        for s in range(region // SPAN):
            at = row_at * (region // SPAN) + s
            inside = slice(s * SPAN, (s + 1) * SPAN)
            toks = slice(at * SPAN, (at + 1) * SPAN)
            q, k, v = (qkv_ref[toks, i * LANES : (i + 1) * LANES] for i in range(3))
            doc, code = misc_ref[at, 4:5], misc_ref[at, 5:6]
            ok = ((u < t) & (jnp.broadcast_to(code, (SPAN, SPAN)).T == doc)) | (u == t)
            present = (doc == misc_ref[at, 2:3]) & (misc_ref[at, 3:4] > 0.0)
            scores = nt(split(k, masks), q)
            probs, weights = [], []
            for half_at in range(2):
                score = jnp.where(ok, scores[half_at * SPAN : (half_at + 1) * SPAN], MASKED)
                far = jnp.where(present, summaries[8 * s + half_at : 8 * s + half_at + 1, inside], MASKED)
                top = jnp.maximum(jnp.max(score, axis=0, keepdims=True), far)
                e = jnp.exp(score - top)
                w = jnp.exp(far - top)
                inverse = 1.0 / (jnp.sum(e, axis=0, keepdims=True) + w)
                probs.append((e * inverse).astype(bf16))
                weights.append(w * inverse)
            probs = jnp.concatenate(probs, axis=0)
            weights = eight(weights)
            p_ref[0, at] = probs
            ps_ref[0, at] = weights
            all_weights.append(weights)
            mix_s[toks] = tn(probs, split(v, masks))
        o_ref[here] = (mix_s[here] + tn(diagonal(all_weights, lines), v_lines)).astype(bf16)


def pair_forward(at, means, misc, h, source, first, parts, region, kept):
    tokens, width = h.shape
    rows = tokens // region
    spans = region // SPAN
    pairs = width // LANES
    lines = means.shape[1]
    kind, *weights = source

    def pair(i, s):
        return i if kind == "all" else s[1] ^ (first + i)

    in_specs = [whole(means.shape), whole(misc.shape), whole(h.shape)]
    w_spec = pl.BlockSpec((width, 3 * LANES), lambda i, s: (0, pair(i, s)))
    if kind == "all":
        in_specs.append(w_spec)
    else:
        in_specs += [whole(w.shape) for w in weights]
    out_specs = [
        pl.BlockSpec((tokens, 3 * LANES), lambda i, s: (0, pair(i, s))),
        pl.BlockSpec((1, rows * spans, 2 * SPAN, SPAN), lambda i, s: (pair(i, s), 0, 0, 0)),
        pl.BlockSpec((1, rows * spans, 8, SPAN), lambda i, s: (pair(i, s), 0, 0, 0)),
        pl.BlockSpec((tokens, LANES), lambda i, s: (0, pair(i, s))),
        pl.BlockSpec((1, rows, lines, 2 * LANES), lambda i, s: (pair(i, s), 0, 0, 0)),
    ]
    out_shape = [
        shape((tokens, 3 * width), bf16),
        shape((pairs, tokens // SPAN, 2 * SPAN, SPAN), bf16),
        shape((pairs, tokens // SPAN, 8, SPAN), f32),
        shape((tokens, width), bf16),
        shape((pairs, rows, lines, 2 * LANES), f32),
    ]
    if kind != "all":
        out_specs.append(w_spec)
        out_shape.append(shape((width, 3 * width), bf16))
    n_in = 3 + len(weights)
    kept = list(kept or ())

    def body(at_s, *refs):
        ins, got, outs, mix_s = refs[:3], refs[3:n_in], refs[n_in + len(kept) : -1], refs[-1]
        if kind == "all":
            w_ref = got[0]
            load = lambda: None
        else:
            w_ref = outs[5]

            def load():
                for i in range(parts):

                    @pl.when(pl.program_id(0) == i)
                    def _(i=i):
                        if first + i == 0:
                            for m in range(3):
                                w_ref[:, m * LANES : (m + 1) * LANES] = got[m][...]
                        else:
                            take_pieces(at_s, first + i, got[3:], w_ref)

        pair_body(load, *ins, w_ref, *outs[:5], mix_s)

    return call(
        body,
        (parts,),
        1,
        in_specs + [pl.BlockSpec(memory_space=pl.ANY)] * len(kept),
        out_specs,
        out_shape,
        us=5 * parts,
        mib=12,
        aliases={1 + n_in + i: i for i in range(len(kept))},
        scratch=[pltpu.VMEM((tokens, LANES), f32)],
    )(at, means, misc, h, *weights, *kept)


def take_hidden(at_s, own, ups, downs, wu_s, wo_s, wd_s, bu_s):
    here, group = at_s[0], at_s[2]
    lines = own[1].shape[0]
    wu_s[group] = own[0][...]
    wo_s[pl.ds(pl.multiple_of(group * lines, lines), lines)] = own[1][...]
    bu_s[group] = jnp.broadcast_to(own[2][...], bu_s.shape[1:])
    wd_s[group] = own[3][...]
    rows, thin = wu_s.shape[1] // 8, lines // 8
    thick = 3 * (rows + thin)
    deep = downs[0].shape[0] // 12
    for core in range(2):
        up = ups[core]
        sender = (here ^ core) % 2
        near = group ^ (1 + sender)
        bu_s[near] = up[4 * thick :]
        for j in range(4):
            owner = here ^ (2 * j + core)
            first = j * thick
            for to, who, n in ((near, owner // 2, 2), (group ^ 3, owner, 1)):
                at = pl.multiple_of(who * n * rows, n * rows)
                wu_s[to, pl.ds(at, n * rows)] = up[first : first + n * rows].astype(bf16)
                first += n * rows
                at = pl.multiple_of(to * lines + who * n * thin, n * thin)
                wo_s[pl.ds(at, n * thin)] = up[first : first + n * thin].astype(bf16)
                first += n * thin
            chip = here ^ (0, 0, 2, 4)[j]
            place = 4 + chip // 4 * 2 if j % 2 else chip // 2 % 2 * 2
            at = pl.multiple_of(place * deep, 2 * deep)
            down = downs[core]
            first = 3 * j * deep
            wd_s[near, pl.ds(at, 2 * deep)] = down[first : first + 2 * deep].astype(bf16)
            at = pl.multiple_of((place + sender) * deep, deep)
            wd_s[group ^ 3, pl.ds(at, deep)] = down[first + 2 * deep : first + 3 * deep].astype(bf16)


def ffn_body(
    at_s, x_ref, g_ref, o_ref, mine_ref, gain_ref, shift_ref, bd_ref, load, wo_ref,
    out_ref, dmid_ref, do_ref, gwo_ref, gbu_ref, small_ref, gwu_ref, gwd_ref, wu_ref, wd_ref, bu_ref, a_s, du_s,
):
    @pl.when(pl.program_id(0) == 0)
    def _():
        load()
        gwu_ref[...] = jnp.zeros_like(gwu_ref)
        gwd_ref[...] = jnp.zeros_like(gwd_ref)
        gwo_ref[...] = jnp.zeros_like(gwo_ref)
        gbu_ref[...] = jnp.zeros_like(gbu_ref)
        small_ref[...] = jnp.zeros_like(small_ref)

    mid = x_ref[...].astype(f32) + nn(o_ref[...], wo_ref[...])
    xhat, rstd = norm_parts(mid)
    h = (xhat * gain_ref[...] + shift_ref[...]).astype(bf16)
    gm = g_ref[...]
    y = dn = None
    halves_of = 2 * wu_ref.shape[0]
    half = wu_ref.shape[2] // 2

    def cut(i):
        return i // 2, slice(i % 2 * half, (i % 2 + 1) * half)

    def finish(i, a, du, y, dn):
        j, c = cut(i)
        y_part = nn(a, wd_ref[j, c, :])
        dn_part = nt(du, wu_ref[j, :, c])
        return (y_part if y is None else y + y_part), (dn_part if dn is None else dn + dn_part)

    for i in range(halves_of):
        j, c = cut(i)
        up = nn(h, wu_ref[j, :, c]) + bu_ref[j, :1, c]
        da = nt(gm, wd_ref[j, c, :])
        if i > 0:
            y, dn = finish(i - 1, a, du, y, dn)
        phi, slope = gelu_parts(up)
        a = (up * phi).astype(bf16)
        du = (da * slope).astype(bf16)
        a_s[j, :, c] = a
        du_s[j, :, c] = du
    y, dn = finish(halves_of - 1, a, du, y, dn)
    out_ref[...] = (mid + y + bd_ref[...]).astype(bf16)
    g = gm.astype(f32)
    small_ref[2:3] += jnp.sum(dn * xhat, axis=0, keepdims=True)
    small_ref[3:4] += jnp.sum(dn, axis=0, keepdims=True)
    small_ref[4:5] += jnp.sum(g, axis=0, keepdims=True)
    dmid = g + norm_back(dn * gain_ref[...], xhat, rstd)
    dmid_ref[...] = dmid
    gx = dmid.astype(bf16)
    do_ref[...] = nt(gx, wo_ref[...]).astype(bf16)
    gwo_ref[...] += tn(mine_ref[...], gx)
    group = at_s[2]
    du = du_s[group]
    gwd_ref[...] += tn(a_s[group], gm)
    gwu_ref[...] += tn(h, du)
    gbu = jnp.sum(du.astype(f32), axis=0, keepdims=True)
    gbu_ref[...] += gbu
    if gbu.shape[1] == small_ref.shape[1]:
        small_ref[5:6] += gbu


def by_core(core, keep_ref, give_ref):
    return (keep_ref, core), (give_ref, 1 - core)


def feed_forward(at, x, g, o, gain, shift, bd, source, devices):
    tokens, width = x.shape
    kind, *weights = source
    came = kind == "came"
    if came:
        *own, ups, downs, bias = weights
        hidden, groups = own[0].shape[1], 4
        args = [*own, *ups, *downs, bias]
        n_up, n_down = 4 + len(ups), 4 + len(ups) + len(downs)
        last = bias.shape[0] // 8 - 1
        specs = [whole(w.shape) for w in args[:n_down]] + [pl.BlockSpec((8, width), lambda i, *_: (last, 0))]
    else:
        args = weights
        groups, _, hidden = args[0].shape
        specs = [whole(w.shape) for w in args]
    steps = 4
    chunk = tokens // steps
    tok = pl.BlockSpec((chunk, width), lambda i, *_: (i, 0))
    n_w = len(args)
    scratch = [pltpu.VMEM((groups, chunk, hidden), bf16)] * 2
    grads = [shape((width, hidden), f32), shape((hidden, width), f32)]
    if came:
        scratch += [pltpu.VMEM(v.shape, f32) for v in grads]
        scratch += [
            pltpu.VMEM((groups, width, hidden), bf16),
            pltpu.VMEM((width, width), bf16),
            pltpu.VMEM((groups, 8, hidden), f32),
            pltpu.VMEM((groups, hidden, width), bf16),
        ]
        grads = [shape((devices // 2, (width + hidden) // devices, width), f32)] * 2

    def body(at_s, *refs):
        ins, got = refs[:7], refs[7 : 7 + n_w]
        outs, acts, held = refs[7 + n_w : 15 + n_w], refs[15 + n_w : 17 + n_w], refs[17 + n_w :]
        if not came:
            wu_r, wo_r, bu_r, wd_r = got
            ffn_body(at_s, *ins, lambda: None, wo_r, *outs, wu_r, wd_r, bu_r, *acts)
            return
        gwu_s, gwd_s, wu_s, wo_s, bu_s, wd_s = held

        def load():
            take_hidden(at_s, got[:4], got[4:n_up], got[n_up:n_down], wu_s, wo_s, wd_s, bu_s)
            bu_s[at_s[2] ^ 3] = got[n_down][...]

        ffn_body(at_s, *ins, load, wo_s, *outs[:6], gwu_s, gwd_s, wu_s, wd_s, bu_s, *acts)

        @pl.when(pl.program_id(0) == steps - 1)
        def _():
            rows = width // devices
            for out, c in by_core(at_s[0] % 2, *outs[6:]):
                for j in range(devices // 2):
                    lines = pl.ds(pl.multiple_of((2 * j + c) * rows, rows), rows)
                    out[j, :rows] = gwu_s[lines]
                    out[j, rows:] = gwd_s[lines]

    return call(
        body,
        (steps,),
        1,
        [tok, tok, tok, pl.BlockSpec((chunk, LANES), lambda i, s: (i, s[1])),
         whole((1, width)), whole((1, width)), whole((1, width))] + specs,
        [tok, tok, tok, whole((LANES, width)), whole((1, hidden)), whole((8, width))] + [whole(v.shape) for v in grads],
        [
            shape((tokens, width), bf16),
            pltpu.HBM((tokens, width), f32),
            shape((tokens, width), bf16),
            shape((LANES, width), f32),
            shape((1, hidden), f32),
            shape((8, width), f32),
        ] + grads,
        scratch=scratch,
        us=38,
        mib=26,
    )(at, x, g, o, o, gain[None], shift[None], bd[None], *args)


def pair_back_body(rows, qkv_ref, do_ref, p_ref, ps_ref, bar_ref, misc_ref, d_ref, g_ref, d_s):
    masks = halves()
    wide = 2 * LANES
    region = do_ref.shape[0] // rows
    spans = region // SPAN
    for row_at in range(rows):
        here = slice(row_at * region, (row_at + 1) * region)
        bars = bar_ref[0, row_at]
        lines = bars.shape[0]
        k_lines, v_lines = head_lines(bars[:, :LANES]), head_lines(bars[:, LANES:])
        dp_far = nt(v_lines, do_ref[here])
        all_far, all_weights = [], []
        for s in range(spans):
            at = row_at * spans + s
            inside = slice(s * SPAN, (s + 1) * SPAN)
            toks = slice(at * SPAN, (at + 1) * SPAN)
            q, k, v = (qkv_ref[toks, i * LANES : (i + 1) * LANES] for i in range(3))
            do = do_ref[toks]
            weight = ps_ref[0, at]
            dp = nt(split(v, masks), do)
            probs, grads, far = [], [], []
            for half in range(2):
                p_half = p_ref[0, at, half * SPAN : (half + 1) * SPAN, :]
                p = p_half.astype(f32)
                dp_half = dp[half * SPAN : (half + 1) * SPAN]
                w, dw = weight[half : half + 1], dp_far[8 * s + half : 8 * s + half + 1, inside]
                r = jnp.sum(p * dp_half, axis=0, keepdims=True) + w * dw
                probs.append(p_half)
                grads.append((p * (dp_half - r)).astype(bf16))
                far.append(w * (dw - r))
            all_far.append(eight(far))
            all_weights.append(weight)
            d_s[toks, :LANES] = tn(jnp.concatenate(grads, axis=0), split(k, masks))
            d_s[toks, LANES:wide] = nn(jnp.concatenate(grads, axis=1), split(q, masks))
            d_s[toks, wide:] = nn(jnp.concatenate(probs, axis=1), split(do, masks))
        far = diagonal(all_far, lines)
        dq = d_s[here, :LANES] + tn(far, k_lines)
        d_ref[here, :LANES] = (dq.astype(bf16).astype(f32) * (1.0 / math.sqrt(HEAD_DIM))).astype(bf16)
        line = lax.broadcasted_iota(jnp.int32, (8 * lines, LANES), 0)
        lane = lax.broadcasted_iota(jnp.int32, (8 * lines, LANES), 1)
        own = lane // HEAD_DIM == line % 8
        gk = jnp.where(own, nn(far, qkv_ref[here, :LANES]), 0.0)
        gv = jnp.where(own, nn(diagonal(all_weights, lines), do_ref[here]), 0.0)
        out = jnp.zeros((1, wide), f32)
        after = None
        for s in reversed(range(spans)):
            at = row_at * spans + s
            toks = slice(at * SPAN, (at + 1) * SPAN)
            dkv = d_s[toks, LANES:]
            gkv = [jnp.sum(v[8 * s : 8 * s + 8], axis=0, keepdims=True) for v in (gk, gv)]
            inverse, flag = misc_ref[at, 0:1, :], misc_ref[at, 1:2, :]
            gkv = jnp.concatenate(gkv, axis=1) * jnp.concatenate([inverse, inverse], axis=1)
            out = out + jnp.concatenate([flag, flag], axis=1) * gkv
            if after is None:
                after = gkv
            else:
                reached = jnp.broadcast_to(misc_ref[at, 5:6], (SPAN, SPAN)).T == misc_ref[at + 1, 2:3]
                dkv = dkv + jnp.where(jnp.concatenate([reached, reached], axis=1), after, 0.0)
                same = (misc_ref[at, 2:3] == misc_ref[at + 1, 2:3]).astype(f32)
                after = gkv + jnp.concatenate([same, same], axis=1) * after
            d_ref[toks, LANES:] = dkv.astype(bf16)
        g_ref[row_at, :, :LANES] = jnp.zeros((1, LANES), f32)
        g_ref[row_at, :, LANES:] = out


def pair_backward(at, qkv, do, p, ps, bars, misc, h, gwo, devices, region, first, parts, kept):
    tokens, width = do.shape
    rows = tokens // region
    spans = region // SPAN
    lines = bars.shape[2]
    own = h is not None

    def pair(i, s):
        return s[1] ^ (first + i)

    tok3 = pl.BlockSpec((tokens, 3 * LANES), lambda i, s: (0, pair(i, s)))
    back = pl.BlockSpec((rows, 1, 3 * LANES), lambda i, s: (0, 0, pair(i, s)))
    in_specs = [
        tok3,
        pl.BlockSpec((tokens, LANES), lambda i, s: (0, pair(i, s))),
        pl.BlockSpec((1, rows * spans, 2 * SPAN, SPAN), lambda i, s: (pair(i, s), 0, 0, 0)),
        pl.BlockSpec((1, rows * spans, 8, SPAN), lambda i, s: (pair(i, s), 0, 0, 0)),
        pl.BlockSpec((1, rows, lines, 2 * LANES), lambda i, s: (pair(i, s), 0, 0, 0)),
        whole(misc.shape),
    ]
    args = [qkv, do, p, ps, bars, misc]
    out_specs = [tok3, back]
    out_shape = [shape((tokens, 3 * width), bf16), shape((rows, 1, 3 * width), f32)]
    if own:
        in_specs.append(whole(h.shape))
        args.append(h)
        grads = [shape((width, 3 * LANES), f32)]
        if gwo is not None:
            in_specs.append(whole(gwo.shape))
            args.append(gwo)
            grads = [shape((devices // 2, width // devices, width), f32)] * 2
        out_specs += [whole(v.shape) for v in grads]
        out_shape += grads
    n_in = len(args)
    kept = list(kept or ())

    def body(at_s, *refs):
        outs = refs[n_in + len(kept) : n_in + len(kept) + len(out_shape)]
        held = refs[n_in + len(kept) + len(out_shape) :]
        pair_back_body(rows, *refs[:6], outs[0], outs[1], held[0])
        if own:
            grads = tn(refs[6][...], outs[0][...])
            if gwo is None:
                outs[2][...] = grads
            else:
                held[1][...] = grads
                lines_q, lines_o = width // devices, LANES // devices
                for out, c in by_core(at_s[0] % 2, *outs[2:]):
                    for j in range(devices // 2):
                        owner = 2 * j + c
                        out[j, :, : 3 * LANES] = held[1][pl.ds(pl.multiple_of(owner * lines_q, lines_q), lines_q)]
                        go = refs[7][pl.ds(pl.multiple_of(owner * lines_o, lines_o), lines_o)]
                        for i in range(width // LANES):
                            out[j, i * lines_o : (i + 1) * lines_o, 3 * LANES :] = go[:, i * LANES : (i + 1) * LANES]

    return call(
        body,
        (parts,),
        1,
        in_specs + [pl.BlockSpec(memory_space=pl.ANY)] * len(kept),
        out_specs,
        out_shape,
        us=6 * parts,
        mib=12,
        aliases={1 + n_in + i: i for i in range(len(kept))},
        scratch=[pltpu.VMEM((tokens, 3 * LANES), f32), pltpu.VMEM((width, 3 * LANES), f32)],
    )(at, *args, *kept)


def input_body(
    rows, at_s, every_ref, backs, misc_ref, x_ref, gain_ref, dmid_ref, d_ref, w_ref, so_far_ref,
    gi_ref, small_ref, late_ref, through_s, tag_s, back_s,
):
    me = at_s[0]
    devices = every_ref.shape[0]
    width = x_ref.shape[-1]
    tiles = width // LANES
    wide = w_ref.shape[1]

    @pl.when(pl.program_id(0) == 0)
    def _():
        small_ref[...] = so_far_ref[...]
        if len(backs) == 1:
            for d in range(devices):
                back_s[d] = backs[0][d * rows : (d + 1) * rows]
        else:
            for core, ref in enumerate(backs):
                for j in range(devices // 2):
                    back_s[me ^ (2 * j + core)] = ref[j * rows : (j + 1) * rows]
        mine_lanes = pl.ds(pl.multiple_of(at_s[1] * 3 * LANES, LANES), 3 * LANES)
        heads, tails = [], []
        for r in range(rows):
            run = mine = jnp.zeros((1, wide), f32)
            own_run = jnp.zeros((1, 3 * LANES), f32)
            tag = None
            for d in reversed(range(devices)):
                sums, _, tag_here = state_of(every_ref, d, r, tiles)
                if tag is not None:
                    same = (tag == tag_here).astype(f32)[:, :1]
                    run = back_s[d + 1, r : r + 1] + same * run
                    own_run = back_s[d + 1, r : r + 1, mine_lanes] + same * own_run
                    mine = jnp.where(me == d, run, mine)
                tag = tag_here
                tag_s[r : r + 1] = jnp.where(me == d, tag, tag_s[r : r + 1])
                heads.append(sums)
                tails.append(own_run)
            through = nt(hi_lo(jnp.broadcast_to(mine, (8, wide))), w_ref[...])
            through_s[r : r + 1] = through[0:1] + through[8:9]
        late_ref[...] = lax.dot_general(
            jnp.concatenate(heads, axis=0), jnp.concatenate(tails, axis=0), (((0,), (0,)), ((), ())),
            preferred_element_type=f32, precision=lax.Precision.HIGHEST,
        )

    dn = nt(d_ref[...], w_ref[...])
    spans = misc_ref.shape[0]
    added = []
    for i in range(spans):
        at = pl.program_id(0) * spans + i
        row_at = at // (pl.num_programs(0) * spans // rows)
        reached = jnp.broadcast_to(misc_ref[i, 5:6], (SPAN, SPAN)).T == tag_s[pl.ds(row_at, 1)]
        added.append(jnp.where(jnp.concatenate([reached] * tiles, axis=1), through_s[pl.ds(row_at, 1)], 0.0))
    dn = dn + jnp.concatenate(added, axis=0)
    xhat, rstd = norm_parts(x_ref[...].astype(f32))
    small_ref[0:1] += jnp.sum(dn * xhat, axis=0, keepdims=True)
    small_ref[1:2] += jnp.sum(dn, axis=0, keepdims=True)
    gi_ref[...] = dmid_ref[...] + norm_back(dn * gain_ref[...], xhat, rstd)


def input_grads(at, every, back, misc, x, gain, dmid, d, w, small, rows):
    tokens, width = x.shape
    devices = every.shape[0]
    steps = 7 if tokens // SPAN % 7 == 0 else tokens // SPAN
    chunk = tokens // steps
    tok = pl.BlockSpec((chunk, width), lambda i, *_: (i, 0))

    def body(at_s, every_ref, *refs):
        input_body(rows, at_s, every_ref, refs[: len(back)], *refs[len(back) :])

    return call(
        body,
        (steps,),
        1,
        [
            whole(every.shape),
            *[whole(v.shape) for v in back],
            pl.BlockSpec((chunk // SPAN,) + misc.shape[1:], lambda i, *_: (i, 0, 0)),
            tok, whole((1, width)), tok,
            pl.BlockSpec((chunk, 3 * width), lambda i, *_: (i, 0)),
            whole(w.shape),
            whole(small.shape),
        ],
        [tok, whole((8, width)), whole((width, 3 * LANES))],
        [shape((tokens, width), f32), shape((8, width), f32), shape((width, 3 * LANES), f32)],
        scratch=[
            pltpu.VMEM((rows, width), f32), pltpu.VMEM((rows, LANES), f32), pltpu.VMEM((devices, rows, 3 * width), f32)
        ],
        us=1,
        mib=10,
    )(at, every, *back, misc, x, gain[None], dmid, d, w, small)


def fold_body(count, at_s, *refs):
    chip = at_s[0] // 2
    outs = refs[2 * count :]
    at = 0
    for keep, got in zip(refs[:count], refs[count : 2 * count]):
        rows = keep.shape[1]
        for j, out in enumerate(outs):
            out[at : at + rows] = keep[chip ^ j] + got[chip ^ j]
        at += rows


def fold(at, keeps, gots):
    chips, _, width = keeps[0].shape
    outs = [shape((sum(v.shape[1] for v in keeps), width), f32)] * chips

    def body(*refs):
        fold_body(len(keeps), *refs)

    args = [*keeps, *gots]
    return call(body, (1,), 1, [whole(v.shape) for v in args], [whole(v.shape) for v in outs], outs)(at, *args)


def add_body(*refs):
    total = refs[0][...]
    for ref in refs[1:-1]:
        total = total + ref[...]
    refs[-1][...] = total


def add_up(parts, after):
    spec = whole(parts[0].shape)
    return call(add_body, (1,), 0, [spec] * len(parts), spec, shape(parts[0].shape, f32), after=after)(*parts)


def unpack_body(at_s, *refs):
    *pieces, late_ref, gq_ref, gk_ref, gv_ref, go_ref, gu_ref, gd_ref = refs
    rows = gu_ref.shape[0] // len(pieces)
    lines = go_ref.shape[0] // len(pieces)
    for owner, ref in owners(at_s[0], pieces):
        at = pl.ds(pl.multiple_of(owner * rows, rows), rows)
        gu_ref[at] = ref[:rows]
        gd_ref[at] = ref[rows : 2 * rows]
        for i, out in enumerate((gq_ref, gk_ref, gv_ref)):
            lanes = slice(i * LANES, (i + 1) * LANES)
            out[at] = ref[2 * rows :, lanes] + late_ref[at, lanes]
        at = pl.ds(pl.multiple_of(owner * lines, lines), lines)
        for i in range(go_ref.shape[1] // LANES):
            first = 2 * rows + i * lines
            go_ref[at, i * LANES : (i + 1) * LANES] = ref[first : first + lines, 3 * LANES :]


def unpack(at, pieces, late):
    width = pieces[0].shape[1]
    thin = shape((width, LANES), f32)
    outs = [thin, thin, thin, shape((LANES, width), f32), shape((width, width), f32), shape((width, width), f32)]
    args = [*pieces, late]
    return call(
        unpack_body, (1,), 1, [whole(v.shape) for v in args], [whole(v.shape) for v in outs], outs
    )(at, *args)


def totals_body(small_ref, *outs):
    total = small_ref[0]
    for d in range(1, small_ref.shape[0]):
        total = total + small_ref[d]
    for i, out in enumerate(outs):
        out[...] = total[i : i + 1]


def totals(small):
    outs = [shape((1, small.shape[2]), f32)] * 6
    return call(totals_body, (1,), 0, [whole(small.shape)], [whole(v.shape) for v in outs], outs)(small)


def narrow_body(w_ref, o_ref):
    o_ref[...] = w_ref[...].astype(bf16)


def gathered(part):
    every = lax.all_gather(part.astype(f32), "head")
    flat = every.reshape(-1, part.shape[1])
    chunk = flat.shape[0] // 8
    block = pl.BlockSpec((chunk, part.shape[1]), lambda i: (i, 0))
    return call(narrow_body, (8,), 0, [block], block, shape(flat.shape, bf16))(flat).reshape(every.shape)


def swap(v, axis, mask):
    return lax.ppermute(v, axis, [(i, i ^ mask) for i in range(lax.axis_size(axis))])


def along_z(both, one):
    groups, devices = lax.axis_size("head"), lax.axis_size("seq")
    by_core = [(d * groups + h, d * groups + (h ^ (1 + d % 2))) for d in range(devices) for h in range(groups)]
    return lax.ppermute(both, ("seq", "head"), by_core), swap(one, "head", 3)


def both_cores(pieces, after):
    first, *rest = pieces
    theirs = [swap(first, "seq", 1)]
    held = lax.optimization_barrier((after, *rest))
    return pieces + theirs + [swap(v, "seq", 1) for v in held[1:]]


def on_device(
    inputs, doc_ids, pad_mask, ln1_gain, ln1_shift, w_query, w_key, w_value, w_out,
    ln2_gain, ln2_shift, w_up, b_up, w_down, b_down, out_grad,
):
    rows, region, width = inputs.shape
    tokens = rows * region
    devices = lax.axis_size("seq")
    groups = lax.axis_size("head")
    here = lax.axis_index("seq")
    group = lax.axis_index("head")
    share = width // groups
    pairs = width // LANES
    spans = region // SPAN
    own_pair = group * share // LANES
    at = jnp.stack([here, own_pair, group]).astype(jnp.int32)
    x = inputs.reshape(tokens, width)
    g = out_grad.reshape(tokens, width)
    by_share = share == LANES and devices == 8 and groups == 4

    if by_share:
        others = range(2, devices, 2)
        a_both, a_one = along_z(*attention_share(at, w_query, w_key, w_value, devices))
    h1, m, prefix, tiny = first_norm(
        doc_ids, pad_mask, x, ln1_gain, ln1_shift, rows, region, []
    )
    tiny = tiny.reshape(rows * 8, LANES)
    if by_share:
        (a_sent,) = cat([[(v, 0, v.shape[0]) for v in (a_both, a_one, tiny)]])
        a_moved = [swap(a_sent, "seq", j) for j in others]
        up_both, up_one, down_both, down_one = hidden_share(at, w_up, w_out, b_up, w_down, devices, [h1])
        up_both, up_one = along_z(up_both, up_one)
        down_both, down_one = along_z(down_both, down_one)
        (up_sent,) = cat([[(v, 0, v.shape[0] - 8) for v in (up_both, up_one)]])
        a_pieces = both_cores([a_sent] + a_moved, up_sent)
        up_moved = [swap(up_sent, "seq", j) for j in others]
        means, misc, every = document_means(at, doc_ids, pad_mask, prefix, a_pieces, devices, rows, region)
        source = ("came", w_query, w_key, w_value, *a_pieces)
        qkv, p, ps, o, bars, w_in = pair_forward(at, means, misc, h1, source, 0, pairs, region, None)
        deep = down_one.shape[0] // 2
        upper, lower = cat([[(down_both, 2 * i * deep, 2 * deep), (down_one, i * deep, deep)] for i in range(2)], after=[o])
        down_moved = [upper, lower, swap(upper, "seq", 2), swap(lower, "seq", 4)]
        (up_half,) = cat(
            [[(v, 0, v.shape[0]) for v in [up_sent] + up_moved] + [(up_both, up_both.shape[0] - 8, 8)]], after=[upper]
        )
        (down_half,) = cat([[(v, 0, v.shape[0]) for v in down_moved]], after=[up_half])
        up_pieces = [up_half, swap(up_half, "seq", 1)]
        down_pieces = [down_half, swap(down_half, "seq", 1)]
        ffn_source = ("came", w_up, w_out, b_up[None], w_down, up_pieces, down_pieces, up_one)
    else:
        every = lax.all_gather(tiny, "seq")
        means, misc, every = document_means(at, doc_ids, pad_mask, prefix, [every], devices, rows, region)
        w_in = gathered(jnp.concatenate([w_query, w_key, w_value], axis=1))
        w_in = w_in.reshape(groups, width, 3, share).transpose(1, 2, 0, 3).reshape(width, 3, pairs, LANES)
        w_in = w_in.transpose(0, 2, 1, 3).reshape(width, 3 * width)
        qkv, p, ps, o, bars = pair_forward(at, means, misc, h1, ("all", w_in), 0, pairs, region, None)
        bu = lax.all_gather(b_up, "head")
        bu = jnp.broadcast_to(bu[:, None], (groups, 8, bu.shape[1]))
        ffn_source = ("all", gathered(w_up), gathered(w_out).reshape(width, width), bu, gathered(w_down))

    out, dmid, do, gwo, gbu, small, *hidden_grads = feed_forward(
        at, x, g, o, ln2_gain, ln2_shift, b_down, ffn_source, devices
    )
    back_args = (at, qkv, do, p, ps, bars, misc)
    d, g_back, *pair_grads = pair_backward(
        *back_args, h1, gwo if by_share else None, devices, region, 0, 1, None
    )
    if by_share:
        keeps, gives = zip(hidden_grads, pair_grads)
        folded = fold(at, keeps, [swap(v, "seq", 1) for v in gives])
        arrived = [swap(v, "seq", j) for v, j in zip(folded[1:], others)]
    d, g_back = pair_backward(*back_args, None, None, devices, region, 1, pairs - 1, (d, g_back))
    if by_share:
        g_back = g_back.reshape(rows, 3 * width)
        total = add_up([folded[0]] + arrived, [g_back])
        near = [swap(g_back, "seq", j) for j in others[:-1]]
        held, _ = lax.optimization_barrier((g_back, total))
        far = swap(held, "seq", others[-1])
        spread = [swap(total, "seq", j) for j in others]
        (back,) = cat([[(v, 0, rows) for v in [g_back] + near + [far]]])
        back = [back, swap(back, "seq", 1)]
    else:
        back = [lax.all_gather(g_back, "seq").reshape(devices * rows, 3 * width)]
    grad_inputs, small, late = input_grads(at, every, back, misc, x, ln1_gain, dmid, d, w_in, small, rows)
    out = out.reshape(rows, region, width)
    grad_inputs = grad_inputs.reshape(rows, region, width)
    if by_share:
        small = lax.all_gather(small, "seq")
        pieces = both_cores([total] + spread, small)
        gq, gk, gv, gwo, gwu, gwd = unpack(at, pieces, late)
        g1, s1, g2, s2, gbd, gbu = (v[0] for v in totals(small))
        return out, grad_inputs, g1, s1, gq, gk, gv, gwo, g2, s2, gwu, gbu, gwd, gbd

    gwu, gwd = hidden_grads
    (gw,) = pair_grads
    gwu, gwd, gwo, gbu, small, gw = lax.psum((gwu, gwd, gwo, gbu, small, gw), "seq")
    gw = gw + late
    gq, gk, gv = (gw[:, i * LANES : (i + 1) * LANES] for i in range(3))
    if share != LANES:
        inner = group * share - own_pair * LANES
        gq, gk, gv = (lax.dynamic_slice_in_dim(v, inner, share, 1) for v in (gq, gk, gv))
        gwo = lax.dynamic_slice_in_dim(gwo, inner, share, 0)
    return (
        out, grad_inputs, small[0], small[1], gq, gk, gv, gwo, small[2], small[3], gwu, gbu[0], gwd, small[4]
    )


def solution(mesh):
    tok = P(None, "seq", None)
    ids = P(None, "seq")
    cols, lines = P(None, "head"), P("head", None)
    in_specs = (
        tok, ids, ids, P(), P(), cols, cols, cols, lines, P(), P(), cols, P("head"), lines, P(), tok,
    )
    out_specs = (
        tok, tok, P(), P(), cols, cols, cols, lines, P(), P(), cols, P("head"), lines, P(),
    )
    return jax.shard_map(on_device, mesh=mesh, in_specs=in_specs, out_specs=out_specs, check_vma=False)
```

```python
import math

import jax
import jax.numpy as jnp
from jax import lax
from jax.experimental import pallas as pl
from jax.experimental.pallas import tpu as pltpu
from jax.sharding import PartitionSpec as P

HEAD_DIM = 64
SPAN = 128
LANES = 128
NORM_EPS = 1e-05
MASKED = -1e30
f32, bf16 = jnp.float32, jnp.bfloat16


def nn(a, b):
    return lax.dot_general(a, b, (((1,), (0,)), ((), ())), preferred_element_type=f32)


def nt(a, b):
    return lax.dot_general(a, b, (((1,), (1,)), ((), ())), preferred_element_type=f32)


def tn(a, b):
    return lax.dot_general(a, b, (((0,), (0,)), ((), ())), preferred_element_type=f32)


def hi_lo(v):
    hi = v.astype(bf16).astype(f32)
    return jnp.concatenate([hi, v - hi], axis=0).astype(bf16)


def twice(v):
    return jnp.concatenate([v, v], axis=0).astype(bf16)


def norm_parts(x):
    mean = jnp.mean(x, axis=-1, keepdims=True)
    centred = x - mean
    rstd = lax.rsqrt(jnp.mean(centred * centred, axis=-1, keepdims=True) + NORM_EPS)
    return centred * rstd, rstd


def norm_back(y, xhat, rstd):
    return rstd * (
        y
        - jnp.mean(y, axis=-1, keepdims=True)
        - xhat * jnp.mean(y * xhat, axis=-1, keepdims=True)
    )


def gelu_parts(u):
    z = jnp.abs(u)
    t = 1.0 / (1.0 + (0.3275911 * math.sqrt(0.5)) * z)
    e = jnp.exp(-0.5 * u * u)
    poly = t * (
        0.5 * 0.254829592
        + t
        * (
            0.5 * -0.284496736
            + t * (0.5 * 1.421413741 + t * (0.5 * -1.453152027 + t * (0.5 * 1.061405429)))
        )
    )
    tail = poly * e
    phi = jnp.where(u >= 0.0, 1.0 - tail, tail)
    return phi, phi + u * e * (1.0 / math.sqrt(2.0 * math.pi))


def call(body, grid, prefetch, in_specs, out_specs, out_shape, scratch=(), us=2, mib=6, aliases=None, after=()):
    first, last = prefetch + len(in_specs), prefetch + len(in_specs) + len(after)

    def only(*refs):
        body(*refs[:first], *refs[last:])

    kernel = pl.pallas_call(
        only,
        input_output_aliases=aliases or {},
        grid_spec=pltpu.PrefetchScalarGridSpec(
            num_scalar_prefetch=prefetch,
            grid=grid,
            in_specs=list(in_specs) + [pl.BlockSpec(memory_space=pl.ANY)] * len(after),
            out_specs=out_specs,
            scratch_shapes=list(scratch),
        ),
        out_shape=out_shape,
        compiler_params=pltpu.CompilerParams(vmem_limit_bytes=mib * 2**20),
        cost_estimate=pl.CostEstimate(flops=int(us * 1.1e9), bytes_accessed=int(us * 3.5e6), transcendentals=0),
    )
    return lambda *operands: kernel(*operands, *after)


def whole(shape):
    return pl.BlockSpec(shape, lambda *_: (0,) * len(shape))


def shape(dims, dtype):
    return jax.ShapeDtypeStruct(dims, dtype)


def halves():
    lane = lax.broadcasted_iota(jnp.int32, (1, LANES), 1)
    first = (lane < HEAD_DIM).astype(f32)
    return first.astype(bf16), (1.0 - first).astype(bf16)


def split(v, masks):
    return jnp.concatenate([v * masks[0], v * masks[1]], axis=0)


def head_lines(bars):
    line = lax.broadcasted_iota(jnp.int32, (8, LANES), 0)
    lane = lax.broadcasted_iota(jnp.int32, (8, LANES), 1)
    own = lane // HEAD_DIM == line
    lines = [jnp.where(own, bars[s : s + 1], 0.0) for s in range(bars.shape[0])]
    return jnp.concatenate(lines, axis=0).astype(bf16)


def eight(rows):
    return jnp.concatenate(rows + [jnp.zeros((8 - len(rows), rows[0].shape[1]), f32)], axis=0)


def diagonal(blocks, lines):
    zero = jnp.zeros_like(blocks[0])
    rows = [jnp.concatenate([b if i == j else zero for j in range(len(blocks))], axis=1) for i, b in enumerate(blocks)]
    rows += [jnp.zeros_like(rows[0])] * (lines - len(blocks))
    return jnp.concatenate(rows, axis=0).astype(bf16)


def from_hbm(*arrays):
    return [pltpu.with_memory_space_constraint(v, pltpu.HBM) for v in arrays]


def put_shares(at_s, ins, both_ref, one_ref):
    at = 0
    for ref in ins:
        rows = ref.shape[0] // 2
        both_ref[2 * at : 2 * (at + rows)] = ref[...].astype(f32)
        mine = pl.ds(pl.multiple_of(at_s[0] % 2 * rows, rows), rows)
        one_ref[at : at + rows] = ref[mine].astype(f32)
        at += rows


def shares_body(at_s, *refs):
    put_shares(at_s, refs[:3], *refs[3:])


def attention_share(at, wq, wk, wv, devices):
    width, share = wq.shape
    rows = width // devices
    spec = pl.BlockSpec((2 * rows, share), lambda i, s: (s[0] // 2, 0))
    outs = [shape((6 * rows, share), f32), shape((3 * rows, share), f32)]
    return call(
        shares_body, (1,), 1, [spec] * 3, [whole(v.shape) for v in outs], outs
    )(at, *from_hbm(wq, wk, wv))


def hidden_body(at_s, u_ref, o_ref, b_ref, upper_ref, lower_ref, up_both, up_one, down_both, down_one):
    put_shares(at_s, (u_ref, o_ref), up_both, up_one)
    for ref in (up_both, up_one):
        ref[ref.shape[0] - 8 :] = jnp.broadcast_to(b_ref[...], (8, b_ref.shape[1]))
    put_shares(at_s, (upper_ref, lower_ref), down_both, down_one)


def hidden_share(at, wu, wo, bu, wd, devices, after):
    width, hidden = wu.shape
    rows, lines, deep = width // devices, wo.shape[0] // devices, 2 * hidden // devices
    chip = lambda i, s: (s[0] // 2, 0)
    heights = [2 * (rows + lines) + 8, rows + lines + 8, 2 * deep, deep]
    outs = [shape((n, width), f32) for n in heights]
    return call(
        hidden_body,
        (1,),
        1,
        [
            pl.BlockSpec((2 * rows, hidden), chip),
            pl.BlockSpec((2 * lines, width), chip),
            whole((1, hidden)),
            pl.BlockSpec((deep, width), lambda i, s: (s[0] // 2 % 2, 0)),
            pl.BlockSpec((deep, width), lambda i, s: (2 + s[0] // 4, 0)),
        ],
        [whole(v.shape) for v in outs],
        outs,
        after=after,
    )(at, *from_hbm(wu, wo, bu[None], wd, wd))


def cat(groups, after=()):
    arrays, outs = [], []
    for group in groups:
        arrays += [v for v, _, _ in group]
        outs.append(shape((sum(n for _, _, n in group),) + group[0][0].shape[1:], f32))

    def body(*refs):
        ins, got = refs[: len(arrays)], 0
        for group, out in zip(groups, refs[len(arrays) :]):
            at = 0
            for _, first, n in group:
                out[at : at + n] = ins[got][first : first + n]
                at += n
                got += 1

    return call(body, (1,), 0, [whole(v.shape) for v in arrays], [whole(v.shape) for v in outs], outs, after=after)(*arrays)


def norm_body(spans, doc_s, doc_ref, pad_ref, x_ref, g_ref, b_ref, h_ref, m_ref, p_ref, t_ref):
    row_at = pl.program_id(0)
    width = x_ref.shape[-1]
    xhat, _ = norm_parts(x_ref[...].astype(f32))
    h = (xhat * g_ref[...] + b_ref[...]).astype(bf16)
    h_ref[...] = h
    doc = doc_ref[pl.ds(row_at, 1)]
    alive = pad_ref[pl.ds(row_at, 1)] == 1
    rows, region = m_ref.shape[1:]
    lane = lax.broadcasted_iota(jnp.int32, (rows, region), 1)
    line = lax.broadcasted_iota(jnp.int32, (rows, region), 0)
    tag_line = lax.broadcasted_iota(jnp.int32, (rows, LANES), 0)
    picked = jnp.zeros((rows, region), f32)
    tag = jnp.zeros((rows, LANES), f32)
    for s in range(1, spans + 1):
        last = doc_s[row_at, s * SPAN - 1]
        hit = (line == s) & (lane < s * SPAN) & (doc == last) & alive
        picked = jnp.where(hit, 1.0, picked)
        tag = jnp.where(tag_line == s, last.astype(f32), tag)
    m_ref[0] = picked
    sums = nn(picked.astype(bf16), h)
    count = jnp.broadcast_to(jnp.sum(picked, axis=1, keepdims=True), (rows, LANES))
    p_ref[0, :, :width] = sums
    p_ref[0, :, width : width + LANES] = count
    p_ref[0, :, width + LANES :] = tag
    tiles = width // LANES
    for c in range(tiles):
        t_ref[0, c : c + 1] = sums[spans : spans + 1, c * LANES : (c + 1) * LANES]
    t_ref[0, tiles : tiles + 1] = count[spans : spans + 1]
    t_ref[0, tiles + 1 : tiles + 2] = tag[spans : spans + 1]
    t_ref[0, tiles + 2 :] = jnp.zeros((8 - tiles - 2, LANES), f32)


def first_norm(docs, pads, x, gain, shift, rows, region, after):
    tokens, width = x.shape
    spans = region // SPAN
    lines = -(-(spans + 1) // 8) * 8
    wide = width + 2 * LANES
    tok = pl.BlockSpec((region, width), lambda i, *_: (i, 0))

    def row(n, w):
        return pl.BlockSpec((1, n, w), lambda i, *_: (i, 0, 0))

    def body(*refs):
        norm_body(spans, *refs)

    return call(
        body,
        (rows,),
        1,
        [whole(docs.shape), whole(docs.shape), tok, whole((1, width)), whole((1, width))],
        [tok, row(lines, region), row(lines, wide), row(8, LANES)],
        [
            shape((tokens, width), bf16),
            shape((rows, lines, region), f32),
            shape((rows, lines, wide), f32),
            shape((rows, 8, LANES), f32),
        ],
        after=after,
        us=4,
    )(docs, docs, pads, x, gain[None], shift[None])


def state_of(every_ref, d, row_at, tiles):
    lines = every_ref[d, row_at * 8 : row_at * 8 + 8]
    sums = jnp.concatenate([lines[c : c + 1] for c in range(tiles)], axis=1)
    return sums, lines[tiles : tiles + 1], lines[tiles + 1 : tiles + 2]


def owners(me, refs):
    half = len(refs) // 2
    return [(me ^ (2 * (i % half) + i // half), ref) for i, ref in enumerate(refs)]


def means_body(rows, spans, take, me_s, doc_s, doc_ref, pad_ref, p_ref, mean_ref, misc_ref, every_ref):
    me = me_s[0]
    take(me)
    devices = every_ref.shape[0]
    width = mean_ref.shape[-1]
    tiles = width // LANES
    mean_ref[...] = jnp.zeros_like(mean_ref)
    misc_ref[...] = jnp.zeros_like(misc_ref)
    for row_at in range(rows):
        sums = carry = jnp.zeros((1, width), f32)
        count = carry_count = jnp.zeros((1, LANES), f32)
        tag = tag_in = jnp.full((1, LANES), -1.0, f32)
        for d in range(1, devices):
            new_sums, new_count, new_tag = state_of(every_ref, d - 1, row_at, tiles)
            same = (new_tag == tag).astype(f32)
            sums = new_sums + same[:, :1] * sums
            count = new_count + same * count
            tag = new_tag
            mine = me == d
            carry = jnp.where(mine, sums, carry)
            carry_count = jnp.where(mine, count, carry_count)
            tag_in = jnp.where(mine, tag, tag_in)
        for s in range(spans):
            if s == 0:
                run_doc = tag_in
            else:
                run_doc = jnp.full((1, LANES), doc_s[row_at, s * SPAN - 1].astype(f32))
            flag = (tag_in == run_doc).astype(f32)
            total = p_ref[row_at, s : s + 1, :width] + flag[:, :1] * carry
            count_here = p_ref[row_at, s : s + 1, width : width + LANES] + flag * carry_count
            divisor = jnp.maximum(count_here, 1.0)
            mean_ref[row_at, s : s + 1] = total / divisor[:, :1]
            at = row_at * spans + s
            toks = slice(s * SPAN, (s + 1) * SPAN)
            doc = doc_ref[row_at : row_at + 1, toks].astype(f32)
            misc_ref[at, 0:1] = 1.0 / divisor
            misc_ref[at, 1:2] = flag
            misc_ref[at, 2:3] = run_doc
            misc_ref[at, 3:4] = count_here
            misc_ref[at, 4:5] = doc
            misc_ref[at, 5:6] = jnp.where(pad_ref[row_at : row_at + 1, toks] == 1, doc, -2.0)


def document_means(me, docs, pads, prefix, sent, devices, rows, region):
    spans = region // SPAN
    lines = prefix.shape[1]
    width = prefix.shape[2] - 2 * LANES
    in_order = len(sent) == 1
    tall = rows * 8
    outs = [
        shape((rows, lines, width), f32),
        shape((rows * spans, 8, LANES), f32),
        shape((devices, tall, LANES), f32),
    ]

    def body(me_s, doc_s, doc_ref, pad_ref, p_ref, *refs):
        got, outs = refs[: len(sent)], refs[len(sent) :]

        def take(me):
            if in_order:
                outs[2][...] = got[0][...]
                return
            for owner, ref in owners(me, got):
                outs[2][owner] = ref[...]

        means_body(rows, spans, take, me_s, doc_s, doc_ref, pad_ref, p_ref, *outs)

    def tail(v):
        if in_order:
            return whole(v.shape)
        last = v.shape[0] // tall - 1
        return pl.BlockSpec((tall, LANES), lambda *_: (last, 0))

    return call(
        body,
        (1,),
        2,
        [whole(docs.shape), whole(docs.shape), whole(prefix.shape)] + [tail(v) for v in sent],
        [whole(v.shape) for v in outs],
        outs,
    )(me, docs, docs, pads, prefix, *sent)


def take_pieces(at_s, k, came, w_ref):
    here = at_s[0]
    rows = w_ref.shape[0] // len(came)

    def take(ref, first, owner, n):
        at = pl.ds(pl.multiple_of(owner * n, n), n)
        for i in range(3):
            w_ref[at, i * LANES : (i + 1) * LANES] = ref[first + i * n : first + (i + 1) * n].astype(bf16)

    if k == 3:
        for owner, ref in owners(here, came):
            take(ref, 6 * rows, owner, rows)
        return
    half = len(came) // 2
    for core in range(2):

        @pl.when((here + core) % 2 == k - 1)
        def _():
            for j in range(half):
                take(came[core * half + j], 0, here // 2 ^ j, 2 * rows)


def pair_body(load, mean_ref, misc_ref, h_ref, w_ref, qkv_ref, p_ref, ps_ref, o_ref, bar_ref, mix_s):
    load()
    rows = mean_ref.shape[0]
    region = h_ref.shape[0] // rows
    both = nn(hi_lo(mean_ref[...].reshape(-1, mean_ref.shape[-1])), w_ref[:, LANES:])
    half = both.shape[0] // 2
    bars = both[:half] + both[half:]
    bar_ref[0] = bars.reshape(bar_ref.shape[1:])
    masks = halves()
    u = lax.broadcasted_iota(jnp.int32, (SPAN, SPAN), 0)
    t = lax.broadcasted_iota(jnp.int32, (SPAN, SPAN), 1)
    lines = half // rows
    for row_at in range(rows):
        here = slice(row_at * region, (row_at + 1) * region)
        qkv = nn(h_ref[here], w_ref[...])
        qkv_ref[here, :LANES] = (qkv[:, :LANES] * (1.0 / math.sqrt(HEAD_DIM))).astype(bf16)
        qkv_ref[here, LANES:] = qkv[:, LANES:].astype(bf16)
        bars_here = bars[row_at * lines : (row_at + 1) * lines]
        k_lines, v_lines = head_lines(bars_here[:, :LANES]), head_lines(bars_here[:, LANES:])
        summaries = nt(k_lines, qkv_ref[here, :LANES]) + math.log(SPAN)
        all_weights = []
        for s in range(region // SPAN):
            at = row_at * (region // SPAN) + s
            inside = slice(s * SPAN, (s + 1) * SPAN)
            toks = slice(at * SPAN, (at + 1) * SPAN)
            q, k, v = (qkv_ref[toks, i * LANES : (i + 1) * LANES] for i in range(3))
            doc, code = misc_ref[at, 4:5], misc_ref[at, 5:6]
            ok = ((u < t) & (jnp.broadcast_to(code, (SPAN, SPAN)).T == doc)) | (u == t)
            present = (doc == misc_ref[at, 2:3]) & (misc_ref[at, 3:4] > 0.0)
            scores = nt(split(k, masks), q)
            probs, weights = [], []
            for half_at in range(2):
                score = jnp.where(ok, scores[half_at * SPAN : (half_at + 1) * SPAN], MASKED)
                far = jnp.where(present, summaries[8 * s + half_at : 8 * s + half_at + 1, inside], MASKED)
                top = jnp.maximum(jnp.max(score, axis=0, keepdims=True), far)
                e = jnp.exp(score - top)
                w = jnp.exp(far - top)
                inverse = 1.0 / (jnp.sum(e, axis=0, keepdims=True) + w)
                probs.append((e * inverse).astype(bf16))
                weights.append(w * inverse)
            probs = jnp.concatenate(probs, axis=0)
            weights = eight(weights)
            p_ref[0, at] = probs
            ps_ref[0, at] = weights
            all_weights.append(weights)
            mix_s[toks] = tn(probs, split(v, masks))
        o_ref[here] = (mix_s[here] + tn(diagonal(all_weights, lines), v_lines)).astype(bf16)


def pair_forward(at, means, misc, h, source, first, parts, region, kept):
    tokens, width = h.shape
    rows = tokens // region
    spans = region // SPAN
    pairs = width // LANES
    lines = means.shape[1]
    kind, *weights = source

    def pair(i, s):
        return i if kind == "all" else s[1] ^ (first + i)

    in_specs = [whole(means.shape), whole(misc.shape), whole(h.shape)]
    w_spec = pl.BlockSpec((width, 3 * LANES), lambda i, s: (0, pair(i, s)))
    if kind == "all":
        in_specs.append(w_spec)
    else:
        in_specs += [whole(w.shape) for w in weights]
    out_specs = [
        pl.BlockSpec((tokens, 3 * LANES), lambda i, s: (0, pair(i, s))),
        pl.BlockSpec((1, rows * spans, 2 * SPAN, SPAN), lambda i, s: (pair(i, s), 0, 0, 0)),
        pl.BlockSpec((1, rows * spans, 8, SPAN), lambda i, s: (pair(i, s), 0, 0, 0)),
        pl.BlockSpec((tokens, LANES), lambda i, s: (0, pair(i, s))),
        pl.BlockSpec((1, rows, lines, 2 * LANES), lambda i, s: (pair(i, s), 0, 0, 0)),
    ]
    out_shape = [
        shape((tokens, 3 * width), bf16),
        shape((pairs, tokens // SPAN, 2 * SPAN, SPAN), bf16),
        shape((pairs, tokens // SPAN, 8, SPAN), f32),
        shape((tokens, width), bf16),
        shape((pairs, rows, lines, 2 * LANES), f32),
    ]
    if kind != "all":
        out_specs.append(w_spec)
        out_shape.append(shape((width, 3 * width), bf16))
    n_in = 3 + len(weights)
    kept = list(kept or ())

    def body(at_s, *refs):
        ins, got, outs, mix_s = refs[:3], refs[3:n_in], refs[n_in + len(kept) : -1], refs[-1]
        if kind == "all":
            w_ref = got[0]
            load = lambda: None
        else:
            w_ref = outs[5]

            def load():
                for i in range(parts):

                    @pl.when(pl.program_id(0) == i)
                    def _(i=i):
                        if first + i == 0:
                            for m in range(3):
                                w_ref[:, m * LANES : (m + 1) * LANES] = got[m][...]
                        else:
                            take_pieces(at_s, first + i, got[3:], w_ref)

        pair_body(load, *ins, w_ref, *outs[:5], mix_s)

    return call(
        body,
        (parts,),
        1,
        in_specs + [pl.BlockSpec(memory_space=pl.ANY)] * len(kept),
        out_specs,
        out_shape,
        us=5 * parts,
        mib=12,
        aliases={1 + n_in + i: i for i in range(len(kept))},
        scratch=[pltpu.VMEM((tokens, LANES), f32)],
    )(at, means, misc, h, *weights, *kept)


def take_hidden(at_s, own, ups, downs, wu_s, wo_s, wd_s, bu_s):
    here, group = at_s[0], at_s[2]
    lines = own[1].shape[0]
    wu_s[group] = own[0][...]
    wo_s[pl.ds(pl.multiple_of(group * lines, lines), lines)] = own[1][...]
    bu_s[group] = jnp.broadcast_to(own[2][...], bu_s.shape[1:])
    wd_s[group] = own[3][...]
    rows, thin = wu_s.shape[1] // 8, lines // 8
    thick = 3 * (rows + thin)
    deep = downs[0].shape[0] // 12
    for core in range(2):
        up = ups[core]
        sender = (here ^ core) % 2
        near = group ^ (1 + sender)
        bu_s[near] = up[4 * thick :]
        for j in range(4):
            owner = here ^ (2 * j + core)
            first = j * thick
            for to, who, n in ((near, owner // 2, 2), (group ^ 3, owner, 1)):
                at = pl.multiple_of(who * n * rows, n * rows)
                wu_s[to, pl.ds(at, n * rows)] = up[first : first + n * rows].astype(bf16)
                first += n * rows
                at = pl.multiple_of(to * lines + who * n * thin, n * thin)
                wo_s[pl.ds(at, n * thin)] = up[first : first + n * thin].astype(bf16)
                first += n * thin
            chip = here ^ (0, 0, 2, 4)[j]
            place = 4 + chip // 4 * 2 if j % 2 else chip // 2 % 2 * 2
            at = pl.multiple_of(place * deep, 2 * deep)
            down = downs[core]
            first = 3 * j * deep
            wd_s[near, pl.ds(at, 2 * deep)] = down[first : first + 2 * deep].astype(bf16)
            at = pl.multiple_of((place + sender) * deep, deep)
            wd_s[group ^ 3, pl.ds(at, deep)] = down[first + 2 * deep : first + 3 * deep].astype(bf16)


def ffn_body(
    at_s, x_ref, g_ref, o_ref, mine_ref, gain_ref, shift_ref, bd_ref, load, wo_ref,
    out_ref, dmid_ref, do_ref, gwo_ref, gbu_ref, small_ref, gwu_ref, gwd_ref, wu_ref, wd_ref, bu_ref, a_s, du_s,
):
    @pl.when(pl.program_id(0) == 0)
    def _():
        load()
        gwu_ref[...] = jnp.zeros_like(gwu_ref)
        gwd_ref[...] = jnp.zeros_like(gwd_ref)
        gwo_ref[...] = jnp.zeros_like(gwo_ref)
        gbu_ref[...] = jnp.zeros_like(gbu_ref)
        small_ref[...] = jnp.zeros_like(small_ref)

    mid = x_ref[...].astype(f32) + nn(o_ref[...], wo_ref[...])
    xhat, rstd = norm_parts(mid)
    h = (xhat * gain_ref[...] + shift_ref[...]).astype(bf16)
    gm = g_ref[...]
    y = dn = None
    halves_of = 2 * wu_ref.shape[0]
    half = wu_ref.shape[2] // 2

    def cut(i):
        return i // 2, slice(i % 2 * half, (i % 2 + 1) * half)

    def finish(i, a, du, y, dn):
        j, c = cut(i)
        y_part = nn(a, wd_ref[j, c, :])
        dn_part = nt(du, wu_ref[j, :, c])
        return (y_part if y is None else y + y_part), (dn_part if dn is None else dn + dn_part)

    for i in range(halves_of):
        j, c = cut(i)
        up = nn(h, wu_ref[j, :, c]) + bu_ref[j, :1, c]
        da = nt(gm, wd_ref[j, c, :])
        if i > 0:
            y, dn = finish(i - 1, a, du, y, dn)
        phi, slope = gelu_parts(up)
        a = (up * phi).astype(bf16)
        du = (da * slope).astype(bf16)
        a_s[j, :, c] = a
        du_s[j, :, c] = du
    y, dn = finish(halves_of - 1, a, du, y, dn)
    out_ref[...] = (mid + y + bd_ref[...]).astype(bf16)
    g = gm.astype(f32)
    small_ref[2:3] += jnp.sum(dn * xhat, axis=0, keepdims=True)
    small_ref[3:4] += jnp.sum(dn, axis=0, keepdims=True)
    small_ref[4:5] += jnp.sum(g, axis=0, keepdims=True)
    dmid = g + norm_back(dn * gain_ref[...], xhat, rstd)
    dmid_ref[...] = dmid
    gx = dmid.astype(bf16)
    do_ref[...] = nt(gx, wo_ref[...]).astype(bf16)
    gwo_ref[...] += tn(mine_ref[...], gx)
    group = at_s[2]
    du = du_s[group]
    gwd_ref[...] += tn(a_s[group], gm)
    gwu_ref[...] += tn(h, du)
    gbu = jnp.sum(du.astype(f32), axis=0, keepdims=True)
    gbu_ref[...] += gbu
    if gbu.shape[1] == small_ref.shape[1]:
        small_ref[5:6] += gbu


def by_core(core, keep_ref, give_ref):
    return (keep_ref, core), (give_ref, 1 - core)


def feed_forward(at, x, g, o, gain, shift, bd, source, devices):
    tokens, width = x.shape
    kind, *weights = source
    came = kind == "came"
    if came:
        *own, ups, downs, bias = weights
        hidden, groups = own[0].shape[1], 4
        args = [*own, *ups, *downs, bias]
        n_up, n_down = 4 + len(ups), 4 + len(ups) + len(downs)
        last = bias.shape[0] // 8 - 1
        specs = [whole(w.shape) for w in args[:n_down]] + [pl.BlockSpec((8, width), lambda i, *_: (last, 0))]
    else:
        args = weights
        groups, _, hidden = args[0].shape
        specs = [whole(w.shape) for w in args]
    steps = 4
    chunk = tokens // steps
    tok = pl.BlockSpec((chunk, width), lambda i, *_: (i, 0))
    n_w = len(args)
    scratch = [pltpu.VMEM((groups, chunk, hidden), bf16)] * 2
    grads = [shape((width, hidden), f32), shape((hidden, width), f32)]
    if came:
        scratch += [pltpu.VMEM(v.shape, f32) for v in grads]
        scratch += [
            pltpu.VMEM((groups, width, hidden), bf16),
            pltpu.VMEM((width, width), bf16),
            pltpu.VMEM((groups, 8, hidden), f32),
            pltpu.VMEM((groups, hidden, width), bf16),
        ]
        grads = [shape((devices // 2, (width + hidden) // devices, width), f32)] * 2

    def body(at_s, *refs):
        ins, got = refs[:7], refs[7 : 7 + n_w]
        outs, acts, held = refs[7 + n_w : 15 + n_w], refs[15 + n_w : 17 + n_w], refs[17 + n_w :]
        if not came:
            wu_r, wo_r, bu_r, wd_r = got
            ffn_body(at_s, *ins, lambda: None, wo_r, *outs, wu_r, wd_r, bu_r, *acts)
            return
        gwu_s, gwd_s, wu_s, wo_s, bu_s, wd_s = held

        def load():
            take_hidden(at_s, got[:4], got[4:n_up], got[n_up:n_down], wu_s, wo_s, wd_s, bu_s)
            bu_s[at_s[2] ^ 3] = got[n_down][...]

        ffn_body(at_s, *ins, load, wo_s, *outs[:6], gwu_s, gwd_s, wu_s, wd_s, bu_s, *acts)

        @pl.when(pl.program_id(0) == steps - 1)
        def _():
            rows = width // devices
            for out, c in by_core(at_s[0] % 2, *outs[6:]):
                for j in range(devices // 2):
                    lines = pl.ds(pl.multiple_of((2 * j + c) * rows, rows), rows)
                    out[j, :rows] = gwu_s[lines]
                    out[j, rows:] = gwd_s[lines]

    return call(
        body,
        (steps,),
        1,
        [tok, tok, tok, pl.BlockSpec((chunk, LANES), lambda i, s: (i, s[1])),
         whole((1, width)), whole((1, width)), whole((1, width))] + specs,
        [tok, tok, tok, whole((LANES, width)), whole((1, hidden)), whole((8, width))] + [whole(v.shape) for v in grads],
        [
            shape((tokens, width), bf16),
            pltpu.HBM((tokens, width), f32),
            shape((tokens, width), bf16),
            shape((LANES, width), f32),
            shape((1, hidden), f32),
            shape((8, width), f32),
        ] + grads,
        scratch=scratch,
        us=38,
        mib=26,
    )(at, x, g, o, o, gain[None], shift[None], bd[None], *args)


def pair_back_body(rows, qkv_ref, do_ref, p_ref, ps_ref, bar_ref, misc_ref, d_ref, g_ref, d_s):
    masks = halves()
    wide = 2 * LANES
    region = do_ref.shape[0] // rows
    spans = region // SPAN
    for row_at in range(rows):
        here = slice(row_at * region, (row_at + 1) * region)
        bars = bar_ref[0, row_at]
        lines = bars.shape[0]
        k_lines, v_lines = head_lines(bars[:, :LANES]), head_lines(bars[:, LANES:])
        dp_far = nt(v_lines, do_ref[here])
        all_far, all_weights = [], []
        for s in range(spans):
            at = row_at * spans + s
            inside = slice(s * SPAN, (s + 1) * SPAN)
            toks = slice(at * SPAN, (at + 1) * SPAN)
            q, k, v = (qkv_ref[toks, i * LANES : (i + 1) * LANES] for i in range(3))
            do = do_ref[toks]
            weight = ps_ref[0, at]
            dp = nt(split(v, masks), do)
            probs, grads, far = [], [], []
            for half in range(2):
                p_half = p_ref[0, at, half * SPAN : (half + 1) * SPAN, :]
                p = p_half.astype(f32)
                dp_half = dp[half * SPAN : (half + 1) * SPAN]
                w, dw = weight[half : half + 1], dp_far[8 * s + half : 8 * s + half + 1, inside]
                r = jnp.sum(p * dp_half, axis=0, keepdims=True) + w * dw
                probs.append(p_half)
                grads.append((p * (dp_half - r)).astype(bf16))
                far.append(w * (dw - r))
            all_far.append(eight(far))
            all_weights.append(weight)
            d_s[toks, :LANES] = tn(jnp.concatenate(grads, axis=0), split(k, masks))
            d_s[toks, LANES:wide] = nn(jnp.concatenate(grads, axis=1), split(q, masks))
            d_s[toks, wide:] = nn(jnp.concatenate(probs, axis=1), split(do, masks))
        far = diagonal(all_far, lines)
        dq = d_s[here, :LANES] + tn(far, k_lines)
        d_ref[here, :LANES] = (dq.astype(bf16).astype(f32) * (1.0 / math.sqrt(HEAD_DIM))).astype(bf16)
        line = lax.broadcasted_iota(jnp.int32, (8 * lines, LANES), 0)
        lane = lax.broadcasted_iota(jnp.int32, (8 * lines, LANES), 1)
        own = lane // HEAD_DIM == line % 8
        gk = jnp.where(own, nn(far, qkv_ref[here, :LANES]), 0.0)
        gv = jnp.where(own, nn(diagonal(all_weights, lines), do_ref[here]), 0.0)
        out = jnp.zeros((1, wide), f32)
        after = None
        for s in reversed(range(spans)):
            at = row_at * spans + s
            toks = slice(at * SPAN, (at + 1) * SPAN)
            dkv = d_s[toks, LANES:]
            gkv = [jnp.sum(v[8 * s : 8 * s + 8], axis=0, keepdims=True) for v in (gk, gv)]
            inverse, flag = misc_ref[at, 0:1, :], misc_ref[at, 1:2, :]
            gkv = jnp.concatenate(gkv, axis=1) * jnp.concatenate([inverse, inverse], axis=1)
            out = out + jnp.concatenate([flag, flag], axis=1) * gkv
            if after is None:
                after = gkv
            else:
                reached = jnp.broadcast_to(misc_ref[at, 5:6], (SPAN, SPAN)).T == misc_ref[at + 1, 2:3]
                dkv = dkv + jnp.where(jnp.concatenate([reached, reached], axis=1), after, 0.0)
                same = (misc_ref[at, 2:3] == misc_ref[at + 1, 2:3]).astype(f32)
                after = gkv + jnp.concatenate([same, same], axis=1) * after
            d_ref[toks, LANES:] = dkv.astype(bf16)
        g_ref[row_at, :, :LANES] = jnp.zeros((1, LANES), f32)
        g_ref[row_at, :, LANES:] = out


def pair_backward(at, qkv, do, p, ps, bars, misc, h, gwo, devices, region, first, parts, kept):
    tokens, width = do.shape
    rows = tokens // region
    spans = region // SPAN
    lines = bars.shape[2]
    own = h is not None

    def pair(i, s):
        return s[1] ^ (first + i)

    tok3 = pl.BlockSpec((tokens, 3 * LANES), lambda i, s: (0, pair(i, s)))
    back = pl.BlockSpec((rows, 1, 3 * LANES), lambda i, s: (0, 0, pair(i, s)))
    in_specs = [
        tok3,
        pl.BlockSpec((tokens, LANES), lambda i, s: (0, pair(i, s))),
        pl.BlockSpec((1, rows * spans, 2 * SPAN, SPAN), lambda i, s: (pair(i, s), 0, 0, 0)),
        pl.BlockSpec((1, rows * spans, 8, SPAN), lambda i, s: (pair(i, s), 0, 0, 0)),
        pl.BlockSpec((1, rows, lines, 2 * LANES), lambda i, s: (pair(i, s), 0, 0, 0)),
        whole(misc.shape),
    ]
    args = [qkv, do, p, ps, bars, misc]
    out_specs = [tok3, back]
    out_shape = [shape((tokens, 3 * width), bf16), shape((rows, 1, 3 * width), f32)]
    if own:
        in_specs.append(whole(h.shape))
        args.append(h)
        grads = [shape((width, 3 * LANES), f32)]
        if gwo is not None:
            in_specs.append(whole(gwo.shape))
            args.append(gwo)
            grads = [shape((devices // 2, width // devices, width), f32)] * 2
        out_specs += [whole(v.shape) for v in grads]
        out_shape += grads
    n_in = len(args)
    kept = list(kept or ())

    def body(at_s, *refs):
        outs = refs[n_in + len(kept) : n_in + len(kept) + len(out_shape)]
        held = refs[n_in + len(kept) + len(out_shape) :]
        pair_back_body(rows, *refs[:6], outs[0], outs[1], held[0])
        if own:
            grads = tn(refs[6][...], outs[0][...])
            if gwo is None:
                outs[2][...] = grads
            else:
                held[1][...] = grads
                lines_q, lines_o = width // devices, LANES // devices
                for out, c in by_core(at_s[0] % 2, *outs[2:]):
                    for j in range(devices // 2):
                        owner = 2 * j + c
                        out[j, :, : 3 * LANES] = held[1][pl.ds(pl.multiple_of(owner * lines_q, lines_q), lines_q)]
                        go = refs[7][pl.ds(pl.multiple_of(owner * lines_o, lines_o), lines_o)]
                        for i in range(width // LANES):
                            out[j, i * lines_o : (i + 1) * lines_o, 3 * LANES :] = go[:, i * LANES : (i + 1) * LANES]

    return call(
        body,
        (parts,),
        1,
        in_specs + [pl.BlockSpec(memory_space=pl.ANY)] * len(kept),
        out_specs,
        out_shape,
        us=6 * parts,
        mib=12,
        aliases={1 + n_in + i: i for i in range(len(kept))},
        scratch=[pltpu.VMEM((tokens, 3 * LANES), f32), pltpu.VMEM((width, 3 * LANES), f32)],
    )(at, *args, *kept)


def input_body(
    rows, at_s, every_ref, backs, misc_ref, x_ref, gain_ref, dmid_ref, d_ref, w_ref, so_far_ref,
    gi_ref, small_ref, late_ref, through_s, tag_s, back_s,
):
    me = at_s[0]
    devices = every_ref.shape[0]
    width = x_ref.shape[-1]
    tiles = width // LANES
    wide = w_ref.shape[1]

    @pl.when(pl.program_id(0) == 0)
    def _():
        small_ref[...] = so_far_ref[...]
        if len(backs) == 1:
            for d in range(devices):
                back_s[d] = backs[0][d * rows : (d + 1) * rows]
        else:
            for core, ref in enumerate(backs):
                for j in range(devices // 2):
                    back_s[me ^ (2 * j + core)] = ref[j * rows : (j + 1) * rows]
        mine_lanes = pl.ds(pl.multiple_of(at_s[1] * 3 * LANES, LANES), 3 * LANES)
        heads, tails = [], []
        for r in range(rows):
            run = mine = jnp.zeros((1, wide), f32)
            own_run = jnp.zeros((1, 3 * LANES), f32)
            tag = None
            for d in reversed(range(devices)):
                sums, _, tag_here = state_of(every_ref, d, r, tiles)
                if tag is not None:
                    same = (tag == tag_here).astype(f32)[:, :1]
                    run = back_s[d + 1, r : r + 1] + same * run
                    own_run = back_s[d + 1, r : r + 1, mine_lanes] + same * own_run
                    mine = jnp.where(me == d, run, mine)
                tag = tag_here
                tag_s[r : r + 1] = jnp.where(me == d, tag, tag_s[r : r + 1])
                heads.append(sums)
                tails.append(own_run)
            through = nt(hi_lo(jnp.broadcast_to(mine, (8, wide))), w_ref[...])
            through_s[r : r + 1] = through[0:1] + through[8:9]
        late_ref[...] = lax.dot_general(
            jnp.concatenate(heads, axis=0), jnp.concatenate(tails, axis=0), (((0,), (0,)), ((), ())),
            preferred_element_type=f32, precision=lax.Precision.HIGHEST,
        )

    dn = nt(d_ref[...], w_ref[...])
    spans = misc_ref.shape[0]
    added = []
    for i in range(spans):
        at = pl.program_id(0) * spans + i
        row_at = at // (pl.num_programs(0) * spans // rows)
        reached = jnp.broadcast_to(misc_ref[i, 5:6], (SPAN, SPAN)).T == tag_s[pl.ds(row_at, 1)]
        added.append(jnp.where(jnp.concatenate([reached] * tiles, axis=1), through_s[pl.ds(row_at, 1)], 0.0))
    dn = dn + jnp.concatenate(added, axis=0)
    xhat, rstd = norm_parts(x_ref[...].astype(f32))
    small_ref[0:1] += jnp.sum(dn * xhat, axis=0, keepdims=True)
    small_ref[1:2] += jnp.sum(dn, axis=0, keepdims=True)
    gi_ref[...] = dmid_ref[...] + norm_back(dn * gain_ref[...], xhat, rstd)


def input_grads(at, every, back, misc, x, gain, dmid, d, w, small, rows):
    tokens, width = x.shape
    devices = every.shape[0]
    steps = 7 if tokens // SPAN % 7 == 0 else tokens // SPAN
    chunk = tokens // steps
    tok = pl.BlockSpec((chunk, width), lambda i, *_: (i, 0))

    def body(at_s, every_ref, *refs):
        input_body(rows, at_s, every_ref, refs[: len(back)], *refs[len(back) :])

    return call(
        body,
        (steps,),
        1,
        [
            whole(every.shape),
            *[whole(v.shape) for v in back],
            pl.BlockSpec((chunk // SPAN,) + misc.shape[1:], lambda i, *_: (i, 0, 0)),
            tok, whole((1, width)), tok,
            pl.BlockSpec((chunk, 3 * width), lambda i, *_: (i, 0)),
            whole(w.shape),
            whole(small.shape),
        ],
        [tok, whole((8, width)), whole((width, 3 * LANES))],
        [shape((tokens, width), f32), shape((8, width), f32), shape((width, 3 * LANES), f32)],
        scratch=[
            pltpu.VMEM((rows, width), f32), pltpu.VMEM((rows, LANES), f32), pltpu.VMEM((devices, rows, 3 * width), f32)
        ],
        us=2,
        mib=10,
    )(at, every, *back, misc, x, gain[None], dmid, d, w, small)


def fold_body(count, at_s, *refs):
    chip = at_s[0] // 2
    outs = refs[2 * count :]
    at = 0
    for keep, got in zip(refs[:count], refs[count : 2 * count]):
        rows = keep.shape[1]
        for j, out in enumerate(outs):
            out[at : at + rows] = keep[chip ^ j] + got[chip ^ j]
        at += rows


def fold(at, keeps, gots):
    chips, _, width = keeps[0].shape
    outs = [shape((sum(v.shape[1] for v in keeps), width), f32)] * chips

    def body(*refs):
        fold_body(len(keeps), *refs)

    args = [*keeps, *gots]
    return call(body, (1,), 1, [whole(v.shape) for v in args], [whole(v.shape) for v in outs], outs)(at, *args)


def add_body(*refs):
    total = refs[0][...]
    for ref in refs[1:-1]:
        total = total + ref[...]
    refs[-1][...] = total


def add_up(parts, after):
    spec = whole(parts[0].shape)
    return call(add_body, (1,), 0, [spec] * len(parts), spec, shape(parts[0].shape, f32), after=after)(*parts)


def unpack_body(at_s, *refs):
    *pieces, late_ref, gq_ref, gk_ref, gv_ref, go_ref, gu_ref, gd_ref = refs
    rows = gu_ref.shape[0] // len(pieces)
    lines = go_ref.shape[0] // len(pieces)
    for owner, ref in owners(at_s[0], pieces):
        at = pl.ds(pl.multiple_of(owner * rows, rows), rows)
        gu_ref[at] = ref[:rows]
        gd_ref[at] = ref[rows : 2 * rows]
        for i, out in enumerate((gq_ref, gk_ref, gv_ref)):
            lanes = slice(i * LANES, (i + 1) * LANES)
            out[at] = ref[2 * rows :, lanes] + late_ref[at, lanes]
        at = pl.ds(pl.multiple_of(owner * lines, lines), lines)
        for i in range(go_ref.shape[1] // LANES):
            first = 2 * rows + i * lines
            go_ref[at, i * LANES : (i + 1) * LANES] = ref[first : first + lines, 3 * LANES :]


def unpack(at, pieces, late):
    width = pieces[0].shape[1]
    thin = shape((width, LANES), f32)
    outs = [thin, thin, thin, shape((LANES, width), f32), shape((width, width), f32), shape((width, width), f32)]
    args = [*pieces, late]
    return call(
        unpack_body, (1,), 1, [whole(v.shape) for v in args], [whole(v.shape) for v in outs], outs
    )(at, *args)


def totals_body(at_s, mine_ref, theirs_ref, *refs):
    *outs, lines_s = refs
    for core, ref in enumerate((mine_ref, theirs_ref)):
        for j in range(lines_s.shape[0] // 2):
            lines_s[at_s[0] ^ (2 * j + core)] = ref[8 * j : 8 * j + 8]
    total = lines_s[0]
    for d in range(1, lines_s.shape[0]):
        total = total + lines_s[d]
    for i, out in enumerate(outs):
        out[...] = total[i : i + 1]


def totals(at, mine, theirs):
    width = mine.shape[1]
    outs = [shape((1, width), f32)] * 6
    return call(
        totals_body, (1,), 1, [whole(mine.shape)] * 2, [whole(v.shape) for v in outs], outs,
        scratch=[pltpu.VMEM((mine.shape[0] // 4, 8, width), f32)],
    )(at, mine, theirs)


def narrow_body(w_ref, o_ref):
    o_ref[...] = w_ref[...].astype(bf16)


def gathered(part):
    every = lax.all_gather(part.astype(f32), "head")
    flat = every.reshape(-1, part.shape[1])
    chunk = flat.shape[0] // 8
    block = pl.BlockSpec((chunk, part.shape[1]), lambda i: (i, 0))
    return call(narrow_body, (8,), 0, [block], block, shape(flat.shape, bf16))(flat).reshape(every.shape)


def swap(v, axis, mask):
    return lax.ppermute(v, axis, [(i, i ^ mask) for i in range(lax.axis_size(axis))])


def along_z(both, one):
    groups, devices = lax.axis_size("head"), lax.axis_size("seq")
    by_core = [(d * groups + h, d * groups + (h ^ (1 + d % 2))) for d in range(devices) for h in range(groups)]
    return lax.ppermute(both, ("seq", "head"), by_core), swap(one, "head", 3)


def both_cores(pieces, after):
    first, *rest = pieces
    theirs = [swap(first, "seq", 1)]
    held = lax.optimization_barrier((after, *rest))
    return pieces + theirs + [swap(v, "seq", 1) for v in held[1:]]


def on_device(
    inputs, doc_ids, pad_mask, ln1_gain, ln1_shift, w_query, w_key, w_value, w_out,
    ln2_gain, ln2_shift, w_up, b_up, w_down, b_down, out_grad,
):
    rows, region, width = inputs.shape
    tokens = rows * region
    devices = lax.axis_size("seq")
    groups = lax.axis_size("head")
    here = lax.axis_index("seq")
    group = lax.axis_index("head")
    share = width // groups
    pairs = width // LANES
    spans = region // SPAN
    own_pair = group * share // LANES
    at = jnp.stack([here, own_pair, group]).astype(jnp.int32)
    x = inputs.reshape(tokens, width)
    g = out_grad.reshape(tokens, width)
    by_share = share == LANES and devices == 8 and groups == 4

    if by_share:
        others = range(2, devices, 2)
        a_both, a_one = along_z(*attention_share(at, w_query, w_key, w_value, devices))
    h1, m, prefix, tiny = first_norm(
        doc_ids, pad_mask, x, ln1_gain, ln1_shift, rows, region, []
    )
    tiny = tiny.reshape(rows * 8, LANES)
    if by_share:
        (a_sent,) = cat([[(v, 0, v.shape[0]) for v in (a_both, a_one, tiny)]])
        a_moved = [swap(a_sent, "seq", j) for j in others]
        up_both, up_one, down_both, down_one = hidden_share(at, w_up, w_out, b_up, w_down, devices, [h1])
        up_both, up_one = along_z(up_both, up_one)
        down_both, down_one = along_z(down_both, down_one)
        (up_sent,) = cat([[(v, 0, v.shape[0] - 8) for v in (up_both, up_one)]])
        a_pieces = both_cores([a_sent] + a_moved, up_sent)
        up_moved = [swap(up_sent, "seq", j) for j in others]
        means, misc, every = document_means(at, doc_ids, pad_mask, prefix, a_pieces, devices, rows, region)
        source = ("came", w_query, w_key, w_value, *a_pieces)
        qkv, p, ps, o, bars, w_in = pair_forward(at, means, misc, h1, source, 0, pairs, region, None)
        deep = down_one.shape[0] // 2
        upper, lower = cat([[(down_both, 2 * i * deep, 2 * deep), (down_one, i * deep, deep)] for i in range(2)], after=[o])
        down_moved = [upper, lower, swap(upper, "seq", 2), swap(lower, "seq", 4)]
        (up_half,) = cat(
            [[(v, 0, v.shape[0]) for v in [up_sent] + up_moved] + [(up_both, up_both.shape[0] - 8, 8)]], after=[upper]
        )
        (down_half,) = cat([[(v, 0, v.shape[0]) for v in down_moved]], after=[up_half])
        up_pieces = [up_half, swap(up_half, "seq", 1)]
        down_pieces = [down_half, swap(down_half, "seq", 1)]
        ffn_source = ("came", w_up, w_out, b_up[None], w_down, up_pieces, down_pieces, up_one)
    else:
        every = lax.all_gather(tiny, "seq")
        means, misc, every = document_means(at, doc_ids, pad_mask, prefix, [every], devices, rows, region)
        w_in = gathered(jnp.concatenate([w_query, w_key, w_value], axis=1))
        w_in = w_in.reshape(groups, width, 3, share).transpose(1, 2, 0, 3).reshape(width, 3, pairs, LANES)
        w_in = w_in.transpose(0, 2, 1, 3).reshape(width, 3 * width)
        qkv, p, ps, o, bars = pair_forward(at, means, misc, h1, ("all", w_in), 0, pairs, region, None)
        bu = lax.all_gather(b_up, "head")
        bu = jnp.broadcast_to(bu[:, None], (groups, 8, bu.shape[1]))
        ffn_source = ("all", gathered(w_up), gathered(w_out).reshape(width, width), bu, gathered(w_down))

    out, dmid, do, gwo, gbu, small, *hidden_grads = feed_forward(
        at, x, g, o, ln2_gain, ln2_shift, b_down, ffn_source, devices
    )
    back_args = (at, qkv, do, p, ps, bars, misc)
    d, g_back, *pair_grads = pair_backward(
        *back_args, h1, gwo if by_share else None, devices, region, 0, 1, None
    )
    if by_share:
        keeps, gives = zip(hidden_grads, pair_grads)
        folded = fold(at, keeps, [swap(v, "seq", 1) for v in gives])
        arrived = [swap(v, "seq", j) for v, j in zip(folded[1:], others)]
    d, g_back = pair_backward(*back_args, None, None, devices, region, 1, pairs - 1, (d, g_back))
    if by_share:
        g_back = g_back.reshape(rows, 3 * width)
        total = add_up([folded[0]] + arrived, [g_back])
        near = [swap(g_back, "seq", j) for j in others[:-1]]
        held, _ = lax.optimization_barrier((g_back, total))
        far = swap(held, "seq", others[-1])
        spread = [swap(total, "seq", j) for j in others]
        (back,) = cat([[(v, 0, rows) for v in [g_back] + near + [far]]])
        back = [back, swap(back, "seq", 1)]
    else:
        back = [lax.all_gather(g_back, "seq").reshape(devices * rows, 3 * width)]
    grad_inputs, small, late = input_grads(at, every, back, misc, x, ln1_gain, dmid, d, w_in, small, rows)
    out = out.reshape(rows, region, width)
    grad_inputs = grad_inputs.reshape(rows, region, width)
    if by_share:
        pieces = both_cores([total] + spread, small)
        (mine,) = cat([[(v, 0, 8) for v in [small] + [swap(small, "seq", j) for j in others]]], after=[])
        gq, gk, gv, gwo, gwu, gwd = unpack(at, pieces, late)
        g1, s1, g2, s2, gbd, gbu = (v[0] for v in totals(at, mine, swap(mine, "seq", 1)))
        return out, grad_inputs, g1, s1, gq, gk, gv, gwo, g2, s2, gwu, gbu, gwd, gbd

    gwu, gwd = hidden_grads
    (gw,) = pair_grads
    gwu, gwd, gwo, gbu, small, gw = lax.psum((gwu, gwd, gwo, gbu, small, gw), "seq")
    gw = gw + late
    gq, gk, gv = (gw[:, i * LANES : (i + 1) * LANES] for i in range(3))
    if share != LANES:
        inner = group * share - own_pair * LANES
        gq, gk, gv = (lax.dynamic_slice_in_dim(v, inner, share, 1) for v in (gq, gk, gv))
        gwo = lax.dynamic_slice_in_dim(gwo, inner, share, 0)
    return (
        out, grad_inputs, small[0], small[1], gq, gk, gv, gwo, small[2], small[3], gwu, gbu[0], gwd, small[4]
    )


def solution(mesh):
    tok = P(None, "seq", None)
    ids = P(None, "seq")
    cols, lines = P(None, "head"), P("head", None)
    in_specs = (
        tok, ids, ids, P(), P(), cols, cols, cols, lines, P(), P(), cols, P("head"), lines, P(), tok,
    )
    out_specs = (
        tok, tok, P(), P(), cols, cols, cols, lines, P(), P(), cols, P("head"), lines, P(),
    )
    return jax.shard_map(on_device, mesh=mesh, in_specs=in_specs, out_specs=out_specs, check_vma=False)
```

```python
import math

import jax
import jax.numpy as jnp
from jax import lax
from jax.experimental import pallas as pl
from jax.experimental.pallas import tpu as pltpu
from jax.sharding import PartitionSpec as P

HEAD_DIM = 64
SPAN = 128
LANES = 128
NORM_EPS = 1e-05
MASKED = -1e30
f32, bf16 = jnp.float32, jnp.bfloat16


def nn(a, b):
    return lax.dot_general(a, b, (((1,), (0,)), ((), ())), preferred_element_type=f32)


def nt(a, b):
    return lax.dot_general(a, b, (((1,), (1,)), ((), ())), preferred_element_type=f32)


def tn(a, b):
    return lax.dot_general(a, b, (((0,), (0,)), ((), ())), preferred_element_type=f32)


def hi_lo(v):
    hi = v.astype(bf16).astype(f32)
    return jnp.concatenate([hi, v - hi], axis=0).astype(bf16)


def twice(v):
    return jnp.concatenate([v, v], axis=0).astype(bf16)


def norm_parts(x):
    mean = jnp.mean(x, axis=-1, keepdims=True)
    centred = x - mean
    rstd = lax.rsqrt(jnp.mean(centred * centred, axis=-1, keepdims=True) + NORM_EPS)
    return centred * rstd, rstd


def norm_back(y, xhat, rstd):
    return rstd * (
        y
        - jnp.mean(y, axis=-1, keepdims=True)
        - xhat * jnp.mean(y * xhat, axis=-1, keepdims=True)
    )


def gelu_parts(u):
    z = jnp.abs(u)
    t = 1.0 / (1.0 + (0.3275911 * math.sqrt(0.5)) * z)
    e = jnp.exp(-0.5 * u * u)
    poly = t * (
        0.5 * 0.254829592
        + t
        * (
            0.5 * -0.284496736
            + t * (0.5 * 1.421413741 + t * (0.5 * -1.453152027 + t * (0.5 * 1.061405429)))
        )
    )
    tail = poly * e
    phi = jnp.where(u >= 0.0, 1.0 - tail, tail)
    return phi, phi + u * e * (1.0 / math.sqrt(2.0 * math.pi))


def call(body, grid, prefetch, in_specs, out_specs, out_shape, scratch=(), us=2, mib=6, aliases=None, after=()):
    first, last = prefetch + len(in_specs), prefetch + len(in_specs) + len(after)

    def only(*refs):
        body(*refs[:first], *refs[last:])

    kernel = pl.pallas_call(
        only,
        input_output_aliases=aliases or {},
        grid_spec=pltpu.PrefetchScalarGridSpec(
            num_scalar_prefetch=prefetch,
            grid=grid,
            in_specs=list(in_specs) + [pl.BlockSpec(memory_space=pl.ANY)] * len(after),
            out_specs=out_specs,
            scratch_shapes=list(scratch),
        ),
        out_shape=out_shape,
        compiler_params=pltpu.CompilerParams(vmem_limit_bytes=mib * 2**20),
        cost_estimate=pl.CostEstimate(flops=int(us * 1.1e9), bytes_accessed=int(us * 3.5e6), transcendentals=0),
    )
    return lambda *operands: kernel(*operands, *after)


def whole(shape):
    return pl.BlockSpec(shape, lambda *_: (0,) * len(shape))


def shape(dims, dtype):
    return jax.ShapeDtypeStruct(dims, dtype)


def halves():
    lane = lax.broadcasted_iota(jnp.int32, (1, LANES), 1)
    first = (lane < HEAD_DIM).astype(f32)
    return first.astype(bf16), (1.0 - first).astype(bf16)


def split(v, masks):
    return jnp.concatenate([v * masks[0], v * masks[1]], axis=0)


def head_lines(bars):
    line = lax.broadcasted_iota(jnp.int32, (8, LANES), 0)
    lane = lax.broadcasted_iota(jnp.int32, (8, LANES), 1)
    own = lane // HEAD_DIM == line
    lines = [jnp.where(own, bars[s : s + 1], 0.0) for s in range(bars.shape[0])]
    return jnp.concatenate(lines, axis=0).astype(bf16)


def eight(rows):
    return jnp.concatenate(rows + [jnp.zeros((8 - len(rows), rows[0].shape[1]), f32)], axis=0)


def diagonal(blocks, lines):
    zero = jnp.zeros_like(blocks[0])
    rows = [jnp.concatenate([b if i == j else zero for j in range(len(blocks))], axis=1) for i, b in enumerate(blocks)]
    rows += [jnp.zeros_like(rows[0])] * (lines - len(blocks))
    return jnp.concatenate(rows, axis=0).astype(bf16)


def from_hbm(*arrays):
    return [pltpu.with_memory_space_constraint(v, pltpu.HBM) for v in arrays]


def put_shares(at_s, ins, both_ref, one_ref):
    at = 0
    for ref in ins:
        rows = ref.shape[0] // 2
        both_ref[2 * at : 2 * (at + rows)] = ref[...].astype(f32)
        mine = pl.ds(pl.multiple_of(at_s[0] % 2 * rows, rows), rows)
        one_ref[at : at + rows] = ref[mine].astype(f32)
        at += rows


def shares_body(at_s, *refs):
    put_shares(at_s, refs[:3], *refs[3:])


def attention_share(at, wq, wk, wv, devices):
    width, share = wq.shape
    rows = width // devices
    spec = pl.BlockSpec((2 * rows, share), lambda i, s: (s[0] // 2, 0))
    outs = [shape((6 * rows, share), f32), shape((3 * rows, share), f32)]
    return call(
        shares_body, (1,), 1, [spec] * 3, [whole(v.shape) for v in outs], outs
    )(at, *from_hbm(wq, wk, wv))


def hidden_body(at_s, u_ref, o_ref, b_ref, upper_ref, lower_ref, up_both, up_one, down_both, down_one):
    put_shares(at_s, (u_ref, o_ref), up_both, up_one)
    for ref in (up_both, up_one):
        ref[ref.shape[0] - 8 :] = jnp.broadcast_to(b_ref[...], (8, b_ref.shape[1]))
    put_shares(at_s, (upper_ref, lower_ref), down_both, down_one)


def hidden_share(at, wu, wo, bu, wd, devices, after):
    width, hidden = wu.shape
    rows, lines, deep = width // devices, wo.shape[0] // devices, 2 * hidden // devices
    chip = lambda i, s: (s[0] // 2, 0)
    heights = [2 * (rows + lines) + 8, rows + lines + 8, 2 * deep, deep]
    outs = [shape((n, width), f32) for n in heights]
    return call(
        hidden_body,
        (1,),
        1,
        [
            pl.BlockSpec((2 * rows, hidden), chip),
            pl.BlockSpec((2 * lines, width), chip),
            whole((1, hidden)),
            pl.BlockSpec((deep, width), lambda i, s: (s[0] // 2 % 2, 0)),
            pl.BlockSpec((deep, width), lambda i, s: (2 + s[0] // 4, 0)),
        ],
        [whole(v.shape) for v in outs],
        outs,
        after=after,
    )(at, *from_hbm(wu, wo, bu[None], wd, wd))


def cat(groups, after=()):
    arrays, outs = [], []
    for group in groups:
        arrays += [v for v, _, _ in group]
        outs.append(shape((sum(n for _, _, n in group),) + group[0][0].shape[1:], f32))

    def body(*refs):
        ins, got = refs[: len(arrays)], 0
        for group, out in zip(groups, refs[len(arrays) :]):
            at = 0
            for _, first, n in group:
                out[at : at + n] = ins[got][first : first + n]
                at += n
                got += 1

    return call(body, (1,), 0, [whole(v.shape) for v in arrays], [whole(v.shape) for v in outs], outs, after=after)(*arrays)


def norm_body(spans, doc_s, doc_ref, pad_ref, x_ref, g_ref, b_ref, h_ref, m_ref, p_ref, t_ref):
    row_at = pl.program_id(0)
    width = x_ref.shape[-1]
    xhat, _ = norm_parts(x_ref[...].astype(f32))
    h = (xhat * g_ref[...] + b_ref[...]).astype(bf16)
    h_ref[...] = h
    doc = doc_ref[pl.ds(row_at, 1)]
    alive = pad_ref[pl.ds(row_at, 1)] == 1
    rows, region = m_ref.shape[1:]
    lane = lax.broadcasted_iota(jnp.int32, (rows, region), 1)
    line = lax.broadcasted_iota(jnp.int32, (rows, region), 0)
    tag_line = lax.broadcasted_iota(jnp.int32, (rows, LANES), 0)
    picked = jnp.zeros((rows, region), f32)
    tag = jnp.zeros((rows, LANES), f32)
    for s in range(1, spans + 1):
        last = doc_s[row_at, s * SPAN - 1]
        hit = (line == s) & (lane < s * SPAN) & (doc == last) & alive
        picked = jnp.where(hit, 1.0, picked)
        tag = jnp.where(tag_line == s, last.astype(f32), tag)
    m_ref[0] = picked
    sums = nn(picked.astype(bf16), h)
    count = jnp.broadcast_to(jnp.sum(picked, axis=1, keepdims=True), (rows, LANES))
    p_ref[0, :, :width] = sums
    p_ref[0, :, width : width + LANES] = count
    p_ref[0, :, width + LANES :] = tag
    tiles = width // LANES
    for c in range(tiles):
        t_ref[0, c : c + 1] = sums[spans : spans + 1, c * LANES : (c + 1) * LANES]
    t_ref[0, tiles : tiles + 1] = count[spans : spans + 1]
    t_ref[0, tiles + 1 : tiles + 2] = tag[spans : spans + 1]
    t_ref[0, tiles + 2 :] = jnp.zeros((8 - tiles - 2, LANES), f32)


def first_norm(docs, pads, x, gain, shift, rows, region, after):
    tokens, width = x.shape
    spans = region // SPAN
    lines = -(-(spans + 1) // 8) * 8
    wide = width + 2 * LANES
    tok = pl.BlockSpec((region, width), lambda i, *_: (i, 0))

    def row(n, w):
        return pl.BlockSpec((1, n, w), lambda i, *_: (i, 0, 0))

    def body(*refs):
        norm_body(spans, *refs)

    return call(
        body,
        (rows,),
        1,
        [whole(docs.shape), whole(docs.shape), tok, whole((1, width)), whole((1, width))],
        [tok, row(lines, region), row(lines, wide), row(8, LANES)],
        [
            shape((tokens, width), bf16),
            shape((rows, lines, region), f32),
            shape((rows, lines, wide), f32),
            shape((rows, 8, LANES), f32),
        ],
        after=after,
        us=4,
    )(docs, docs, pads, x, gain[None], shift[None])


def state_of(every_ref, d, row_at, tiles):
    lines = every_ref[d, row_at * 8 : row_at * 8 + 8]
    sums = jnp.concatenate([lines[c : c + 1] for c in range(tiles)], axis=1)
    return sums, lines[tiles : tiles + 1], lines[tiles + 1 : tiles + 2]


def owners(me, refs):
    half = len(refs) // 2
    return [(me ^ (2 * (i % half) + i // half), ref) for i, ref in enumerate(refs)]


def means_body(rows, spans, take, me_s, doc_s, doc_ref, pad_ref, p_ref, mean_ref, misc_ref, every_ref):
    me = me_s[0]
    take(me)
    devices = every_ref.shape[0]
    width = mean_ref.shape[-1]
    tiles = width // LANES
    mean_ref[...] = jnp.zeros_like(mean_ref)
    misc_ref[...] = jnp.zeros_like(misc_ref)
    for row_at in range(rows):
        sums = carry = jnp.zeros((1, width), f32)
        count = carry_count = jnp.zeros((1, LANES), f32)
        tag = tag_in = jnp.full((1, LANES), -1.0, f32)
        for d in range(1, devices):
            new_sums, new_count, new_tag = state_of(every_ref, d - 1, row_at, tiles)
            same = (new_tag == tag).astype(f32)
            sums = new_sums + same[:, :1] * sums
            count = new_count + same * count
            tag = new_tag
            mine = me == d
            carry = jnp.where(mine, sums, carry)
            carry_count = jnp.where(mine, count, carry_count)
            tag_in = jnp.where(mine, tag, tag_in)
        for s in range(spans):
            if s == 0:
                run_doc = tag_in
            else:
                run_doc = jnp.full((1, LANES), doc_s[row_at, s * SPAN - 1].astype(f32))
            flag = (tag_in == run_doc).astype(f32)
            total = p_ref[row_at, s : s + 1, :width] + flag[:, :1] * carry
            count_here = p_ref[row_at, s : s + 1, width : width + LANES] + flag * carry_count
            divisor = jnp.maximum(count_here, 1.0)
            mean_ref[row_at, s : s + 1] = total / divisor[:, :1]
            at = row_at * spans + s
            toks = slice(s * SPAN, (s + 1) * SPAN)
            doc = doc_ref[row_at : row_at + 1, toks].astype(f32)
            misc_ref[at, 0:1] = 1.0 / divisor
            misc_ref[at, 1:2] = flag
            misc_ref[at, 2:3] = run_doc
            misc_ref[at, 3:4] = count_here
            misc_ref[at, 4:5] = doc
            misc_ref[at, 5:6] = jnp.where(pad_ref[row_at : row_at + 1, toks] == 1, doc, -2.0)


def document_means(me, docs, pads, prefix, sent, devices, rows, region):
    spans = region // SPAN
    lines = prefix.shape[1]
    width = prefix.shape[2] - 2 * LANES
    in_order = len(sent) == 1
    tall = rows * 8
    outs = [
        shape((rows, lines, width), f32),
        shape((rows * spans, 8, LANES), f32),
        shape((devices, tall, LANES), f32),
    ]

    def body(me_s, doc_s, doc_ref, pad_ref, p_ref, *refs):
        got, outs = refs[: len(sent)], refs[len(sent) :]

        def take(me):
            if in_order:
                outs[2][...] = got[0][...]
                return
            for owner, ref in owners(me, got):
                outs[2][owner] = ref[...]

        means_body(rows, spans, take, me_s, doc_s, doc_ref, pad_ref, p_ref, *outs)

    def tail(v):
        if in_order:
            return whole(v.shape)
        last = v.shape[0] // tall - 1
        return pl.BlockSpec((tall, LANES), lambda *_: (last, 0))

    return call(
        body,
        (1,),
        2,
        [whole(docs.shape), whole(docs.shape), whole(prefix.shape)] + [tail(v) for v in sent],
        [whole(v.shape) for v in outs],
        outs,
    )(me, docs, docs, pads, prefix, *sent)


def take_pieces(at_s, k, came, w_ref):
    here = at_s[0]
    rows = w_ref.shape[0] // len(came)

    def take(ref, first, owner, n):
        at = pl.ds(pl.multiple_of(owner * n, n), n)
        for i in range(3):
            w_ref[at, i * LANES : (i + 1) * LANES] = ref[first + i * n : first + (i + 1) * n].astype(bf16)

    if k == 3:
        for owner, ref in owners(here, came):
            take(ref, 6 * rows, owner, rows)
        return
    half = len(came) // 2
    for core in range(2):

        @pl.when((here + core) % 2 == k - 1)
        def _():
            for j in range(half):
                take(came[core * half + j], 0, here // 2 ^ j, 2 * rows)


def pair_body(load, mean_ref, misc_ref, h_ref, w_ref, qkv_ref, p_ref, ps_ref, o_ref, bar_ref, mix_s):
    load()
    rows = mean_ref.shape[0]
    region = h_ref.shape[0] // rows
    both = nn(hi_lo(mean_ref[...].reshape(-1, mean_ref.shape[-1])), w_ref[:, LANES:])
    half = both.shape[0] // 2
    bars = both[:half] + both[half:]
    bar_ref[0] = bars.reshape(bar_ref.shape[1:])
    masks = halves()
    u = lax.broadcasted_iota(jnp.int32, (SPAN, SPAN), 0)
    t = lax.broadcasted_iota(jnp.int32, (SPAN, SPAN), 1)
    lines = half // rows
    for row_at in range(rows):
        here = slice(row_at * region, (row_at + 1) * region)
        qkv = nn(h_ref[here], w_ref[...])
        qkv_ref[here, :LANES] = (qkv[:, :LANES] * (1.0 / math.sqrt(HEAD_DIM))).astype(bf16)
        qkv_ref[here, LANES:] = qkv[:, LANES:].astype(bf16)
        bars_here = bars[row_at * lines : (row_at + 1) * lines]
        k_lines, v_lines = head_lines(bars_here[:, :LANES]), head_lines(bars_here[:, LANES:])
        summaries = nt(k_lines, qkv_ref[here, :LANES]) + math.log(SPAN)
        all_weights = []
        for s in range(region // SPAN):
            at = row_at * (region // SPAN) + s
            inside = slice(s * SPAN, (s + 1) * SPAN)
            toks = slice(at * SPAN, (at + 1) * SPAN)
            q, k, v = (qkv_ref[toks, i * LANES : (i + 1) * LANES] for i in range(3))
            doc, code = misc_ref[at, 4:5], misc_ref[at, 5:6]
            ok = ((u < t) & (jnp.broadcast_to(code, (SPAN, SPAN)).T == doc)) | (u == t)
            present = (doc == misc_ref[at, 2:3]) & (misc_ref[at, 3:4] > 0.0)
            scores = nt(split(k, masks), q)
            probs, weights = [], []
            for half_at in range(2):
                score = jnp.where(ok, scores[half_at * SPAN : (half_at + 1) * SPAN], MASKED)
                far = jnp.where(present, summaries[8 * s + half_at : 8 * s + half_at + 1, inside], MASKED)
                top = jnp.maximum(jnp.max(score, axis=0, keepdims=True), far)
                e = jnp.exp(score - top)
                w = jnp.exp(far - top)
                inverse = 1.0 / (jnp.sum(e, axis=0, keepdims=True) + w)
                probs.append((e * inverse).astype(bf16))
                weights.append(w * inverse)
            probs = jnp.concatenate(probs, axis=0)
            weights = eight(weights)
            p_ref[0, at] = probs
            ps_ref[0, at] = weights
            all_weights.append(weights)
            mix_s[toks] = tn(probs, split(v, masks))
        o_ref[here] = (mix_s[here] + tn(diagonal(all_weights, lines), v_lines)).astype(bf16)


def pair_forward(at, means, misc, h, source, first, parts, region, kept):
    tokens, width = h.shape
    rows = tokens // region
    spans = region // SPAN
    pairs = width // LANES
    lines = means.shape[1]
    kind, *weights = source

    def pair(i, s):
        return i if kind == "all" else s[1] ^ (first + i)

    in_specs = [whole(means.shape), whole(misc.shape), whole(h.shape)]
    w_spec = pl.BlockSpec((width, 3 * LANES), lambda i, s: (0, pair(i, s)))
    if kind == "all":
        in_specs.append(w_spec)
    else:
        in_specs += [whole(w.shape) for w in weights]
    out_specs = [
        pl.BlockSpec((tokens, 3 * LANES), lambda i, s: (0, pair(i, s))),
        pl.BlockSpec((1, rows * spans, 2 * SPAN, SPAN), lambda i, s: (pair(i, s), 0, 0, 0)),
        pl.BlockSpec((1, rows * spans, 8, SPAN), lambda i, s: (pair(i, s), 0, 0, 0)),
        pl.BlockSpec((tokens, LANES), lambda i, s: (0, pair(i, s))),
        pl.BlockSpec((1, rows, lines, 2 * LANES), lambda i, s: (pair(i, s), 0, 0, 0)),
    ]
    out_shape = [
        shape((tokens, 3 * width), bf16),
        shape((pairs, tokens // SPAN, 2 * SPAN, SPAN), bf16),
        shape((pairs, tokens // SPAN, 8, SPAN), f32),
        shape((tokens, width), bf16),
        shape((pairs, rows, lines, 2 * LANES), f32),
    ]
    if kind != "all":
        out_specs.append(w_spec)
        out_shape.append(shape((width, 3 * width), bf16))
    n_in = 3 + len(weights)
    kept = list(kept or ())

    def body(at_s, *refs):
        ins, got, outs, mix_s = refs[:3], refs[3:n_in], refs[n_in + len(kept) : -1], refs[-1]
        if kind == "all":
            w_ref = got[0]
            load = lambda: None
        else:
            w_ref = outs[5]

            def load():
                for i in range(parts):

                    @pl.when(pl.program_id(0) == i)
                    def _(i=i):
                        if first + i == 0:
                            for m in range(3):
                                w_ref[:, m * LANES : (m + 1) * LANES] = got[m][...]
                        else:
                            take_pieces(at_s, first + i, got[3:], w_ref)

        pair_body(load, *ins, w_ref, *outs[:5], mix_s)

    return call(
        body,
        (parts,),
        1,
        in_specs + [pl.BlockSpec(memory_space=pl.ANY)] * len(kept),
        out_specs,
        out_shape,
        us=5 * parts,
        mib=12,
        aliases={1 + n_in + i: i for i in range(len(kept))},
        scratch=[pltpu.VMEM((tokens, LANES), f32)],
    )(at, means, misc, h, *weights, *kept)


def take_hidden(at_s, own, ups, downs, wu_s, wo_s, wd_s, bu_s):
    here, group = at_s[0], at_s[2]
    lines = own[1].shape[0]
    wu_s[group] = own[0][...]
    wo_s[pl.ds(pl.multiple_of(group * lines, lines), lines)] = own[1][...]
    bu_s[group] = jnp.broadcast_to(own[2][...], bu_s.shape[1:])
    wd_s[group] = own[3][...]
    rows, thin = wu_s.shape[1] // 8, lines // 8
    thick = 3 * (rows + thin)
    deep = downs[0].shape[0] // 12
    for core in range(2):
        up = ups[core]
        sender = (here ^ core) % 2
        near = group ^ (1 + sender)
        bu_s[near] = up[4 * thick :]
        for j in range(4):
            owner = here ^ (2 * j + core)
            first = j * thick
            for to, who, n in ((near, owner // 2, 2), (group ^ 3, owner, 1)):
                at = pl.multiple_of(who * n * rows, n * rows)
                wu_s[to, pl.ds(at, n * rows)] = up[first : first + n * rows].astype(bf16)
                first += n * rows
                at = pl.multiple_of(to * lines + who * n * thin, n * thin)
                wo_s[pl.ds(at, n * thin)] = up[first : first + n * thin].astype(bf16)
                first += n * thin
            chip = here ^ (0, 0, 2, 4)[j]
            place = 4 + chip // 4 * 2 if j % 2 else chip // 2 % 2 * 2
            at = pl.multiple_of(place * deep, 2 * deep)
            down = downs[core]
            first = 3 * j * deep
            wd_s[near, pl.ds(at, 2 * deep)] = down[first : first + 2 * deep].astype(bf16)
            at = pl.multiple_of((place + sender) * deep, deep)
            wd_s[group ^ 3, pl.ds(at, deep)] = down[first + 2 * deep : first + 3 * deep].astype(bf16)


def ffn_body(
    at_s, x_ref, g_ref, o_ref, mine_ref, gain_ref, shift_ref, bd_ref, load, wo_ref,
    out_ref, dmid_ref, do_ref, gwo_ref, gbu_ref, small_ref, gwu_ref, gwd_ref, wu_ref, wd_ref, bu_ref, a_s, du_s,
):
    @pl.when(pl.program_id(0) == 0)
    def _():
        load()
        gwu_ref[...] = jnp.zeros_like(gwu_ref)
        gwd_ref[...] = jnp.zeros_like(gwd_ref)
        gwo_ref[...] = jnp.zeros_like(gwo_ref)
        gbu_ref[...] = jnp.zeros_like(gbu_ref)
        small_ref[...] = jnp.zeros_like(small_ref)

    mid = x_ref[...].astype(f32) + nn(o_ref[...], wo_ref[...])
    xhat, rstd = norm_parts(mid)
    h = (xhat * gain_ref[...] + shift_ref[...]).astype(bf16)
    gm = g_ref[...]
    y = dn = None
    halves_of = 2 * wu_ref.shape[0]
    half = wu_ref.shape[2] // 2

    def cut(i):
        return i // 2, slice(i % 2 * half, (i % 2 + 1) * half)

    def finish(i, a, du, y, dn):
        j, c = cut(i)
        y_part = nn(a, wd_ref[j, c, :])
        dn_part = nt(du, wu_ref[j, :, c])
        return (y_part if y is None else y + y_part), (dn_part if dn is None else dn + dn_part)

    for i in range(halves_of):
        j, c = cut(i)
        up = nn(h, wu_ref[j, :, c]) + bu_ref[j, :1, c]
        da = nt(gm, wd_ref[j, c, :])
        if i > 0:
            y, dn = finish(i - 1, a, du, y, dn)
        phi, slope = gelu_parts(up)
        a = (up * phi).astype(bf16)
        du = (da * slope).astype(bf16)
        a_s[j, :, c] = a
        du_s[j, :, c] = du
    y, dn = finish(halves_of - 1, a, du, y, dn)
    group = at_s[2]
    du = du_s[group]
    gwd_ref[...] += tn(a_s[group], gm)
    gwu_ref[...] += tn(h, du)
    gbu = jnp.sum(du.astype(f32), axis=0, keepdims=True)
    gbu_ref[...] += gbu
    if gbu.shape[1] == small_ref.shape[1]:
        small_ref[5:6] += gbu
    out_ref[...] = (mid + y + bd_ref[...]).astype(bf16)
    g = gm.astype(f32)
    small_ref[2:3] += jnp.sum(dn * xhat, axis=0, keepdims=True)
    small_ref[3:4] += jnp.sum(dn, axis=0, keepdims=True)
    small_ref[4:5] += jnp.sum(g, axis=0, keepdims=True)
    dmid = g + norm_back(dn * gain_ref[...], xhat, rstd)
    dmid_ref[...] = dmid
    gx = dmid.astype(bf16)
    do_ref[...] = nt(gx, wo_ref[...]).astype(bf16)
    gwo_ref[...] += tn(mine_ref[...], gx)


def by_core(core, keep_ref, give_ref):
    return (keep_ref, core), (give_ref, 1 - core)


def feed_forward(at, x, g, o, gain, shift, bd, source, devices):
    tokens, width = x.shape
    kind, *weights = source
    came = kind == "came"
    if came:
        *own, ups, downs, bias = weights
        hidden, groups = own[0].shape[1], 4
        args = [*own, *ups, *downs, bias]
        n_up, n_down = 4 + len(ups), 4 + len(ups) + len(downs)
        last = bias.shape[0] // 8 - 1
        specs = [whole(w.shape) for w in args[:n_down]] + [pl.BlockSpec((8, width), lambda i, *_: (last, 0))]
    else:
        args = weights
        groups, _, hidden = args[0].shape
        specs = [whole(w.shape) for w in args]
    steps = 4
    chunk = tokens // steps
    tok = pl.BlockSpec((chunk, width), lambda i, *_: (i, 0))
    n_w = len(args)
    scratch = [pltpu.VMEM((groups, chunk, hidden), bf16)] * 2
    grads = [shape((width, hidden), f32), shape((hidden, width), f32)]
    if came:
        scratch += [pltpu.VMEM(v.shape, f32) for v in grads]
        scratch += [
            pltpu.VMEM((groups, width, hidden), bf16),
            pltpu.VMEM((width, width), bf16),
            pltpu.VMEM((groups, 8, hidden), f32),
            pltpu.VMEM((groups, hidden, width), bf16),
        ]
        grads = [shape((devices // 2, (width + hidden) // devices, width), f32)] * 2

    def body(at_s, *refs):
        ins, got = refs[:7], refs[7 : 7 + n_w]
        outs, acts, held = refs[7 + n_w : 15 + n_w], refs[15 + n_w : 17 + n_w], refs[17 + n_w :]
        if not came:
            wu_r, wo_r, bu_r, wd_r = got
            ffn_body(at_s, *ins, lambda: None, wo_r, *outs, wu_r, wd_r, bu_r, *acts)
            return
        gwu_s, gwd_s, wu_s, wo_s, bu_s, wd_s = held

        def load():
            take_hidden(at_s, got[:4], got[4:n_up], got[n_up:n_down], wu_s, wo_s, wd_s, bu_s)
            bu_s[at_s[2] ^ 3] = got[n_down][...]

        ffn_body(at_s, *ins, load, wo_s, *outs[:6], gwu_s, gwd_s, wu_s, wd_s, bu_s, *acts)

        @pl.when(pl.program_id(0) == steps - 1)
        def _():
            rows = width // devices
            for out, c in by_core(at_s[0] % 2, *outs[6:]):
                for j in range(devices // 2):
                    lines = pl.ds(pl.multiple_of((2 * j + c) * rows, rows), rows)
                    out[j, :rows] = gwu_s[lines]
                    out[j, rows:] = gwd_s[lines]

    return call(
        body,
        (steps,),
        1,
        [tok, tok, tok, pl.BlockSpec((chunk, LANES), lambda i, s: (i, s[1])),
         whole((1, width)), whole((1, width)), whole((1, width))] + specs,
        [tok, tok, tok, whole((LANES, width)), whole((1, hidden)), whole((8, width))] + [whole(v.shape) for v in grads],
        [
            shape((tokens, width), bf16),
            pltpu.HBM((tokens, width), f32),
            shape((tokens, width), bf16),
            shape((LANES, width), f32),
            shape((1, hidden), f32),
            shape((8, width), f32),
        ] + grads,
        scratch=scratch,
        us=38,
        mib=26,
    )(at, x, g, o, o, gain[None], shift[None], bd[None], *args)


def pair_back_body(rows, qkv_ref, do_ref, p_ref, ps_ref, bar_ref, misc_ref, d_ref, g_ref, d_s):
    masks = halves()
    wide = 2 * LANES
    region = do_ref.shape[0] // rows
    spans = region // SPAN
    for row_at in range(rows):
        here = slice(row_at * region, (row_at + 1) * region)
        bars = bar_ref[0, row_at]
        lines = bars.shape[0]
        k_lines, v_lines = head_lines(bars[:, :LANES]), head_lines(bars[:, LANES:])
        dp_far = nt(v_lines, do_ref[here])
        all_far, all_weights = [], []
        for s in range(spans):
            at = row_at * spans + s
            inside = slice(s * SPAN, (s + 1) * SPAN)
            toks = slice(at * SPAN, (at + 1) * SPAN)
            q, k, v = (qkv_ref[toks, i * LANES : (i + 1) * LANES] for i in range(3))
            do = do_ref[toks]
            weight = ps_ref[0, at]
            dp = nt(split(v, masks), do)
            probs, grads, far = [], [], []
            for half in range(2):
                p_half = p_ref[0, at, half * SPAN : (half + 1) * SPAN, :]
                p = p_half.astype(f32)
                dp_half = dp[half * SPAN : (half + 1) * SPAN]
                w, dw = weight[half : half + 1], dp_far[8 * s + half : 8 * s + half + 1, inside]
                r = jnp.sum(p * dp_half, axis=0, keepdims=True) + w * dw
                probs.append(p_half)
                grads.append((p * (dp_half - r)).astype(bf16))
                far.append(w * (dw - r))
            all_far.append(eight(far))
            all_weights.append(weight)
            d_s[toks, :LANES] = tn(jnp.concatenate(grads, axis=0), split(k, masks))
            d_s[toks, LANES:wide] = nn(jnp.concatenate(grads, axis=1), split(q, masks))
            d_s[toks, wide:] = nn(jnp.concatenate(probs, axis=1), split(do, masks))
        far = diagonal(all_far, lines)
        dq = d_s[here, :LANES] + tn(far, k_lines)
        d_ref[here, :LANES] = (dq.astype(bf16).astype(f32) * (1.0 / math.sqrt(HEAD_DIM))).astype(bf16)
        line = lax.broadcasted_iota(jnp.int32, (8 * lines, LANES), 0)
        lane = lax.broadcasted_iota(jnp.int32, (8 * lines, LANES), 1)
        own = lane // HEAD_DIM == line % 8
        gk = jnp.where(own, nn(far, qkv_ref[here, :LANES]), 0.0)
        gv = jnp.where(own, nn(diagonal(all_weights, lines), do_ref[here]), 0.0)
        out = jnp.zeros((1, wide), f32)
        after = None
        for s in reversed(range(spans)):
            at = row_at * spans + s
            toks = slice(at * SPAN, (at + 1) * SPAN)
            dkv = d_s[toks, LANES:]
            gkv = [jnp.sum(v[8 * s : 8 * s + 8], axis=0, keepdims=True) for v in (gk, gv)]
            inverse, flag = misc_ref[at, 0:1, :], misc_ref[at, 1:2, :]
            gkv = jnp.concatenate(gkv, axis=1) * jnp.concatenate([inverse, inverse], axis=1)
            out = out + jnp.concatenate([flag, flag], axis=1) * gkv
            if after is None:
                after = gkv
            else:
                reached = jnp.broadcast_to(misc_ref[at, 5:6], (SPAN, SPAN)).T == misc_ref[at + 1, 2:3]
                dkv = dkv + jnp.where(jnp.concatenate([reached, reached], axis=1), after, 0.0)
                same = (misc_ref[at, 2:3] == misc_ref[at + 1, 2:3]).astype(f32)
                after = gkv + jnp.concatenate([same, same], axis=1) * after
            d_ref[toks, LANES:] = dkv.astype(bf16)
        g_ref[row_at, :, :LANES] = jnp.zeros((1, LANES), f32)
        g_ref[row_at, :, LANES:] = out


def pair_backward(at, qkv, do, p, ps, bars, misc, h, gwo, devices, region, first, parts, kept):
    tokens, width = do.shape
    rows = tokens // region
    spans = region // SPAN
    lines = bars.shape[2]
    own = h is not None

    def pair(i, s):
        return s[1] ^ (first + i)

    tok3 = pl.BlockSpec((tokens, 3 * LANES), lambda i, s: (0, pair(i, s)))
    back = pl.BlockSpec((rows, 1, 3 * LANES), lambda i, s: (0, 0, pair(i, s)))
    in_specs = [
        tok3,
        pl.BlockSpec((tokens, LANES), lambda i, s: (0, pair(i, s))),
        pl.BlockSpec((1, rows * spans, 2 * SPAN, SPAN), lambda i, s: (pair(i, s), 0, 0, 0)),
        pl.BlockSpec((1, rows * spans, 8, SPAN), lambda i, s: (pair(i, s), 0, 0, 0)),
        pl.BlockSpec((1, rows, lines, 2 * LANES), lambda i, s: (pair(i, s), 0, 0, 0)),
        whole(misc.shape),
    ]
    args = [qkv, do, p, ps, bars, misc]
    out_specs = [tok3, back]
    out_shape = [shape((tokens, 3 * width), bf16), shape((rows, 1, 3 * width), f32)]
    if own:
        in_specs.append(whole(h.shape))
        args.append(h)
        grads = [shape((width, 3 * LANES), f32)]
        if gwo is not None:
            in_specs.append(whole(gwo.shape))
            args.append(gwo)
            grads = [shape((devices // 2, width // devices, width), f32)] * 2
        out_specs += [whole(v.shape) for v in grads]
        out_shape += grads
    n_in = len(args)
    kept = list(kept or ())

    def body(at_s, *refs):
        outs = refs[n_in + len(kept) : n_in + len(kept) + len(out_shape)]
        held = refs[n_in + len(kept) + len(out_shape) :]
        pair_back_body(rows, *refs[:6], outs[0], outs[1], held[0])
        if own:
            grads = tn(refs[6][...], outs[0][...])
            if gwo is None:
                outs[2][...] = grads
            else:
                held[1][...] = grads
                lines_q, lines_o = width // devices, LANES // devices
                for out, c in by_core(at_s[0] % 2, *outs[2:]):
                    for j in range(devices // 2):
                        owner = 2 * j + c
                        out[j, :, : 3 * LANES] = held[1][pl.ds(pl.multiple_of(owner * lines_q, lines_q), lines_q)]
                        go = refs[7][pl.ds(pl.multiple_of(owner * lines_o, lines_o), lines_o)]
                        for i in range(width // LANES):
                            out[j, i * lines_o : (i + 1) * lines_o, 3 * LANES :] = go[:, i * LANES : (i + 1) * LANES]

    return call(
        body,
        (parts,),
        1,
        in_specs + [pl.BlockSpec(memory_space=pl.ANY)] * len(kept),
        out_specs,
        out_shape,
        us=6 * parts,
        mib=12,
        aliases={1 + n_in + i: i for i in range(len(kept))},
        scratch=[pltpu.VMEM((tokens, 3 * LANES), f32), pltpu.VMEM((width, 3 * LANES), f32)],
    )(at, *args, *kept)


def input_body(
    rows, at_s, every_ref, backs, misc_ref, x_ref, gain_ref, dmid_ref, d_ref, w_ref, so_far_ref,
    gi_ref, small_ref, late_ref, through_s, tag_s, back_s,
):
    me = at_s[0]
    devices = every_ref.shape[0]
    width = x_ref.shape[-1]
    tiles = width // LANES
    wide = w_ref.shape[1]

    @pl.when(pl.program_id(0) == 0)
    def _():
        small_ref[...] = so_far_ref[...]
        if len(backs) == 1:
            for d in range(devices):
                back_s[d] = backs[0][d * rows : (d + 1) * rows]
        else:
            for core, ref in enumerate(backs):
                for j in range(devices // 2):
                    back_s[me ^ (2 * j + core)] = ref[j * rows : (j + 1) * rows]
        mine_lanes = pl.ds(pl.multiple_of(at_s[1] * 3 * LANES, LANES), 3 * LANES)
        heads, tails = [], []
        for r in range(rows):
            run = mine = jnp.zeros((1, wide), f32)
            own_run = jnp.zeros((1, 3 * LANES), f32)
            tag = None
            for d in reversed(range(devices)):
                sums, _, tag_here = state_of(every_ref, d, r, tiles)
                if tag is not None:
                    same = (tag == tag_here).astype(f32)[:, :1]
                    run = back_s[d + 1, r : r + 1] + same * run
                    own_run = back_s[d + 1, r : r + 1, mine_lanes] + same * own_run
                    mine = jnp.where(me == d, run, mine)
                tag = tag_here
                tag_s[r : r + 1] = jnp.where(me == d, tag, tag_s[r : r + 1])
                heads.append(sums)
                tails.append(own_run)
            through = nt(hi_lo(jnp.broadcast_to(mine, (8, wide))), w_ref[...])
            through_s[r : r + 1] = through[0:1] + through[8:9]
        late_ref[...] = lax.dot_general(
            jnp.concatenate(heads, axis=0), jnp.concatenate(tails, axis=0), (((0,), (0,)), ((), ())),
            preferred_element_type=f32, precision=lax.Precision.HIGHEST,
        )

    dn = nt(d_ref[...], w_ref[...])
    spans = misc_ref.shape[0]
    added = []
    for i in range(spans):
        at = pl.program_id(0) * spans + i
        row_at = at // (pl.num_programs(0) * spans // rows)
        reached = jnp.broadcast_to(misc_ref[i, 5:6], (SPAN, SPAN)).T == tag_s[pl.ds(row_at, 1)]
        added.append(jnp.where(jnp.concatenate([reached] * tiles, axis=1), through_s[pl.ds(row_at, 1)], 0.0))
    dn = dn + jnp.concatenate(added, axis=0)
    xhat, rstd = norm_parts(x_ref[...].astype(f32))
    small_ref[0:1] += jnp.sum(dn * xhat, axis=0, keepdims=True)
    small_ref[1:2] += jnp.sum(dn, axis=0, keepdims=True)
    gi_ref[...] = dmid_ref[...] + norm_back(dn * gain_ref[...], xhat, rstd)


def input_grads(at, every, back, misc, x, gain, dmid, d, w, small, rows):
    tokens, width = x.shape
    devices = every.shape[0]
    steps = 7 if tokens // SPAN % 7 == 0 else tokens // SPAN
    chunk = tokens // steps
    tok = pl.BlockSpec((chunk, width), lambda i, *_: (i, 0))

    def body(at_s, every_ref, *refs):
        input_body(rows, at_s, every_ref, refs[: len(back)], *refs[len(back) :])

    return call(
        body,
        (steps,),
        1,
        [
            whole(every.shape),
            *[whole(v.shape) for v in back],
            pl.BlockSpec((chunk // SPAN,) + misc.shape[1:], lambda i, *_: (i, 0, 0)),
            tok, whole((1, width)), tok,
            pl.BlockSpec((chunk, 3 * width), lambda i, *_: (i, 0)),
            whole(w.shape),
            whole(small.shape),
        ],
        [tok, whole((8, width)), whole((width, 3 * LANES))],
        [shape((tokens, width), f32), shape((8, width), f32), shape((width, 3 * LANES), f32)],
        scratch=[
            pltpu.VMEM((rows, width), f32), pltpu.VMEM((rows, LANES), f32), pltpu.VMEM((devices, rows, 3 * width), f32)
        ],
        us=2,
        mib=10,
    )(at, every, *back, misc, x, gain[None], dmid, d, w, small)


def fold_body(count, at_s, *refs):
    chip = at_s[0] // 2
    outs = refs[2 * count :]
    at = 0
    for keep, got in zip(refs[:count], refs[count : 2 * count]):
        rows = keep.shape[1]
        for j, out in enumerate(outs):
            out[at : at + rows] = keep[chip ^ j] + got[chip ^ j]
        at += rows


def fold(at, keeps, gots):
    chips, _, width = keeps[0].shape
    outs = [shape((sum(v.shape[1] for v in keeps), width), f32)] * chips

    def body(*refs):
        fold_body(len(keeps), *refs)

    args = [*keeps, *gots]
    return call(body, (1,), 1, [whole(v.shape) for v in args], [whole(v.shape) for v in outs], outs)(at, *args)


def add_body(*refs):
    total = refs[0][...]
    for ref in refs[1:-1]:
        total = total + ref[...]
    refs[-1][...] = total


def add_up(parts, after):
    spec = whole(parts[0].shape)
    return call(add_body, (1,), 0, [spec] * len(parts), spec, shape(parts[0].shape, f32), after=after)(*parts)


def unpack_body(at_s, *refs):
    *pieces, late_ref, gq_ref, gk_ref, gv_ref, go_ref, gu_ref, gd_ref = refs
    rows = gu_ref.shape[0] // len(pieces)
    lines = go_ref.shape[0] // len(pieces)
    for owner, ref in owners(at_s[0], pieces):
        at = pl.ds(pl.multiple_of(owner * rows, rows), rows)
        gu_ref[at] = ref[:rows]
        gd_ref[at] = ref[rows : 2 * rows]
        for i, out in enumerate((gq_ref, gk_ref, gv_ref)):
            lanes = slice(i * LANES, (i + 1) * LANES)
            out[at] = ref[2 * rows :, lanes] + late_ref[at, lanes]
        at = pl.ds(pl.multiple_of(owner * lines, lines), lines)
        for i in range(go_ref.shape[1] // LANES):
            first = 2 * rows + i * lines
            go_ref[at, i * LANES : (i + 1) * LANES] = ref[first : first + lines, 3 * LANES :]


def unpack(at, pieces, late):
    width = pieces[0].shape[1]
    thin = shape((width, LANES), f32)
    outs = [thin, thin, thin, shape((LANES, width), f32), shape((width, width), f32), shape((width, width), f32)]
    args = [*pieces, late]
    return call(
        unpack_body, (1,), 1, [whole(v.shape) for v in args], [whole(v.shape) for v in outs], outs
    )(at, *args)


def totals_body(at_s, mine_ref, theirs_ref, *refs):
    *outs, lines_s = refs
    for core, ref in enumerate((mine_ref, theirs_ref)):
        for j in range(lines_s.shape[0] // 2):
            lines_s[at_s[0] ^ (2 * j + core)] = ref[8 * j : 8 * j + 8]
    total = lines_s[0]
    for d in range(1, lines_s.shape[0]):
        total = total + lines_s[d]
    for i, out in enumerate(outs):
        out[...] = total[i : i + 1]


def totals(at, mine, theirs):
    width = mine.shape[1]
    outs = [shape((1, width), f32)] * 6
    return call(
        totals_body, (1,), 1, [whole(mine.shape)] * 2, [whole(v.shape) for v in outs], outs,
        scratch=[pltpu.VMEM((mine.shape[0] // 4, 8, width), f32)],
    )(at, mine, theirs)


def narrow_body(w_ref, o_ref):
    o_ref[...] = w_ref[...].astype(bf16)


def gathered(part):
    every = lax.all_gather(part.astype(f32), "head")
    flat = every.reshape(-1, part.shape[1])
    chunk = flat.shape[0] // 8
    block = pl.BlockSpec((chunk, part.shape[1]), lambda i: (i, 0))
    return call(narrow_body, (8,), 0, [block], block, shape(flat.shape, bf16))(flat).reshape(every.shape)


def swap(v, axis, mask):
    return lax.ppermute(v, axis, [(i, i ^ mask) for i in range(lax.axis_size(axis))])


def along_z(both, one):
    groups, devices = lax.axis_size("head"), lax.axis_size("seq")
    by_core = [(d * groups + h, d * groups + (h ^ (1 + d % 2))) for d in range(devices) for h in range(groups)]
    return lax.ppermute(both, ("seq", "head"), by_core), swap(one, "head", 3)


def both_cores(pieces, after):
    first, *rest = pieces
    theirs = [swap(first, "seq", 1)]
    held = lax.optimization_barrier((after, *rest))
    return pieces + theirs + [swap(v, "seq", 1) for v in held[1:]]


def on_device(
    inputs, doc_ids, pad_mask, ln1_gain, ln1_shift, w_query, w_key, w_value, w_out,
    ln2_gain, ln2_shift, w_up, b_up, w_down, b_down, out_grad,
):
    rows, region, width = inputs.shape
    tokens = rows * region
    devices = lax.axis_size("seq")
    groups = lax.axis_size("head")
    here = lax.axis_index("seq")
    group = lax.axis_index("head")
    share = width // groups
    pairs = width // LANES
    spans = region // SPAN
    own_pair = group * share // LANES
    at = jnp.stack([here, own_pair, group]).astype(jnp.int32)
    x = inputs.reshape(tokens, width)
    g = out_grad.reshape(tokens, width)
    by_share = share == LANES and devices == 8 and groups == 4

    if by_share:
        others = range(2, devices, 2)
        a_both, a_one = along_z(*attention_share(at, w_query, w_key, w_value, devices))
    h1, m, prefix, tiny = first_norm(
        doc_ids, pad_mask, x, ln1_gain, ln1_shift, rows, region, []
    )
    tiny = tiny.reshape(rows * 8, LANES)
    if by_share:
        (a_sent,) = cat([[(v, 0, v.shape[0]) for v in (a_both, a_one, tiny)]])
        a_moved = [swap(a_sent, "seq", j) for j in others]
        up_both, up_one, down_both, down_one = hidden_share(at, w_up, w_out, b_up, w_down, devices, [h1])
        up_both, up_one = along_z(up_both, up_one)
        down_both, down_one = along_z(down_both, down_one)
        (up_sent,) = cat([[(v, 0, v.shape[0] - 8) for v in (up_both, up_one)]])
        a_pieces = both_cores([a_sent] + a_moved, up_sent)
        up_moved = [swap(up_sent, "seq", j) for j in others]
        means, misc, every = document_means(at, doc_ids, pad_mask, prefix, a_pieces, devices, rows, region)
        source = ("came", w_query, w_key, w_value, *a_pieces)
        qkv, p, ps, o, bars, w_in = pair_forward(at, means, misc, h1, source, 0, pairs, region, None)
        deep = down_one.shape[0] // 2
        upper, lower = cat([[(down_both, 2 * i * deep, 2 * deep), (down_one, i * deep, deep)] for i in range(2)], after=[o])
        down_moved = [upper, lower, swap(upper, "seq", 2), swap(lower, "seq", 4)]
        (up_half,) = cat(
            [[(v, 0, v.shape[0]) for v in [up_sent] + up_moved] + [(up_both, up_both.shape[0] - 8, 8)]], after=[upper]
        )
        (down_half,) = cat([[(v, 0, v.shape[0]) for v in down_moved]], after=[up_half])
        up_pieces = [up_half, swap(up_half, "seq", 1)]
        down_pieces = [down_half, swap(down_half, "seq", 1)]
        ffn_source = ("came", w_up, w_out, b_up[None], w_down, up_pieces, down_pieces, up_one)
    else:
        every = lax.all_gather(tiny, "seq")
        means, misc, every = document_means(at, doc_ids, pad_mask, prefix, [every], devices, rows, region)
        w_in = gathered(jnp.concatenate([w_query, w_key, w_value], axis=1))
        w_in = w_in.reshape(groups, width, 3, share).transpose(1, 2, 0, 3).reshape(width, 3, pairs, LANES)
        w_in = w_in.transpose(0, 2, 1, 3).reshape(width, 3 * width)
        qkv, p, ps, o, bars = pair_forward(at, means, misc, h1, ("all", w_in), 0, pairs, region, None)
        bu = lax.all_gather(b_up, "head")
        bu = jnp.broadcast_to(bu[:, None], (groups, 8, bu.shape[1]))
        ffn_source = ("all", gathered(w_up), gathered(w_out).reshape(width, width), bu, gathered(w_down))

    out, dmid, do, gwo, gbu, small, *hidden_grads = feed_forward(
        at, x, g, o, ln2_gain, ln2_shift, b_down, ffn_source, devices
    )
    back_args = (at, qkv, do, p, ps, bars, misc)
    d, g_back, *pair_grads = pair_backward(
        *back_args, h1, gwo if by_share else None, devices, region, 0, 1, None
    )
    if by_share:
        keeps, gives = zip(hidden_grads, pair_grads)
        folded = fold(at, keeps, [swap(v, "seq", 1) for v in gives])
        arrived = [swap(v, "seq", j) for v, j in zip(folded[1:], others)]
    d, g_back = pair_backward(*back_args, None, None, devices, region, 1, pairs - 1, (d, g_back))
    if by_share:
        g_back = g_back.reshape(rows, 3 * width)
        total = add_up([folded[0]] + arrived, [g_back])
        near = [swap(g_back, "seq", j) for j in others[:-1]]
        held, _ = lax.optimization_barrier((g_back, total))
        far = swap(held, "seq", others[-1])
        spread = [swap(total, "seq", j) for j in others]
        (back,) = cat([[(v, 0, rows) for v in [g_back] + near + [far]]])
        back = [back, swap(back, "seq", 1)]
    else:
        back = [lax.all_gather(g_back, "seq").reshape(devices * rows, 3 * width)]
    grad_inputs, small, late = input_grads(at, every, back, misc, x, ln1_gain, dmid, d, w_in, small, rows)
    out = out.reshape(rows, region, width)
    grad_inputs = grad_inputs.reshape(rows, region, width)
    if by_share:
        pieces = both_cores([total] + spread, small)
        (mine,) = cat([[(v, 0, 8) for v in [small] + [swap(small, "seq", j) for j in others]]], after=[])
        gq, gk, gv, gwo, gwu, gwd = unpack(at, pieces, late)
        g1, s1, g2, s2, gbd, gbu = (v[0] for v in totals(at, mine, swap(mine, "seq", 1)))
        return out, grad_inputs, g1, s1, gq, gk, gv, gwo, g2, s2, gwu, gbu, gwd, gbd

    gwu, gwd = hidden_grads
    (gw,) = pair_grads
    gwu, gwd, gwo, gbu, small, gw = lax.psum((gwu, gwd, gwo, gbu, small, gw), "seq")
    gw = gw + late
    gq, gk, gv = (gw[:, i * LANES : (i + 1) * LANES] for i in range(3))
    if share != LANES:
        inner = group * share - own_pair * LANES
        gq, gk, gv = (lax.dynamic_slice_in_dim(v, inner, share, 1) for v in (gq, gk, gv))
        gwo = lax.dynamic_slice_in_dim(gwo, inner, share, 0)
    return (
        out, grad_inputs, small[0], small[1], gq, gk, gv, gwo, small[2], small[3], gwu, gbu[0], gwd, small[4]
    )


def solution(mesh):
    tok = P(None, "seq", None)
    ids = P(None, "seq")
    cols, lines = P(None, "head"), P("head", None)
    in_specs = (
        tok, ids, ids, P(), P(), cols, cols, cols, lines, P(), P(), cols, P("head"), lines, P(), tok,
    )
    out_specs = (
        tok, tok, P(), P(), cols, cols, cols, lines, P(), P(), cols, P("head"), lines, P(),
    )
    return jax.shard_map(on_device, mesh=mesh, in_specs=in_specs, out_specs=out_specs, check_vma=False)
```
